32 devices in a mesh: parts: 2 (over x), grp: 16 (over z, y, core).
Axes of the slice: x: 2, y: 2, z: 4, core: 2. Of those that a mesh axis runs over, the one named last changes fastest.
Arguments:
- features: bfloat16 [64, 16, 1024], P(('parts', 'grp')), parts along dimension 0, may hold values from -6 to 6
- counts: int32 [64], P(('parts', 'grp')), parts along dimension 0, may hold values from 1 to 16, as said below
- pick_owner: int32 [32, 8], P(('parts', 'grp')), parts along dimension 0, may hold values from 0 to 15, all different within a row
- pick_local: int32 [32, 8], P(('parts', 'grp')), parts along dimension 0, may hold values from 0 to 1
- adjacency: bfloat16 [32, 128, 128], P(('parts', 'grp')), parts along dimension 0, may hold values from 0 to 2
- cotangent: bfloat16 [32, 128, 1024], P(('parts', 'grp')), parts along dimension 0, may hold values from -6 to 6
- w_first: bfloat16 [1024, 1024], replicated, may hold values from -0.1875 to 0.1875
- w_second: bfloat16 [1024, 1024], replicated, may hold values from -0.1875 to 0.1875
Outputs:
- output: bfloat16 [32, 128, 1024], P(('parts', 'grp')), parts along dimension 0
- grad_first: float32 [2048, 1024], P(('parts', 'grp')), parts along dimension 0
- grad_second: float32 [2048, 1024], P(('parts', 'grp')), parts along dimension 0
The draws below stay inside these ranges and needn't reach their ends.
There are 2 independent parts, one for each index of `parts`. The reference program is written for one: setup_inputs(seed, part) draws one part's arguments, and reference() takes and returns one part's arrays. A program takes and returns all parts, laid end to end along the dimension named above; an argument that names none is the same for every part. Nothing has to cross between parts.
Inputs may be any that keep to these rules, and one draw needn't show every extreme that they name: `counts`: each cluster has 1 to 16 live nodes; some cluster has exactly 16. `pick_owner`: within one row the 8 holders differ; every device holds some picked cluster.
All inputs are finite; a program needn't handle non-finite values.
Results may differ from the reference program's by a relative error of at most 0.0062.
Values may be sent and summed in bfloat16 or wider, within the bound.
No kernel may reach another device: no remote copies, remote signals or barrier semaphores. Data moves between devices by JAX's collectives and lax.ppermute only.
A program may use at most 64 MiB of HBM per device.

```python
import jax
import jax.numpy as jnp
from jax import lax

D = 1024
R = 16
OWN = 2
PICK = 8
CLUSTERS = 32
ROWS = 128
N_GRP = 16


def draw_counts(key, part):
    key = jax.random.fold_in(key, 11)
    first, second = jax.random.split(key)
    values = jax.random.randint(first, (CLUSTERS,), 1, R + 1)
    where_full = jax.random.randint(second, (), 0, CLUSTERS)
    return values.at[where_full].set(R).astype(jnp.int32)


def draw_adjacency(key, part):
    key = jax.random.fold_in(key, 23)
    first = jax.random.fold_in(key, 0)
    noise = jax.random.uniform(first, (N_GRP, ROWS, ROWS), jnp.float32, 0.0, 2.0)
    block = jnp.arange(ROWS) // R
    same = block[:, None] == block[None, :]
    weights = jnp.where(same, noise / R, noise / ROWS)
    weights = weights + jnp.eye(ROWS, dtype=jnp.float32)[None]
    return weights.astype(jnp.bfloat16)


def set_ends(values, own_key, low, largest):
    longest = values.shape.index(max(values.shape))
    spots = []
    for shift in (0, 1):
        where = [jax.random.randint(jax.random.fold_in(own_key, axis), (), 0, length) for axis, length in enumerate(values.shape)]
        where[longest] = (where[longest] + shift) % values.shape[longest]
        spots.append(tuple(where))
    return values.at[spots[0]].set(low).at[spots[1]].set(largest)


def strengthened(result, own_key, source, target, shards_of, factor):
    def block_of(position):
        return (jnp.arange(result.shape[position]) // (result.shape[position] // shards_of)).reshape((-1,) + (1,) * (result.ndim - 1 - position))

    first = jax.random.permutation(own_key, shards_of)[block_of(target)]
    other_side = (block_of(target) + shards_of // 2) % shards_of
    return jnp.where((block_of(source) == first) | (block_of(source) == other_side), factor * result, result)


def block_levels(stream_key, dims, pieces, smallest, largest):
    def one(axis_at, parts):
        heights = jax.random.uniform(jax.random.fold_in(jax.random.fold_in(stream_key, 6), axis_at), (parts,), jnp.float32, smallest / len(pieces), largest / len(pieces))
        return jnp.repeat(jnp.exp(heights), dims[axis_at] // parts).reshape((-1,) + (1,) * (len(dims) - axis_at - 1))

    level = one(*pieces[0])
    for cut in pieces[1:]:
        level = level * one(*cut)
    return level


def choose_distinct(stream_key, rows, number_of, top, lift):
    order = jax.random.permutation(jax.random.fold_in(stream_key, 1), number_of)
    boost = order
    for power in range(3):
        boost = boost * boost // number_of
    boost = boost * lift // number_of
    chance = jax.random.randint(jax.random.fold_in(stream_key, 2), (rows, number_of), 0, 4096) + boost
    sure = jax.random.permutation(jax.random.fold_in(stream_key, 3), rows)[jnp.arange(number_of) % rows]
    chance = jnp.where(jnp.arange(rows)[:, None] == sure[None, :], 1 << 14, chance)
    score = chance * number_of + jnp.arange(number_of)
    return lax.top_k(score.astype(jnp.int32), top)[1].astype(jnp.int32)


def normal_values(key, dims, deviation, limit, shards=(), kind=jnp.bfloat16):
    factor_of = block_levels(key, dims, shards, -0.22, 0.18) if shards else 1.0
    drawn = jax.random.normal(key, dims, jnp.float32) * deviation * factor_of
    return jnp.minimum(jnp.maximum(drawn, -limit), limit).astype(kind)


def heavy_noise(rng, dims, deviation, most, pieces, heavy, kind=jnp.bfloat16):
    drawn = deviation * jax.random.normal(rng, dims, jnp.float32)
    if pieces:
        drawn = drawn * block_levels(rng, dims, pieces, -0.22, 0.18)
    return jnp.clip(strengthened(drawn, jax.random.fold_in(rng, 3), *heavy), -most, most).astype(kind)


def setup_inputs(seed: int = 0, part: int = 0) -> dict:
    key_of = jax.random.split(jax.random.key(seed), 9)
    part_keys = jax.random.split(jax.random.fold_in(key_of[8], part), 9)
    features = normal_values(part_keys[0], (CLUSTERS, R, D), 1.0, 6.0, ((0, 16),))
    counts = draw_counts(jax.random.fold_in(jax.random.fold_in(key_of[8], part), 71), part)
    pick_owner = choose_distinct(part_keys[2], N_GRP, N_GRP, PICK, 8192)
    pick_local = set_ends(jax.random.randint(part_keys[3], (N_GRP, PICK), 0, OWN), jax.random.fold_in(part_keys[3], 1), 0, OWN - 1).astype(jnp.int32)
    adjacency = draw_adjacency(jax.random.fold_in(jax.random.fold_in(key_of[8], part), 71), part)
    cotangent = heavy_noise(part_keys[5], (N_GRP, ROWS, D), 1.0, 6.0, ((0, 16),), (0, 2, 16, 2.0))
    w_first = normal_values(key_of[6], (D, D), D ** -0.5, 0.1875)
    w_second = normal_values(key_of[7], (D, D), D ** -0.5, 0.1875)
    return dict(features=features, counts=counts, pick_owner=pick_owner, pick_local=pick_local, adjacency=adjacency, cotangent=cotangent, w_first=w_first, w_second=w_second)


def one_graph(features, counts, w_first, w_second, owners, picks, adj, cot):
    ids = (owners * OWN + picks).astype(jnp.int32)
    inputs = features[ids].reshape(PICK * R, D)
    live = counts[ids]
    mask = (jnp.arange(R)[None, :] < live[:, None]).reshape(PICK * R, 1).astype(jnp.bfloat16)
    inputs = inputs * mask
    maskf = mask.astype(jnp.float32)
    agg_first = jnp.dot(adj, inputs, preferred_element_type=jnp.float32).astype(jnp.bfloat16)
    pre = jnp.dot(agg_first, w_first, preferred_element_type=jnp.float32)
    hidden = (maskf * jax.nn.silu(pre)).astype(jnp.bfloat16)
    agg_second = jnp.dot(adj, hidden, preferred_element_type=jnp.float32).astype(jnp.bfloat16)
    output = (maskf * jnp.dot(agg_second, w_second, preferred_element_type=jnp.float32)).astype(jnp.bfloat16)
    dout = cot * mask
    grad_second = jnp.dot(dout.T, agg_second, preferred_element_type=jnp.float32)
    dagg = jnp.dot(dout, w_second.T, preferred_element_type=jnp.float32).astype(jnp.bfloat16)
    back = jnp.dot(adj.T, dagg, preferred_element_type=jnp.float32)
    sig = jax.nn.sigmoid(pre)
    dpre = (maskf * back * sig * (1.0 + pre * (1.0 - sig))).astype(jnp.bfloat16)
    grad_first = jnp.dot(dpre.T, agg_first, preferred_element_type=jnp.float32)
    return output, grad_first, grad_second


def reference(features, counts, pick_owner, pick_local, adjacency, cotangent, w_first, w_second):
    def step(carry, items):
        owners, picks, adj, cot = items
        output, grad_first, grad_second = one_graph(features, counts, w_first, w_second, owners, picks, adj, cot)
        return (carry[0] + grad_first, carry[1] + grad_second), output

    start = (jnp.zeros((D, D), jnp.float32), jnp.zeros((D, D), jnp.float32))
    sums, outputs = lax.scan(step, start, (pick_owner, pick_local, adjacency, cotangent))
    return outputs, sums[0], sums[1]
```

```python
import functools

import jax
import jax.numpy as jnp
from jax import lax
from jax.experimental import pallas as pl
from jax.experimental.pallas import tpu as pltpu
from jax.sharding import PartitionSpec as P

F32 = jnp.float32
BF16 = jnp.bfloat16
VMEM = pl.BlockSpec(memory_space=pltpu.VMEM)
SMEM = pl.BlockSpec(memory_space=pltpu.SMEM)
LANES = 128
META = 16


def nn(a, b):
    return jnp.dot(a, b, preferred_element_type=F32)


def nt(a, b):
    return lax.dot_general(a, b, (((1,), (1,)), ((), ())), preferred_element_type=F32)


def pack_kernel(counts, owner, local, features, adjacency, out):
    own, slots, width = features.shape
    rows = adjacency.shape[1]
    held = own * slots
    slot = lax.broadcasted_iota(jnp.int32, (slots, LANES), 0)
    for i in range(own):
        live = slot < counts[i]
        for b in range(width // LANES):
            block = features[i, :, b * LANES : (b + 1) * LANES]
            at = b * held + i * slots
            out[at : at + slots, :] = jnp.where(live, block, jnp.zeros_like(block))
    at = held * (width // LANES)
    out[at : at + rows, :] = adjacency[0]
    at += rows
    line = lax.broadcasted_iota(jnp.int32, (META, LANES), 0)
    pick = lax.broadcasted_iota(jnp.int32, (META, LANES), 1) // slots
    meta = jnp.zeros((META, LANES), jnp.int32)
    for k in range(owner.shape[1]):
        wanted = owner[0, k] * own + local[0, k]
        meta = jnp.where((line == 0) & (pick == k), wanted, meta)
    for i in range(own):
        meta = jnp.where(line == 1 + i, counts[i], meta)
    out[at : at + META, :] = meta.astype(F32).astype(BF16)


def columns_kernel(cotangent, w_second, out):
    n, both, _ = out.shape
    each = both // 2
    cot = cotangent[0]
    for d in range(n):
        part = cot[:, d * each : (d + 1) * each]
        out[d, :each, :] = part.astype(F32).T.astype(BF16)
    for d in range(n):
        out[d, each:, :] = nt(w_second[d * each : (d + 1) * each, :], cot).astype(BF16)


def step_kernel(n, own, slots, me, *refs):
    packs = refs[:n]
    columns, w_first, w_piece, w_second = refs[n : n + 4]
    output, grad_first, grad_second = refs[n + 4 : n + 7]
    feat, adj, lifted, total = refs[n + 7 :]
    width = w_first.shape[0]
    held = own * slots
    rows = adj.shape[1]
    each = grad_first.shape[0]
    clusters = n * own
    place = me[0]

    for s in range(n):
        for b in range(width // LANES):
            feat[s * held : (s + 1) * held, b * LANES : (b + 1) * LANES] = packs[s][
                b * held : (b + 1) * held, :
            ]
        at = held * (width // LANES)
        adj[s] = packs[s][at : at + rows, :]
    at = held * (width // LANES) + rows
    metas = [packs[s][at : at + META, :].astype(F32) for s in range(n)]
    picks = jnp.concatenate([m[0:1] for m in metas], axis=0).astype(jnp.int32)
    lane = lax.broadcasted_iota(jnp.int32, (n, LANES), 1) % slots
    count = jnp.zeros((n, LANES), jnp.int32)
    for s in range(n):
        for i in range(own):
            cluster = (place ^ s) * own + i
            count = jnp.where(picks == cluster, metas[s][1 + i : 2 + i].astype(jnp.int32), count)
    masks = (lane < count).astype(F32)
    wanted = picks * slots + lane
    code = lax.broadcasted_iota(jnp.int32, (clusters * slots, LANES), 0) ^ (place * held)

    lifted[...] = nn(feat[...], w_first[...]).astype(BF16)
    lifted_piece = nt(w_piece[...], feat[...]).astype(BF16)
    total[...] = jnp.zeros_like(total)

    moved = jnp.zeros((each, clusters * slots), F32)
    for j in range(n):
        chosen = jnp.where(code == wanted[j : j + 1], 1.0, 0.0).astype(BF16)
        spread = nt(adj[j], chosen).astype(BF16)
        pre = nn(spread, lifted[...])
        hidden = (pre / (1.0 + jnp.exp(-pre))).astype(BF16)
        mask = masks[j : j + 1]
        source = columns[place ^ j]
        back = nn((source.astype(F32) * mask).astype(BF16), adj[j]) * mask
        total[...] += nn(back[:each].astype(BF16), hidden)
        pre_piece = nt(lifted_piece, spread)
        sig = 1.0 / (1.0 + jnp.exp(-pre_piece))
        dpre = (back[each:] * sig * (1.0 + pre_piece * (1.0 - sig))).astype(BF16)
        moved += nn(dpre, spread)
        if j == 0:
            live = jnp.broadcast_to(mask, (rows, LANES)).T[:, :1]
            agg = nn(adj[0], (hidden.astype(F32) * live).astype(BF16)).astype(BF16)
            output[0] = (nn(agg, w_second[...]) * live).astype(BF16)
    grad_second[...] = total[...]
    grad_first[...] = nn(moved.astype(BF16), feat[...])


def gather_pieces(piece, n):
    def swap(x, s):
        return lax.ppermute(x, "grp", [(i, i ^ s) for i in range(n)])

    got = {0: piece}
    for s in range(4, n, 4):
        got[s] = swap(piece, s)
    for s in range(0, n, 4):
        if n > 2:
            got[s + 2] = swap(got[s], 2)
    for s in range(0, n, 2):
        if n > 1:
            got[s + 1] = swap(got[s], 1)
    return [got[s] for s in range(n)]


def whole_body(n, features, counts, pick_owner, pick_local, adjacency, cotangent, w_first, w_second):
    own, slots, width = features.shape
    rows = adjacency.shape[1]
    held = own * slots
    each = width // n
    piece_rows = held * (width // LANES) + rows + META
    piece = pl.pallas_call(
        pack_kernel,
        out_shape=jax.ShapeDtypeStruct((piece_rows, LANES), BF16),
        in_specs=[SMEM, SMEM, SMEM, VMEM, VMEM],
        out_specs=VMEM,
    )(counts, pick_owner, pick_local, features, adjacency)
    pieces = gather_pieces(piece, n)
    columns = pl.pallas_call(
        columns_kernel,
        out_shape=jax.ShapeDtypeStruct((n, 2 * each, rows), BF16),
        in_specs=[VMEM, VMEM],
        out_specs=VMEM,
        compiler_params=pltpu.CompilerParams(vmem_limit_bytes=32 * 2**20),
        cost_estimate=pl.CostEstimate(
            flops=2 * rows * width * width, bytes_accessed=3 * 2**20, transcendentals=0
        ),
    )(cotangent, w_second)
    columns = lax.all_to_all(columns, "grp", 0, 0, tiled=True)
    me = lax.axis_index("grp")
    w_piece = lax.dynamic_slice_in_dim(w_first, me * each, each, axis=1).T
    total_rows = n * held
    return pl.pallas_call(
        functools.partial(step_kernel, n, own, slots),
        out_shape=(
            jax.ShapeDtypeStruct((1, rows, width), BF16),
            jax.ShapeDtypeStruct((each, width), F32),
            jax.ShapeDtypeStruct((each, width), F32),
        ),
        in_specs=[SMEM] + [VMEM] * (n + 4),
        out_specs=(VMEM, VMEM, VMEM),
        scratch_shapes=[
            pltpu.VMEM((total_rows, width), BF16),
            pltpu.VMEM((n, rows, rows), BF16),
            pltpu.VMEM((total_rows, width), BF16),
            pltpu.VMEM((each, width), F32),
        ],
        compiler_params=pltpu.CompilerParams(vmem_limit_bytes=48 * 2**20),
        cost_estimate=pl.CostEstimate(
            flops=6 * 10**9, bytes_accessed=10 * 2**20, transcendentals=2 * 10**6
        ),
    )(me.reshape(1).astype(jnp.int32), *pieces, columns, w_first, w_piece, w_second)


def split_body(features, counts, pick_owner, pick_local, adjacency, cotangent, w_first, w_second):
    owners = pick_owner[0]
    picks = pick_local[0]
    width = w_first.shape[0]
    slots = features.shape[1]
    count_picks = owners.shape[0]
    wanted = owners * features.shape[0] + picks
    feat_piece = lax.all_gather(features, "grp", axis=0, tiled=True)
    count_piece = lax.all_gather(counts, "grp", axis=0, tiled=True)
    live = jnp.take(count_piece, wanted, axis=0)
    rows = count_picks * slots
    inputs = jnp.take(feat_piece, wanted, axis=0).reshape(rows, width)
    mask = (jnp.arange(slots)[None, :] < live[:, None]).reshape(rows, 1).astype(BF16)
    inputs = inputs * mask
    maskf = mask.astype(F32)
    adj = adjacency[0]
    agg_first = nn(adj, inputs).astype(BF16)
    pre = nn(agg_first, w_first)
    hidden = (maskf * jax.nn.silu(pre)).astype(BF16)
    agg_second = nn(adj, hidden).astype(BF16)
    output = (maskf * nn(agg_second, w_second)).astype(BF16)
    dout = cotangent[0] * mask

    def summed(a, b):
        part = lax.dot_general(a, b, (((0,), (0,)), ((), ())), preferred_element_type=F32)
        return lax.psum_scatter(part, "grp", scatter_dimension=0, tiled=True)

    grad_second = summed(dout, agg_second)
    dagg = nt(dout, w_second).astype(BF16)
    back = lax.dot_general(adj, dagg, (((0,), (0,)), ((), ())), preferred_element_type=F32)
    sig = jax.nn.sigmoid(pre)
    dpre = (maskf * back * sig * (1.0 + pre * (1.0 - sig))).astype(BF16)
    grad_first = summed(dpre, agg_first)
    return (output.reshape(1, rows, width), grad_first, grad_second)


def solution(mesh):
    n = mesh.shape["grp"]

    def body(*args):
        rows = args[4].shape[1]
        small = n & (n - 1) == 0 and rows == LANES and n * rows <= 4096
        return whole_body(n, *args) if small else split_body(*args)

    in_specs = (
        P(("parts", "grp"), None, None),
        P(("parts", "grp")),
        P(("parts", "grp"), None),
        P(("parts", "grp"), None),
        P(("parts", "grp"), None, None),
        P(("parts", "grp"), None, None),
        P(),
        P(),
    )
    out_specs = (
        P(("parts", "grp"), None, None),
        P(("parts", "grp"), None),
        P(("parts", "grp"), None),
    )
    return jax.shard_map(body, mesh=mesh, in_specs=in_specs, out_specs=out_specs, check_vma=False)
```

```python
import functools

import jax
import jax.numpy as jnp
from jax import lax
from jax.experimental import pallas as pl
from jax.experimental.pallas import tpu as pltpu
from jax.sharding import PartitionSpec as P

F32 = jnp.float32
BF16 = jnp.bfloat16
VMEM = pl.BlockSpec(memory_space=pltpu.VMEM)
SMEM = pl.BlockSpec(memory_space=pltpu.SMEM)
LANES = 128
META = 16


def nn(a, b):
    return jnp.dot(a, b, preferred_element_type=F32)


def nt(a, b):
    return lax.dot_general(a, b, (((1,), (1,)), ((), ())), preferred_element_type=F32)


def pack_kernel(counts, owner, local, features, adjacency, out):
    own, slots, width = features.shape
    rows = adjacency.shape[1]
    held = own * slots
    slot = lax.broadcasted_iota(jnp.int32, (slots, LANES), 0)
    for i in range(own):
        live = slot < counts[i]
        for b in range(width // LANES):
            block = features[i, :, b * LANES : (b + 1) * LANES]
            at = b * held + i * slots
            out[at : at + slots, :] = jnp.where(live, block, jnp.zeros_like(block))
    at = held * (width // LANES)
    out[at : at + rows, :] = adjacency[0]
    at += rows
    line = lax.broadcasted_iota(jnp.int32, (META, LANES), 0)
    pick = lax.broadcasted_iota(jnp.int32, (META, LANES), 1) // slots
    meta = jnp.zeros((META, LANES), jnp.int32)
    for k in range(owner.shape[1]):
        wanted = owner[0, k] * own + local[0, k]
        meta = jnp.where((line == 0) & (pick == k), wanted, meta)
    for i in range(own):
        meta = jnp.where(line == 1 + i, counts[i], meta)
    out[at : at + META, :] = meta.astype(F32).astype(BF16)


def columns_kernel(me, cotangent, w_second, w_first, out, w_piece):
    n, both, _ = out.shape
    each = both // 2
    cot = cotangent[0]
    for d in range(n):
        part = cot[:, d * each : (d + 1) * each]
        out[d, :each, :] = part.astype(F32).T.astype(BF16)
    for d in range(n):
        out[d, each:, :] = nt(w_second[d * each : (d + 1) * each, :], cot).astype(BF16)
    wide = max(each, LANES)
    per = wide // each
    start = pl.multiple_of((me[0] // per) * wide, wide)
    block = w_first[:, pl.ds(start, wide)].astype(F32).T
    part = block[:each]
    for q in range(1, per):
        part = jnp.where(me[0] % per == q, block[q * each : (q + 1) * each], part)
    w_piece[...] = part.astype(BF16)


def forward_kernel(n, own, slots, me, *refs):
    packs = refs[:n]
    w_first, w_piece, w_second = refs[n : n + 3]
    output, hidden, spread, feat, adj, masks, pre_piece = refs[n + 3 : n + 10]
    lifted = refs[n + 10]
    width = w_first.shape[0]
    held = own * slots
    rows = adj.shape[1]
    clusters = n * own
    place = me[0]

    for s in range(n):
        for b in range(width // LANES):
            feat[s * held : (s + 1) * held, b * LANES : (b + 1) * LANES] = packs[s][
                b * held : (b + 1) * held, :
            ]
        at = held * (width // LANES)
        adj[s] = packs[s][at : at + rows, :]
    at = held * (width // LANES) + rows
    metas = [packs[s][at : at + META, :].astype(F32) for s in range(n)]
    picks = jnp.concatenate([m[0:1] for m in metas], axis=0).astype(jnp.int32)
    lane = lax.broadcasted_iota(jnp.int32, (n, LANES), 1) % slots
    count = jnp.zeros((n, LANES), jnp.int32)
    for s in range(n):
        for i in range(own):
            cluster = (place ^ s) * own + i
            count = jnp.where(picks == cluster, metas[s][1 + i : 2 + i].astype(jnp.int32), count)
    masks[...] = (lane < count).astype(F32)
    wanted = picks * slots + lane
    code = lax.broadcasted_iota(jnp.int32, (clusters * slots, LANES), 0) ^ (place * held)

    lifted[...] = nn(feat[...], w_first[...]).astype(BF16)
    lifted_piece = nt(w_piece[...], feat[...]).astype(BF16)
    for j in range(n):
        chosen = jnp.where(code == wanted[j : j + 1], 1.0, 0.0).astype(BF16)
        spread[j * rows : (j + 1) * rows, :] = nt(adj[j], chosen).astype(BF16)
    step = min(width, 2 * LANES)
    for c in range(0, width, step):
        half = 0.5 * nn(spread[...], lifted[:, c : c + step])
        hidden[:, c : c + step] = (half + half * jnp.tanh(half)).astype(BF16)
    pre_piece[...] = nt(lifted_piece, spread[...])
    live = jnp.broadcast_to(masks[0:1, :], (rows, LANES)).T[:, :1]
    agg = nn(adj[0], (hidden[:rows, :].astype(F32) * live).astype(BF16)).astype(BF16)
    output[0] = (nn(agg, w_second[...]) * live).astype(BF16)


def gradient_kernel(n, me, columns, hidden, spread, feat, adj, masks, pre_piece, grad_first, grad_second, dout, dpre):
    each = grad_first.shape[0]
    rows = adj.shape[1]
    place = me[0]
    for j in range(n):
        mask = masks[j : j + 1, :]
        span = slice(j * rows, (j + 1) * rows)
        source = columns[place ^ j].astype(F32) * mask
        back = nn(source.astype(BF16), adj[j]) * mask
        dout[:, span] = back[:each].astype(BF16)
        pre = pre_piece[:, span]
        sig = 0.5 + 0.5 * jnp.tanh(0.5 * pre)
        dpre[:, span] = (back[each:] * sig * (1.0 + pre * (1.0 - sig))).astype(BF16)
    grad_second[...] = nn(dout[...], hidden[...])
    moved = nn(dpre[...], spread[...])
    grad_first[...] = nn(moved.astype(BF16), feat[...])


def gather_pieces(piece, n):
    def swap(x, s):
        return lax.ppermute(x, "grp", [(i, i ^ s) for i in range(n)])

    got = {0: piece}
    for s in range(4, n, 4):
        got[s] = swap(piece, s)
    for s in range(0, n, 4):
        if n > 2:
            got[s + 2] = swap(got[s], 2)
    for s in range(0, n, 2):
        if n > 1:
            got[s + 1] = swap(got[s], 1)
    return [got[s] for s in range(n)]


def whole_body(n, features, counts, pick_owner, pick_local, adjacency, cotangent, w_first, w_second):
    own, slots, width = features.shape
    rows = adjacency.shape[1]
    held = own * slots
    each = width // n
    piece_rows = held * (width // LANES) + rows + META
    piece = pl.pallas_call(
        pack_kernel,
        out_shape=jax.ShapeDtypeStruct((piece_rows, LANES), BF16),
        in_specs=[SMEM, SMEM, SMEM, VMEM, VMEM],
        out_specs=VMEM,
    )(counts, pick_owner, pick_local, features, adjacency)
    pieces = gather_pieces(piece, n)
    me = lax.axis_index("grp").reshape(1).astype(jnp.int32)
    limit = pltpu.CompilerParams(vmem_limit_bytes=24 * 2**20)
    cotangent, _ = lax.optimization_barrier((cotangent, piece))
    columns, w_piece = pl.pallas_call(
        columns_kernel,
        out_shape=(
            jax.ShapeDtypeStruct((n, 2 * each, rows), BF16),
            jax.ShapeDtypeStruct((each, width), BF16),
        ),
        in_specs=[SMEM, VMEM, VMEM, VMEM],
        out_specs=(VMEM, VMEM),
        compiler_params=limit,
        cost_estimate=pl.CostEstimate(
            flops=2 * rows * width * width, bytes_accessed=5 * 2**20, transcendentals=0
        ),
    )(me, cotangent, w_second, w_first)
    columns = lax.all_to_all(columns, "grp", 0, 0, tiled=True)
    total_rows = n * held
    output, *kept = pl.pallas_call(
        functools.partial(forward_kernel, n, own, slots),
        out_shape=(
            jax.ShapeDtypeStruct((1, rows, width), BF16),
            jax.ShapeDtypeStruct((n * rows, width), BF16),
            jax.ShapeDtypeStruct((n * rows, total_rows), BF16),
            jax.ShapeDtypeStruct((total_rows, width), BF16),
            jax.ShapeDtypeStruct((n, rows, rows), BF16),
            jax.ShapeDtypeStruct((n, LANES), F32),
            jax.ShapeDtypeStruct((each, n * rows), F32),
        ),
        in_specs=[SMEM] + [VMEM] * (n + 3),
        out_specs=(VMEM,) * 7,
        scratch_shapes=[pltpu.VMEM((total_rows, width), BF16)],
        compiler_params=limit,
        cost_estimate=pl.CostEstimate(
            flops=4 * 10**9, bytes_accessed=10 * 2**20, transcendentals=2 * 10**6
        ),
    )(me, *pieces, w_first, w_piece, w_second)
    grad_first, grad_second = pl.pallas_call(
        functools.partial(gradient_kernel, n),
        out_shape=(jax.ShapeDtypeStruct((each, width), F32),) * 2,
        in_specs=[SMEM] + [VMEM] * 7,
        out_specs=(VMEM,) * 2,
        scratch_shapes=[pltpu.VMEM((each, n * rows), BF16)] * 2,
        compiler_params=limit,
        cost_estimate=pl.CostEstimate(
            flops=10**9, bytes_accessed=8 * 2**20, transcendentals=10**5
        ),
    )(me, columns, *kept)
    return output, grad_first, grad_second


def split_body(features, counts, pick_owner, pick_local, adjacency, cotangent, w_first, w_second):
    owners = pick_owner[0]
    picks = pick_local[0]
    width = w_first.shape[0]
    slots = features.shape[1]
    count_picks = owners.shape[0]
    wanted = owners * features.shape[0] + picks
    feat_piece = lax.all_gather(features, "grp", axis=0, tiled=True)
    count_piece = lax.all_gather(counts, "grp", axis=0, tiled=True)
    live = jnp.take(count_piece, wanted, axis=0)
    rows = count_picks * slots
    inputs = jnp.take(feat_piece, wanted, axis=0).reshape(rows, width)
    mask = (jnp.arange(slots)[None, :] < live[:, None]).reshape(rows, 1).astype(BF16)
    inputs = inputs * mask
    maskf = mask.astype(F32)
    adj = adjacency[0]
    agg_first = nn(adj, inputs).astype(BF16)
    pre = nn(agg_first, w_first)
    hidden = (maskf * jax.nn.silu(pre)).astype(BF16)
    agg_second = nn(adj, hidden).astype(BF16)
    output = (maskf * nn(agg_second, w_second)).astype(BF16)
    dout = cotangent[0] * mask

    def summed(a, b):
        part = lax.dot_general(a, b, (((0,), (0,)), ((), ())), preferred_element_type=F32)
        return lax.psum_scatter(part, "grp", scatter_dimension=0, tiled=True)

    grad_second = summed(dout, agg_second)
    dagg = nt(dout, w_second).astype(BF16)
    back = lax.dot_general(adj, dagg, (((0,), (0,)), ((), ())), preferred_element_type=F32)
    sig = jax.nn.sigmoid(pre)
    dpre = (maskf * back * sig * (1.0 + pre * (1.0 - sig))).astype(BF16)
    grad_first = summed(dpre, agg_first)
    return (output.reshape(1, rows, width), grad_first, grad_second)


def solution(mesh):
    n = mesh.shape["grp"]

    def body(*args):
        rows = args[4].shape[1]
        small = n & (n - 1) == 0 and rows == LANES and n * rows <= 4096
        return whole_body(n, *args) if small else split_body(*args)

    in_specs = (
        P(("parts", "grp"), None, None),
        P(("parts", "grp")),
        P(("parts", "grp"), None),
        P(("parts", "grp"), None),
        P(("parts", "grp"), None, None),
        P(("parts", "grp"), None, None),
        P(),
        P(),
    )
    out_specs = (
        P(("parts", "grp"), None, None),
        P(("parts", "grp"), None),
        P(("parts", "grp"), None),
    )
    return jax.shard_map(body, mesh=mesh, in_specs=in_specs, out_specs=out_specs, check_vma=False)
```

```python
import functools

import jax
import jax.numpy as jnp
from jax import lax
from jax.experimental import pallas as pl
from jax.experimental.pallas import tpu as pltpu
from jax.sharding import PartitionSpec as P

F32 = jnp.float32
BF16 = jnp.bfloat16
VMEM = pl.BlockSpec(memory_space=pltpu.VMEM)
SMEM = pl.BlockSpec(memory_space=pltpu.SMEM)
HBM = pl.BlockSpec(memory_space=pltpu.HBM)
PLANE = 4
LANES = 128
META = 16


def nn(a, b):
    return jnp.dot(a, b, preferred_element_type=F32)


def nt(a, b):
    return lax.dot_general(a, b, (((1,), (1,)), ((), ())), preferred_element_type=F32)


def pack_kernel(counts, owner, local, features, adjacency, out):
    own, slots, width = features.shape
    rows = adjacency.shape[1]
    held = own * slots
    slot = lax.broadcasted_iota(jnp.int32, (slots, LANES), 0)
    for i in range(own):
        live = slot < counts[i]
        for b in range(width // LANES):
            block = features[i, :, b * LANES : (b + 1) * LANES]
            at = b * held + i * slots
            out[at : at + slots, :] = jnp.where(live, block, jnp.zeros_like(block))
    at = held * (width // LANES)
    out[at : at + rows, :] = adjacency[0]
    at += rows
    line = lax.broadcasted_iota(jnp.int32, (META, LANES), 0)
    pick = lax.broadcasted_iota(jnp.int32, (META, LANES), 1) // slots
    meta = jnp.zeros((META, LANES), jnp.int32)
    for k in range(owner.shape[1]):
        wanted = owner[0, k] * own + local[0, k]
        meta = jnp.where((line == 0) & (pick == k), wanted, meta)
    for i in range(own):
        meta = jnp.where(line == 1 + i, counts[i], meta)
    out[at : at + META, :] = meta.astype(F32).astype(BF16)


def columns_kernel(me, cotangent, w_second, w_first, *refs):
    *outs, w_piece, turned, back, second, strip, sems = refs
    each = w_piece.shape[0]
    wide = strip.shape[1]
    per = wide // each
    start = pl.multiple_of((me[0] // per) * wide, wide)
    weights = pltpu.make_async_copy(w_second, second, sems.at[0])
    weights.start()
    columns = pltpu.make_async_copy(w_first.at[:, pl.ds(start, wide)], strip, sems.at[1])
    columns.start()
    cot = cotangent[0]
    turned[...] = cot.astype(F32).T.astype(BF16)
    weights.wait()
    back[...] = nt(second[...], cot).astype(BF16)
    for q, out in enumerate(outs):
        for s in range(out.shape[0] // (2 * each)):
            span = pl.ds(pl.multiple_of((me[0] ^ (PLANE * s + q)) * each, each), each)
            at = s * 2 * each
            out[at : at + each, :] = turned[span, :]
            out[at + each : at + 2 * each, :] = back[span, :]
    columns.wait()
    block = strip[...].astype(F32).T
    part = block[:each]
    for q in range(1, per):
        part = jnp.where(me[0] % per == q, block[q * each : (q + 1) * each], part)
    w_piece[...] = part.astype(BF16)


def regroup_kernel(parts, *refs):
    pieces, columns = refs[:parts], refs[parts : parts + PLANE]
    stack, *sent = refs[parts + PLANE :]
    rows = pieces[0].shape[0]
    for i, ref in enumerate(pieces):
        stack[i * rows : (i + 1) * rows, :] = ref[...]
    rows = sent[0].shape[0] // PLANE
    for s, out in enumerate(sent, 1):
        for q, ref in enumerate(columns):
            out[q * rows : (q + 1) * rows, :] = ref[s * rows : (s + 1) * rows, :]


def forward_kernel(n, own, slots, me, *refs):
    packs = refs[:PLANE]
    w_first, w_piece, w_second = refs[PLANE : PLANE + 3]
    output, hidden, spread, feat, adj, masks, pre_piece = refs[PLANE + 3 : PLANE + 10]
    lifted, first, second, sems = refs[PLANE + 10 :]
    first_copy = pltpu.make_async_copy(w_first, first, sems.at[0])
    first_copy.start()
    second_copy = pltpu.make_async_copy(w_second, second, sems.at[1])
    second_copy.start()
    width = w_first.shape[0]
    held = own * slots
    rows = adj.shape[1]
    clusters = n * own
    place = me[0]
    deep = held * (width // LANES) + rows + META

    metas = []
    for s in range(n):
        pack, at = packs[s % PLANE], (s // PLANE) * deep
        for b in range(width // LANES):
            feat[s * held : (s + 1) * held, b * LANES : (b + 1) * LANES] = pack[at : at + held, :]
            at += held
        adj[s] = pack[at : at + rows, :]
        at += rows
        metas.append(pack[at : at + META, :].astype(F32))
    picks = jnp.concatenate([m[0:1] for m in metas], axis=0).astype(jnp.int32)
    lane = lax.broadcasted_iota(jnp.int32, (n, LANES), 1) % slots
    count = jnp.zeros((n, LANES), jnp.int32)
    for s in range(n):
        for i in range(own):
            cluster = (place ^ s) * own + i
            count = jnp.where(picks == cluster, metas[s][1 + i : 2 + i].astype(jnp.int32), count)
    masks[...] = (lane < count).astype(F32)
    wanted = picks * slots + lane
    code = lax.broadcasted_iota(jnp.int32, (clusters * slots, LANES), 0) ^ (place * held)

    for j in range(n):
        chosen = jnp.where(code == wanted[j : j + 1], 1.0, 0.0).astype(BF16)
        spread[j * rows : (j + 1) * rows, :] = nt(adj[j], chosen).astype(BF16)
    first_copy.wait()
    lifted[...] = nn(feat[...], first[...]).astype(BF16)
    lifted_piece = nt(w_piece[...], feat[...]).astype(BF16)
    step = min(width, 2 * LANES)
    for c in range(0, width, step):
        half = 0.5 * nn(spread[...], lifted[:, c : c + step])
        hidden[:, c : c + step] = (half + half * jnp.tanh(half)).astype(BF16)
    pre_piece[...] = nt(lifted_piece, spread[...])
    live = jnp.broadcast_to(masks[0:1, :], (rows, LANES)).T[:, :1]
    agg = nn(adj[0], (hidden[:rows, :].astype(F32) * live).astype(BF16)).astype(BF16)
    second_copy.wait()
    output[0] = (nn(agg, second[...]) * live).astype(BF16)


def gradient_kernel(n, *refs):
    mine, sent = refs[:PLANE], refs[PLANE : PLANE + n // PLANE - 1]
    hidden, spread, feat, adj, masks, pre_piece = refs[PLANE + len(sent) :][:6]
    grad_first, grad_second, dout, dpre = refs[PLANE + len(sent) + 6 :]
    each = grad_first.shape[0]
    rows = adj.shape[1]
    for j in range(n):
        mask = masks[j : j + 1, :]
        span = slice(j * rows, (j + 1) * rows)
        s, q = divmod(j, PLANE)
        source = sent[s - 1][q * 2 * each : (q + 1) * 2 * each, :] if s else mine[q][: 2 * each, :]
        back = nn((source.astype(F32) * mask).astype(BF16), adj[j]) * mask
        dout[:, span] = back[:each].astype(BF16)
        pre = pre_piece[:, span]
        sig = 0.5 + 0.5 * jnp.tanh(0.5 * pre)
        dpre[:, span] = (back[each:] * sig * (1.0 + pre * (1.0 - sig))).astype(BF16)
    grad_second[...] = nn(dout[...], hidden[...])
    moved = nn(dpre[...], spread[...])
    grad_first[...] = nn(moved.astype(BF16), feat[...])


def whole_body(n, features, counts, pick_owner, pick_local, adjacency, cotangent, w_first, w_second):
    own, slots, width = features.shape
    rows = adjacency.shape[1]
    held = own * slots
    each = width // n
    total_rows = n * held
    piece_rows = held * (width // LANES) + rows + META
    limit = pltpu.CompilerParams(vmem_limit_bytes=24 * 2**20)
    me = lax.axis_index("grp").reshape(1).astype(jnp.int32)

    def swap(x, s):
        return lax.ppermute(x, "grp", [(i, i ^ s) for i in range(n)])

    piece = pl.pallas_call(
        pack_kernel,
        out_shape=jax.ShapeDtypeStruct((piece_rows, LANES), BF16),
        in_specs=[SMEM, SMEM, SMEM, VMEM, VMEM],
        out_specs=VMEM,
    )(counts, pick_owner, pick_local, features, adjacency)

    far = range(PLANE, n, PLANE)
    along = [swap(piece, s) for s in far]
    cotangent, _ = lax.optimization_barrier((cotangent, piece))
    *columns, w_piece = pl.pallas_call(
        columns_kernel,
        out_shape=(jax.ShapeDtypeStruct((n // PLANE * 2 * each, rows), BF16),) * PLANE
        + (jax.ShapeDtypeStruct((each, width), BF16),),
        in_specs=[SMEM, VMEM, HBM, HBM],
        out_specs=(VMEM,) * (PLANE + 1),
        scratch_shapes=[
            pltpu.VMEM((width, rows), BF16),
            pltpu.VMEM((width, rows), BF16),
            pltpu.VMEM((width, width), BF16),
            pltpu.VMEM((width, max(each, LANES)), BF16),
            pltpu.SemaphoreType.DMA((2,)),
        ],
        compiler_params=limit,
        cost_estimate=pl.CostEstimate(
            flops=2 * rows * width * width, bytes_accessed=3 * 2**20, transcendentals=0
        ),
    )(me, cotangent, w_second, w_first)
    columns = [columns[0]] + [swap(columns[q], q) for q in range(1, PLANE)]
    stack, *sent = pl.pallas_call(
        functools.partial(regroup_kernel, n // PLANE),
        out_shape=(jax.ShapeDtypeStruct((n // PLANE * piece_rows, LANES), BF16),)
        + (jax.ShapeDtypeStruct((PLANE * 2 * each, rows), BF16),) * len(far),
        in_specs=[VMEM] * (n // PLANE + PLANE),
        out_specs=(VMEM,) * (1 + len(far)),
        compiler_params=limit,
    )(piece, *along, *columns)
    across = swap(stack, 2)
    pieces = [stack, swap(stack, 1), across, swap(across, 1)]
    sent = [swap(x, s) for x, s in zip(sent, far)]

    output, *kept = pl.pallas_call(
        functools.partial(forward_kernel, n, own, slots),
        out_shape=(
            jax.ShapeDtypeStruct((1, rows, width), BF16),
            jax.ShapeDtypeStruct((n * rows, width), BF16),
            jax.ShapeDtypeStruct((n * rows, total_rows), BF16),
            jax.ShapeDtypeStruct((total_rows, width), BF16),
            jax.ShapeDtypeStruct((n, rows, rows), BF16),
            jax.ShapeDtypeStruct((n, LANES), F32),
            jax.ShapeDtypeStruct((each, n * rows), F32),
        ),
        in_specs=[SMEM] + [VMEM] * PLANE + [HBM, VMEM, HBM],
        out_specs=(VMEM,) * 7,
        scratch_shapes=[
            pltpu.VMEM((total_rows, width), BF16),
            pltpu.VMEM((width, width), BF16),
            pltpu.VMEM((width, width), BF16),
            pltpu.SemaphoreType.DMA((2,)),
        ],
        compiler_params=limit,
        cost_estimate=pl.CostEstimate(
            flops=4 * 10**9, bytes_accessed=10 * 2**20, transcendentals=2 * 10**6
        ),
    )(me, *pieces, w_first, w_piece, w_second)
    grad_first, grad_second = pl.pallas_call(
        functools.partial(gradient_kernel, n),
        out_shape=(jax.ShapeDtypeStruct((each, width), F32),) * 2,
        in_specs=[VMEM] * (PLANE + len(far) + 6),
        out_specs=(VMEM,) * 2,
        scratch_shapes=[pltpu.VMEM((each, n * rows), BF16)] * 2,
        compiler_params=limit,
        cost_estimate=pl.CostEstimate(
            flops=10**9, bytes_accessed=8 * 2**20, transcendentals=10**5
        ),
    )(*columns, *sent, *kept)
    return output, grad_first, grad_second


def split_body(features, counts, pick_owner, pick_local, adjacency, cotangent, w_first, w_second):
    owners = pick_owner[0]
    picks = pick_local[0]
    width = w_first.shape[0]
    slots = features.shape[1]
    count_picks = owners.shape[0]
    wanted = owners * features.shape[0] + picks
    feat_piece = lax.all_gather(features, "grp", axis=0, tiled=True)
    count_piece = lax.all_gather(counts, "grp", axis=0, tiled=True)
    live = jnp.take(count_piece, wanted, axis=0)
    rows = count_picks * slots
    inputs = jnp.take(feat_piece, wanted, axis=0).reshape(rows, width)
    mask = (jnp.arange(slots)[None, :] < live[:, None]).reshape(rows, 1).astype(BF16)
    inputs = inputs * mask
    maskf = mask.astype(F32)
    adj = adjacency[0]
    agg_first = nn(adj, inputs).astype(BF16)
    pre = nn(agg_first, w_first)
    hidden = (maskf * jax.nn.silu(pre)).astype(BF16)
    agg_second = nn(adj, hidden).astype(BF16)
    output = (maskf * nn(agg_second, w_second)).astype(BF16)
    dout = cotangent[0] * mask

    def summed(a, b):
        part = lax.dot_general(a, b, (((0,), (0,)), ((), ())), preferred_element_type=F32)
        return lax.psum_scatter(part, "grp", scatter_dimension=0, tiled=True)

    grad_second = summed(dout, agg_second)
    dagg = nt(dout, w_second).astype(BF16)
    back = lax.dot_general(adj, dagg, (((0,), (0,)), ((), ())), preferred_element_type=F32)
    sig = jax.nn.sigmoid(pre)
    dpre = (maskf * back * sig * (1.0 + pre * (1.0 - sig))).astype(BF16)
    grad_first = summed(dpre, agg_first)
    return (output.reshape(1, rows, width), grad_first, grad_second)


def solution(mesh):
    n = mesh.shape["grp"]

    def body(*args):
        rows = args[4].shape[1]
        small = n & (n - 1) == 0 and n > PLANE and rows == LANES and n * rows <= 4096
        return whole_body(n, *args) if small else split_body(*args)

    in_specs = (
        P(("parts", "grp"), None, None),
        P(("parts", "grp")),
        P(("parts", "grp"), None),
        P(("parts", "grp"), None),
        P(("parts", "grp"), None, None),
        P(("parts", "grp"), None, None),
        P(),
        P(),
    )
    out_specs = (
        P(("parts", "grp"), None, None),
        P(("parts", "grp"), None),
        P(("parts", "grp"), None),
    )
    return jax.shard_map(body, mesh=mesh, in_specs=in_specs, out_specs=out_specs, check_vma=False)
```

```python
import functools

import jax
import jax.numpy as jnp
from jax import lax
from jax.experimental import pallas as pl
from jax.experimental.pallas import tpu as pltpu
from jax.sharding import PartitionSpec as P

F32 = jnp.float32
BF16 = jnp.bfloat16
VMEM = pl.BlockSpec(memory_space=pltpu.VMEM)
SMEM = pl.BlockSpec(memory_space=pltpu.SMEM)
ANY = pl.BlockSpec(memory_space=pl.ANY)
PLANE = 4
LIMIT = 60 * 2**20
SMALL = 8 * 2**20
CHUNKS = 4
LANES = 128
META = 16


def nn(a, b):
    return jnp.dot(a, b, preferred_element_type=F32)


def nt(a, b):
    return lax.dot_general(a, b, (((1,), (1,)), ((), ())), preferred_element_type=F32)


def prepare_kernel(me, counts, owner, local, features, adjacency, cotangent, w_second, w_first, *refs):
    piece, near, across, w_piece, feat, adj, cot, turned, back, second, strip, sems = refs
    own, slots, width = features.shape
    rows = adjacency.shape[1]
    each = w_piece.shape[0]
    wide = strip.shape[1]
    per = wide // each
    start = pl.multiple_of((me[0] // per) * wide, wide)
    moves = [(features, feat), (adjacency, adj), (cotangent, cot)]
    some = width // CHUNKS
    for c in range(CHUNKS):
        moves.append((w_second.at[c * some : (c + 1) * some], second.at[c * some : (c + 1) * some]))
    moves.append((w_first.at[:, pl.ds(start, wide)], strip))
    copies = [pltpu.make_async_copy(a, b, sems.at[i]) for i, (a, b) in enumerate(moves)]
    for copy in copies:
        copy.start()

    held = own * slots
    slot = lax.broadcasted_iota(jnp.int32, (slots, LANES), 0)
    copies[0].wait()
    for i in range(own):
        live = slot < counts[i]
        for b in range(width // LANES):
            block = feat[i, :, b * LANES : (b + 1) * LANES]
            at = b * held + i * slots
            piece[at : at + slots, :] = jnp.where(live, block, jnp.zeros_like(block))
    at = held * (width // LANES)
    copies[1].wait()
    piece[at : at + rows, :] = adj[0]
    at += rows
    line = lax.broadcasted_iota(jnp.int32, (META, LANES), 0)
    pick = lax.broadcasted_iota(jnp.int32, (META, LANES), 1) // slots
    meta = jnp.zeros((META, LANES), jnp.int32)
    for k in range(owner.shape[1]):
        wanted = owner[0, k] * own + local[0, k]
        meta = jnp.where((line == 0) & (pick == k), wanted, meta)
    for i in range(own):
        meta = jnp.where(line == 1 + i, counts[i], meta)
    piece[at : at + META, :] = meta.astype(F32).astype(BF16)

    copies[2].wait()
    turned[...] = cot[0].astype(F32).T.astype(BF16)
    for c in range(CHUNKS):
        copies[3 + c].wait()
        span = slice(c * some, (c + 1) * some)
        back[span, :] = nt(second[span, :], cot[0]).astype(BF16)
    for h, out in enumerate((near, across)):
        for i in range(out.shape[0] // (2 * each)):
            to = PLANE * (i // 2) + 2 * h + i % 2
            span = pl.ds(pl.multiple_of((me[0] ^ to) * each, each), each)
            at = i * 2 * each
            out[at : at + each, :] = turned[span, :]
            out[at + each : at + 2 * each, :] = back[span, :]
    copies[3 + CHUNKS].wait()
    block = strip[...].astype(F32).T
    part = block[:each]
    for q in range(1, per):
        part = jnp.where(me[0] % per == q, block[q * each : (q + 1) * each], part)
    w_piece[...] = part.astype(BF16)


def regroup_kernel(parts, *refs):
    pieces, near, across = refs[:parts], refs[parts], refs[parts + 1]
    stack, *sent = refs[parts + 2 :]
    rows = pieces[0].shape[0]
    for i, ref in enumerate(pieces):
        stack[i * rows : (i + 1) * rows, :] = ref[...]
    half = sent[0].shape[0] // 2
    for s, out in enumerate(sent, 1):
        out[:half, :] = near[s * half : (s + 1) * half, :]
        out[half:, :] = across[s * half : (s + 1) * half, :]


def pair_kernel(parts, across, near, other, *refs):
    sent, out = refs[: parts - 1], refs[parts - 1]
    deep = across.shape[0]
    out[:deep, :] = across[...]
    half = near.shape[0] // parts
    rows = half // 2
    for s in range(parts):
        for h in range(2):
            if s:
                block = sent[s - 1][h * half + rows : (h + 1) * half, :]
            else:
                block = (near, other)[h][rows:half, :]
            at = deep + (2 * s + h) * rows
            out[at : at + rows, :] = block


def step_kernel(n, own, slots, me, *refs):
    parts = n // PLANE
    packs = refs[:PLANE]
    pair = packs[3]
    near, other, *sent = refs[PLANE : PLANE + parts + 1]
    w_first, w_piece, w_second = refs[PLANE + parts + 1 : PLANE + parts + 4]
    output, grad_first, grad_second = refs[PLANE + parts + 4 : PLANE + parts + 7]
    hidden, spread, feat, adj, dout, dpre, lifted, first, second, sems = refs[PLANE + parts + 7 :]
    first_copy = pltpu.make_async_copy(w_first, first, sems.at[0])
    first_copy.start()
    second_copy = pltpu.make_async_copy(w_second, second, sems.at[1])
    second_copy.start()
    width = w_first.shape[0]
    held = own * slots
    rows = adj.shape[1]
    clusters = n * own
    place = me[0]
    deep = held * (width // LANES) + rows + META

    metas = []
    for s in range(n):
        pack, at = packs[s % PLANE], (s // PLANE) * deep
        for b in range(width // LANES):
            feat[s * held : (s + 1) * held, b * LANES : (b + 1) * LANES] = pack[at : at + held, :]
            at += held
        adj[s] = pack[at : at + rows, :]
        at += rows
        metas.append(pack[at : at + META, :].astype(F32))
    picks = jnp.concatenate([m[0:1] for m in metas], axis=0).astype(jnp.int32)
    lane = lax.broadcasted_iota(jnp.int32, (n, LANES), 1) % slots
    count = jnp.zeros((n, LANES), jnp.int32)
    for s in range(n):
        for i in range(own):
            cluster = (place ^ s) * own + i
            count = jnp.where(picks == cluster, metas[s][1 + i : 2 + i].astype(jnp.int32), count)
    masks = (lane < count).astype(F32)
    wanted = picks * slots + lane
    code = lax.broadcasted_iota(jnp.int32, (clusters * slots, LANES), 0) ^ (place * held)

    for j in range(n):
        chosen = jnp.where(code == wanted[j : j + 1], 1.0, 0.0).astype(BF16)
        spread[j * rows : (j + 1) * rows, :] = nt(adj[j], chosen).astype(BF16)
    first_copy.wait()
    lifted[...] = nn(feat[...], first[...]).astype(BF16)
    lifted_piece = nt(w_piece[...], feat[...]).astype(BF16)
    step = min(width, 2 * LANES)
    for c in range(0, width, step):
        half = 0.5 * nn(spread[...], lifted[:, c : c + step])
        hidden[:, c : c + step] = (half + half * jnp.tanh(half)).astype(BF16)
    pre_piece = nt(lifted_piece, spread[...])
    live = jnp.broadcast_to(masks[0:1], (rows, LANES)).T[:, :1]
    agg = nn(adj[0], (hidden[:rows, :].astype(F32) * live).astype(BF16)).astype(BF16)
    second_copy.wait()
    output[0] = (nn(agg, second[...]) * live).astype(BF16)

    each = grad_first.shape[0]
    half = near.shape[0] // parts
    deep *= parts
    for j in range(n):
        mask = masks[j : j + 1]
        span = slice(j * rows, (j + 1) * rows)
        s, h, b = j // PLANE, j % PLANE // 2, j % 2
        if b:
            at = deep + (2 * s + h) * 2 * each
            source = pair[at : at + 2 * each, :]
        elif s:
            source = sent[s - 1][h * half : h * half + 2 * each, :]
        else:
            source = (near, other)[h][: 2 * each, :]
        back = nn((source.astype(F32) * mask).astype(BF16), adj[j]) * mask
        dout[:, span] = back[:each].astype(BF16)
        pre = pre_piece[:, span]
        sig = 0.5 + 0.5 * jnp.tanh(0.5 * pre)
        dpre[:, span] = (back[each:] * sig * (1.0 + pre * (1.0 - sig))).astype(BF16)
    grad_second[...] = nn(dout[...], hidden[...])
    moved = nn(dpre[...], spread[...])
    grad_first[...] = nn(moved.astype(BF16), feat[...])


def whole_body(n, features, counts, pick_owner, pick_local, adjacency, cotangent, w_first, w_second):
    own, slots, width = features.shape
    rows = adjacency.shape[1]
    held = own * slots
    each = width // n
    total_rows = n * held
    piece_rows = held * (width // LANES) + rows + META
    limit = pltpu.CompilerParams(vmem_limit_bytes=LIMIT)
    me = lax.axis_index("grp").reshape(1).astype(jnp.int32)

    def swap(x, s):
        return lax.ppermute(x, "grp", [(i, i ^ s) for i in range(n)])

    piece, near, other, w_piece = pl.pallas_call(
        prepare_kernel,
        out_shape=(
            jax.ShapeDtypeStruct((piece_rows, LANES), BF16),
            jax.ShapeDtypeStruct((n * each, rows), BF16),
            jax.ShapeDtypeStruct((n * each, rows), BF16),
            jax.ShapeDtypeStruct((each, width), BF16),
        ),
        in_specs=[SMEM] * 4 + [ANY] * 5,
        out_specs=(VMEM,) * 4,
        scratch_shapes=[
            pltpu.VMEM(features.shape, BF16),
            pltpu.VMEM(adjacency.shape, BF16),
            pltpu.VMEM(cotangent.shape, BF16),
            pltpu.VMEM((width, rows), BF16),
            pltpu.VMEM((width, rows), BF16),
            pltpu.VMEM((width, width), BF16),
            pltpu.VMEM((width, max(each, LANES)), BF16),
            pltpu.SemaphoreType.DMA((4 + CHUNKS,)),
        ],
        compiler_params=limit,
    )(me, counts, pick_owner, pick_local, features, adjacency, cotangent, w_second, w_first)
    far = range(PLANE, n, PLANE)
    parts = n // PLANE
    along = [swap(piece, s) for s in far]
    other = swap(other, 2)
    stack, *sent = pl.pallas_call(
        functools.partial(regroup_kernel, parts),
        out_shape=(jax.ShapeDtypeStruct((parts * piece_rows, LANES), BF16),)
        + (jax.ShapeDtypeStruct((PLANE * 2 * each, rows), BF16),) * len(far),
        in_specs=[VMEM] * (parts + 2),
        out_specs=(VMEM,) * parts,
        compiler_params=pltpu.CompilerParams(vmem_limit_bytes=SMALL),
    )(piece, *along, near, other)
    sent = [swap(x, s) for x, s in zip(sent, far)]
    beside = swap(stack, 1)
    across = swap(stack, 2)
    pair = pl.pallas_call(
        functools.partial(pair_kernel, parts),
        out_shape=jax.ShapeDtypeStruct((parts * piece_rows + n * each, LANES), BF16),
        in_specs=[VMEM] * (parts + 2),
        out_specs=VMEM,
        compiler_params=pltpu.CompilerParams(vmem_limit_bytes=SMALL),
    )(across, near, other, *sent)
    pair = swap(pair, 1)
    pieces = [stack, beside, across, pair]

    return pl.pallas_call(
        functools.partial(step_kernel, n, own, slots),
        out_shape=(
            jax.ShapeDtypeStruct((1, rows, width), BF16),
            jax.ShapeDtypeStruct((each, width), F32),
            jax.ShapeDtypeStruct((each, width), F32),
        ),
        in_specs=[SMEM] + [VMEM] * (PLANE + parts + 1) + [ANY, VMEM, ANY],
        out_specs=(VMEM,) * 3,
        scratch_shapes=[
            pltpu.VMEM((n * rows, width), BF16),
            pltpu.VMEM((n * rows, total_rows), BF16),
            pltpu.VMEM((total_rows, width), BF16),
            pltpu.VMEM((n, rows, rows), BF16),
            pltpu.VMEM((each, n * rows), BF16),
            pltpu.VMEM((each, n * rows), BF16),
            pltpu.VMEM((total_rows, width), BF16),
            pltpu.VMEM((width, width), BF16),
            pltpu.VMEM((width, width), BF16),
            pltpu.SemaphoreType.DMA((2,)),
        ],
        compiler_params=limit,
    )(me, *pieces, near, other, *sent, w_first, w_piece, w_second)


def split_body(features, counts, pick_owner, pick_local, adjacency, cotangent, w_first, w_second):
    owners = pick_owner[0]
    picks = pick_local[0]
    width = w_first.shape[0]
    slots = features.shape[1]
    count_picks = owners.shape[0]
    wanted = owners * features.shape[0] + picks
    feat_piece = lax.all_gather(features, "grp", axis=0, tiled=True)
    count_piece = lax.all_gather(counts, "grp", axis=0, tiled=True)
    live = jnp.take(count_piece, wanted, axis=0)
    rows = count_picks * slots
    inputs = jnp.take(feat_piece, wanted, axis=0).reshape(rows, width)
    mask = (jnp.arange(slots)[None, :] < live[:, None]).reshape(rows, 1).astype(BF16)
    inputs = inputs * mask
    maskf = mask.astype(F32)
    adj = adjacency[0]
    agg_first = nn(adj, inputs).astype(BF16)
    pre = nn(agg_first, w_first)
    hidden = (maskf * jax.nn.silu(pre)).astype(BF16)
    agg_second = nn(adj, hidden).astype(BF16)
    output = (maskf * nn(agg_second, w_second)).astype(BF16)
    dout = cotangent[0] * mask

    def summed(a, b):
        part = lax.dot_general(a, b, (((0,), (0,)), ((), ())), preferred_element_type=F32)
        return lax.psum_scatter(part, "grp", scatter_dimension=0, tiled=True)

    grad_second = summed(dout, agg_second)
    dagg = nt(dout, w_second).astype(BF16)
    back = lax.dot_general(adj, dagg, (((0,), (0,)), ((), ())), preferred_element_type=F32)
    sig = jax.nn.sigmoid(pre)
    dpre = (maskf * back * sig * (1.0 + pre * (1.0 - sig))).astype(BF16)
    grad_first = summed(dpre, agg_first)
    return (output.reshape(1, rows, width), grad_first, grad_second)


def solution(mesh):
    n = mesh.shape["grp"]

    def body(*args):
        rows = args[4].shape[1]
        small = n & (n - 1) == 0 and n > PLANE and rows == LANES and n * rows <= 4096
        return whole_body(n, *args) if small else split_body(*args)

    in_specs = (
        P(("parts", "grp"), None, None),
        P(("parts", "grp")),
        P(("parts", "grp"), None),
        P(("parts", "grp"), None),
        P(("parts", "grp"), None, None),
        P(("parts", "grp"), None, None),
        P(),
        P(),
    )
    out_specs = (
        P(("parts", "grp"), None, None),
        P(("parts", "grp"), None),
        P(("parts", "grp"), None),
    )
    return jax.shard_map(body, mesh=mesh, in_specs=in_specs, out_specs=out_specs, check_vma=False)
```

```python
import functools

import jax
import jax.numpy as jnp
from jax import lax
from jax.experimental import pallas as pl
from jax.experimental.pallas import tpu as pltpu
from jax.sharding import PartitionSpec as P

F32 = jnp.float32
BF16 = jnp.bfloat16
VMEM = pl.BlockSpec(memory_space=pltpu.VMEM)
SMEM = pl.BlockSpec(memory_space=pltpu.SMEM)
PLANE = 4
LIMIT = 24 * 2**20
SMALL = 8 * 2**20
LANES = 128
META = 16


def nn(a, b):
    return jnp.dot(a, b, preferred_element_type=F32)


def nt(a, b):
    return lax.dot_general(a, b, (((1,), (1,)), ((), ())), preferred_element_type=F32)


def pack_kernel(counts, owner, local, features, adjacency, piece):
    own, slots, width = features.shape
    rows = adjacency.shape[1]
    held = own * slots
    slot = lax.broadcasted_iota(jnp.int32, (slots, LANES), 0)
    for i in range(own):
        live = slot < counts[i]
        for b in range(width // LANES):
            block = features[i, :, b * LANES : (b + 1) * LANES]
            at = b * held + i * slots
            piece[at : at + slots, :] = jnp.where(live, block, jnp.zeros_like(block))
    at = held * (width // LANES)
    piece[at : at + rows, :] = adjacency[0]
    at += rows
    line = lax.broadcasted_iota(jnp.int32, (META, LANES), 0)
    pick = lax.broadcasted_iota(jnp.int32, (META, LANES), 1) // slots
    meta = jnp.zeros((META, LANES), jnp.int32)
    for k in range(owner.shape[1]):
        wanted = owner[0, k] * own + local[0, k]
        meta = jnp.where((line == 0) & (pick == k), wanted, meta)
    for i in range(own):
        meta = jnp.where(line == 1 + i, counts[i], meta)
    piece[at : at + META, :] = meta.astype(F32).astype(BF16)


def columns_kernel(n, me, cotangent, w_second, near, across, turned, back):
    each = near.shape[0] // n
    cot = cotangent[0]
    turned[...] = cot.astype(F32).T.astype(BF16)
    back[...] = nt(w_second[...], cot).astype(BF16)
    for h, out in enumerate((near, across)):
        for i in range(out.shape[0] // (2 * each)):
            to = PLANE * (i // 2) + 2 * h + i % 2
            span = pl.ds(pl.multiple_of((me[0] ^ to) * each, each), each)
            at = i * 2 * each
            out[at : at + each, :] = turned[span, :]
            out[at + each : at + 2 * each, :] = back[span, :]


def regroup_kernel(parts, *refs):
    pieces, near, across = refs[:parts], refs[parts], refs[parts + 1]
    stack, *sent = refs[parts + 2 :]
    rows = pieces[0].shape[0]
    for i, ref in enumerate(pieces):
        stack[i * rows : (i + 1) * rows, :] = ref[...]
    half = sent[0].shape[0] // 2
    for s, out in enumerate(sent, 1):
        out[:half, :] = near[s * half : (s + 1) * half, :]
        out[half:, :] = across[s * half : (s + 1) * half, :]


def pair_kernel(parts, across, near, other, *refs):
    sent, out = refs[: parts - 1], refs[parts - 1]
    deep = across.shape[0]
    out[:deep, :] = across[...]
    half = near.shape[0] // parts
    rows = half // 2
    for s in range(parts):
        for h in range(2):
            if s:
                block = sent[s - 1][h * half + rows : (h + 1) * half, :]
            else:
                block = (near, other)[h][rows:half, :]
            at = deep + (2 * s + h) * rows
            out[at : at + rows, :] = block


def lay_out(pack, q, parts, held, rows, width, feat, adj, meta):
    at = 0
    for p in range(q * parts, (q + 1) * parts):
        for b in range(width // LANES):
            feat[p * held : (p + 1) * held, b * LANES : (b + 1) * LANES] = pack[at : at + held, :]
            at += held
        adj[p] = pack[at : at + rows, :]
        at += rows
        meta[p] = pack[at : at + META, :]
        at += META


def spread_of(n, place, held, slots, adj, picks):
    parts = n // PLANE
    line = lax.broadcasted_iota(jnp.int32, (held, LANES), 0)
    lane = lax.broadcasted_iota(jnp.int32, (1, LANES), 1) % slots
    owners = [place ^ (PLANE * (p % parts) + p // parts) for p in range(n)]
    code = jnp.concatenate([line + owner * held for owner in owners], axis=0)
    chosen = jnp.where(code == picks * slots + lane, 1.0, 0.0).astype(BF16)
    return nt(adj, chosen).astype(BF16)


def early_kernel(n, own, slots, me, stack, beside, w_first, feat, lifted, spread, adj, meta, w_piece):
    parts = n // PLANE
    width = w_first.shape[0]
    held = own * slots
    rows = adj.shape[1]
    place = me[0]
    lay_out(stack, 0, parts, held, rows, width, feat, adj, meta)
    lay_out(beside, 1, parts, held, rows, width, feat, adj, meta)
    lifted[...] = nn(feat[...], w_first[...]).astype(BF16)
    for p in range(n // 2):
        picks = meta[p, 0:1, :].astype(F32).astype(jnp.int32)
        spread[p * rows : (p + 1) * rows, :] = spread_of(n, place, held, slots, adj[p], picks)
    each = w_piece.shape[0]
    wide = max(each, LANES)
    per = wide // each
    start = pl.multiple_of((place // per) * wide, wide)
    block = w_first[:, pl.ds(start, wide)].astype(F32).T
    part = block[:each]
    for q in range(1, per):
        part = jnp.where(place % per == q, block[q * each : (q + 1) * each], part)
    w_piece[...] = part.astype(BF16)


def step_kernel(n, own, slots, me, *refs):
    parts = n // PLANE
    across, pair, near, other, *sent = refs[: 3 + parts]
    early_feat, early_lifted, early_spread, early_adj, early_meta, w_piece = refs[3 + parts : 9 + parts]
    w_first, w_second, output, grad_first, grad_second = refs[9 + parts : 14 + parts]
    hidden, spread, feat, adj, meta, dout, dpre, lifted = refs[14 + parts :]
    width = w_first.shape[0]
    held = own * slots
    rows = adj.shape[1]
    place = me[0]
    deep = across.shape[0]
    first = n // 2

    feat[: first * held, :] = early_feat[...]
    lifted[: first * held, :] = early_lifted[...]
    spread[: first * rows, :] = early_spread[...]
    adj[:first] = early_adj[...]
    meta[:first] = early_meta[...]
    lay_out(across, 2, parts, held, rows, width, feat, adj, meta)
    lay_out(pair, 3, parts, held, rows, width, feat, adj, meta)
    metas = [meta[p].astype(F32) for p in range(n)]
    picks = jnp.concatenate([m[0:1] for m in metas], axis=0).astype(jnp.int32)
    lane = lax.broadcasted_iota(jnp.int32, (n, LANES), 1) % slots
    count = jnp.zeros((n, LANES), jnp.int32)
    for p in range(n):
        for i in range(own):
            cluster = (place ^ (PLANE * (p % parts) + p // parts)) * own + i
            count = jnp.where(picks == cluster, metas[p][1 + i : 2 + i].astype(jnp.int32), count)
    masks = (lane < count).astype(F32)

    late = slice(first * held, n * held)
    lifted[late, :] = nn(feat[late, :], w_first[...]).astype(BF16)
    for p in range(first, n):
        span = slice(p * rows, (p + 1) * rows)
        spread[span, :] = spread_of(n, place, held, slots, adj[p], picks[p : p + 1])
    lifted_piece = nt(w_piece[...], feat[...]).astype(BF16)
    step = min(width, 2 * LANES)
    for c in range(0, width, step):
        half = 0.5 * nn(spread[...], lifted[:, c : c + step])
        hidden[:, c : c + step] = (half + half * jnp.tanh(half)).astype(BF16)
    pre_piece = nt(lifted_piece, spread[...])
    live = jnp.broadcast_to(masks[0:1], (rows, LANES)).T[:, :1]
    agg = nn(adj[0], (hidden[:rows, :].astype(F32) * live).astype(BF16)).astype(BF16)
    output[0] = (nn(agg, w_second[...]) * live).astype(BF16)

    each = grad_first.shape[0]
    half = near.shape[0] // parts
    for p in range(n):
        mask = masks[p : p + 1]
        span = slice(p * rows, (p + 1) * rows)
        s, h, b = p % parts, p // parts // 2, p // parts % 2
        if b:
            at = deep + (2 * s + h) * 2 * each
            source = pair[at : at + 2 * each, :]
        elif s:
            source = sent[s - 1][h * half : h * half + 2 * each, :]
        else:
            source = (near, other)[h][: 2 * each, :]
        back = nn((source.astype(F32) * mask).astype(BF16), adj[p]) * mask
        dout[:, span] = back[:each].astype(BF16)
        pre = pre_piece[:, span]
        sig = 0.5 + 0.5 * jnp.tanh(0.5 * pre)
        dpre[:, span] = (back[each:] * sig * (1.0 + pre * (1.0 - sig))).astype(BF16)
    grad_second[...] = nn(dout[...], hidden[...])
    moved = nn(dpre[...], spread[...])
    grad_first[...] = nn(moved.astype(BF16), feat[...])


def whole_body(n, features, counts, pick_owner, pick_local, adjacency, cotangent, w_first, w_second):
    own, slots, width = features.shape
    rows = adjacency.shape[1]
    held = own * slots
    each = width // n
    total_rows = n * held
    piece_rows = held * (width // LANES) + rows + META
    limit = pltpu.CompilerParams(vmem_limit_bytes=LIMIT)
    small = pltpu.CompilerParams(vmem_limit_bytes=SMALL)
    me = lax.axis_index("grp").reshape(1).astype(jnp.int32)

    def swap(x, s):
        return lax.ppermute(x, "grp", [(i, i ^ s) for i in range(n)])

    piece = pl.pallas_call(
        pack_kernel,
        out_shape=jax.ShapeDtypeStruct((piece_rows, LANES), BF16),
        in_specs=[SMEM] * 3 + [VMEM] * 2,
        out_specs=VMEM,
        compiler_params=small,
        cost_estimate=pl.CostEstimate(flops=10**10, bytes_accessed=2**18, transcendentals=0),
    )(counts, pick_owner, pick_local, features, adjacency)
    cotangent, _ = lax.optimization_barrier((cotangent, piece))
    near, other = pl.pallas_call(
        functools.partial(columns_kernel, n),
        out_shape=(jax.ShapeDtypeStruct((n * each, rows), BF16),) * 2,
        in_specs=[SMEM, VMEM, VMEM],
        out_specs=(VMEM,) * 2,
        scratch_shapes=[pltpu.VMEM((width, rows), BF16)] * 2,
        compiler_params=small,
    )(me, cotangent, w_second)
    far = range(PLANE, n, PLANE)
    parts = n // PLANE
    along = [swap(piece, s) for s in far]
    other = swap(other, 2)
    stack, *sent = pl.pallas_call(
        functools.partial(regroup_kernel, parts),
        out_shape=(jax.ShapeDtypeStruct((parts * piece_rows, LANES), BF16),)
        + (jax.ShapeDtypeStruct((PLANE * 2 * each, rows), BF16),) * len(far),
        in_specs=[VMEM] * (parts + 2),
        out_specs=(VMEM,) * parts,
        compiler_params=small,
    )(piece, *along, near, other)
    sent = [swap(x, s) for x, s in zip(sent, far)]
    beside = swap(stack, 1)
    across = swap(stack, 2)
    across, beside = lax.optimization_barrier((across, beside))
    pair = pl.pallas_call(
        functools.partial(pair_kernel, parts),
        out_shape=jax.ShapeDtypeStruct((parts * piece_rows + n * each, LANES), BF16),
        in_specs=[VMEM] * (parts + 2),
        out_specs=VMEM,
        compiler_params=small,
    )(across, near, other, *sent)
    pair = swap(pair, 1)
    early = pl.pallas_call(
        functools.partial(early_kernel, n, own, slots),
        out_shape=(
            jax.ShapeDtypeStruct((total_rows // 2, width), BF16),
            jax.ShapeDtypeStruct((total_rows // 2, width), BF16),
            jax.ShapeDtypeStruct((n // 2 * rows, total_rows), BF16),
            jax.ShapeDtypeStruct((n // 2, rows, rows), BF16),
            jax.ShapeDtypeStruct((n // 2, META, LANES), BF16),
            jax.ShapeDtypeStruct((each, width), BF16),
        ),
        in_specs=[SMEM] + [VMEM] * 3,
        out_specs=(VMEM,) * 6,
        compiler_params=limit,
        cost_estimate=pl.CostEstimate(flops=2 * 10**9, bytes_accessed=2**20, transcendentals=0),
    )(me, stack, beside, w_first)
    return pl.pallas_call(
        functools.partial(step_kernel, n, own, slots),
        out_shape=(
            jax.ShapeDtypeStruct((1, rows, width), BF16),
            jax.ShapeDtypeStruct((each, width), F32),
            jax.ShapeDtypeStruct((each, width), F32),
        ),
        in_specs=[SMEM] + [VMEM] * (parts + 11),
        out_specs=(VMEM,) * 3,
        scratch_shapes=[
            pltpu.VMEM((n * rows, width), BF16),
            pltpu.VMEM((n * rows, total_rows), BF16),
            pltpu.VMEM((total_rows, width), BF16),
            pltpu.VMEM((n, rows, rows), BF16),
            pltpu.VMEM((n, META, LANES), BF16),
            pltpu.VMEM((each, n * rows), BF16),
            pltpu.VMEM((each, n * rows), BF16),
            pltpu.VMEM((total_rows, width), BF16),
        ],
        compiler_params=limit,
    )(me, across, pair, near, other, *sent, *early, w_first, w_second)


def split_body(features, counts, pick_owner, pick_local, adjacency, cotangent, w_first, w_second):
    owners = pick_owner[0]
    picks = pick_local[0]
    width = w_first.shape[0]
    slots = features.shape[1]
    count_picks = owners.shape[0]
    wanted = owners * features.shape[0] + picks
    feat_piece = lax.all_gather(features, "grp", axis=0, tiled=True)
    count_piece = lax.all_gather(counts, "grp", axis=0, tiled=True)
    live = jnp.take(count_piece, wanted, axis=0)
    rows = count_picks * slots
    inputs = jnp.take(feat_piece, wanted, axis=0).reshape(rows, width)
    mask = (jnp.arange(slots)[None, :] < live[:, None]).reshape(rows, 1).astype(BF16)
    inputs = inputs * mask
    maskf = mask.astype(F32)
    adj = adjacency[0]
    agg_first = nn(adj, inputs).astype(BF16)
    pre = nn(agg_first, w_first)
    hidden = (maskf * jax.nn.silu(pre)).astype(BF16)
    agg_second = nn(adj, hidden).astype(BF16)
    output = (maskf * nn(agg_second, w_second)).astype(BF16)
    dout = cotangent[0] * mask

    def summed(a, b):
        part = lax.dot_general(a, b, (((0,), (0,)), ((), ())), preferred_element_type=F32)
        return lax.psum_scatter(part, "grp", scatter_dimension=0, tiled=True)

    grad_second = summed(dout, agg_second)
    dagg = nt(dout, w_second).astype(BF16)
    back = lax.dot_general(adj, dagg, (((0,), (0,)), ((), ())), preferred_element_type=F32)
    sig = jax.nn.sigmoid(pre)
    dpre = (maskf * back * sig * (1.0 + pre * (1.0 - sig))).astype(BF16)
    grad_first = summed(dpre, agg_first)
    return (output.reshape(1, rows, width), grad_first, grad_second)


def solution(mesh):
    n = mesh.shape["grp"]

    def body(*args):
        rows = args[4].shape[1]
        small = n & (n - 1) == 0 and n > PLANE and rows == LANES and n * rows <= 4096
        return whole_body(n, *args) if small else split_body(*args)

    in_specs = (
        P(("parts", "grp"), None, None),
        P(("parts", "grp")),
        P(("parts", "grp"), None),
        P(("parts", "grp"), None),
        P(("parts", "grp"), None, None),
        P(("parts", "grp"), None, None),
        P(),
        P(),
    )
    out_specs = (
        P(("parts", "grp"), None, None),
        P(("parts", "grp"), None),
        P(("parts", "grp"), None),
    )
    return jax.shard_map(body, mesh=mesh, in_specs=in_specs, out_specs=out_specs, check_vma=False)
```

```python
import functools

import jax
import jax.numpy as jnp
from jax import lax
from jax.experimental import pallas as pl
from jax.experimental.pallas import tpu as pltpu
from jax.sharding import PartitionSpec as P

F32 = jnp.float32
BF16 = jnp.bfloat16
VMEM = pl.BlockSpec(memory_space=pltpu.VMEM)
HBM = pl.BlockSpec(memory_space=pltpu.HBM)
LANES = 128
META = 16
CHUNKS = 4
LIMIT = 24 * 2**20
SMALL = 8 * 2**20
Z2, Z1, Y, CORE = 8, 4, 2, 1
GROUP = 16
FAR = (Z2 | Z1, Z2, Z1)
HALF_A = ((0, Z2, Z1, Z1 | Z2), (Y, Y | Z2, Y | Z1, Y | Z1 | Z2))
HALF_B = ((0, Z2, Y, Y | Z2), (Z1, Z1 | Z2, Z1 | Y, Z1 | Y | Z2))


def nn(a, b):
    return jnp.dot(a, b, preferred_element_type=F32)


def nt(a, b):
    return lax.dot_general(a, b, (((1,), (1,)), ((), ())), preferred_element_type=F32)


def prepare_kernel(counts, owner, local, features, adjacency, cotangent, w_second, *refs):
    piece, near, across, count, own_by, own_at, feat, adj, cot, second, turned, back, sems = refs
    own, slots, width = features.shape
    rows = adjacency.shape[1]
    each = width // GROUP
    place = lax.axis_index("grp")
    moves = [(features, feat), (adjacency, adj), (counts, count), (owner, own_by), (local, own_at)]
    moves.append((cotangent, cot))
    some = width // CHUNKS
    for c in range(CHUNKS):
        span = slice(c * some, (c + 1) * some)
        moves.append((w_second.at[span], second.at[span]))
    copies = [pltpu.make_async_copy(a, b, sems.at[i]) for i, (a, b) in enumerate(moves)]
    for copy in copies:
        copy.start()

    held = own * slots
    slot = lax.broadcasted_iota(jnp.int32, (slots, LANES), 0)
    line = lax.broadcasted_iota(jnp.int32, (META, LANES), 0)
    pick = lax.broadcasted_iota(jnp.int32, (META, LANES), 1) // slots
    meta = jnp.zeros((META, LANES), jnp.int32)
    for copy in copies[:5]:
        copy.wait()
    for i in range(own):
        live = slot < count[i]
        for b in range(width // LANES):
            block = feat[i, :, b * LANES : (b + 1) * LANES]
            at = b * held + i * slots
            piece[at : at + slots, :] = jnp.where(live, block, jnp.zeros_like(block))
        meta = jnp.where(line == 1 + i, count[i], meta)
    for k in range(owner.shape[1]):
        meta = jnp.where((line == 0) & (pick == k), own_by[0, k] * own + own_at[0, k], meta)
    at = held * (width // LANES)
    piece[at : at + rows, :] = adj[0]
    piece[at + rows : at + rows + META, :] = meta.astype(F32).astype(BF16)

    copies[5].wait()
    turned[...] = cot[0].astype(F32).T.astype(BF16)
    for c in range(CHUNKS):
        copies[6 + c].wait()
        span = slice(c * some, (c + 1) * some)
        back[span, :] = nt(second[span, :], cot[0]).astype(BF16)
    for h, out in enumerate((near, across)):
        for i in range(out.shape[0] // (2 * each)):
            to = 4 * (i // 2) + 2 * h + i % 2
            span = pl.ds(pl.multiple_of((place ^ to) * each, each), each)
            at = i * 2 * each
            out[at : at + each, :] = turned[span, :]
            out[at + each : at + 2 * each, :] = back[span, :]


def stack(out, at, *blocks):
    for block in blocks:
        out[at : at + block.shape[0], :] = block[...]
        at += block.shape[0]
    return at


def split_kernel(piece, came, near, across, half_a, half_b, *sent):
    cut = half_a.shape[0] // 2
    stack(half_a, 0, piece.at[:cut], came.at[:cut])
    stack(half_b, 0, piece.at[cut:], came.at[cut:])
    size = sent[0].shape[0] // 2
    for slot, out in zip(FAR + (0,), sent):
        span = slice(slot // 4 * size, (slot // 4 + 1) * size)
        stack(out, 0, near.at[span], across.at[span])


def join_kernel(a, came_a, b, came_b, out_a, out_b):
    stack(out_a, 0, a, came_a)
    stack(out_b, 0, b, came_b)


def pair_kernel(a, far_a, b, far_b, *refs):
    *sent, out = refs
    at = stack(out, 0, a, far_a, b, far_b)
    size = sent[0].shape[0] // 2
    rows = size // 2
    for s in range(GROUP // 4):
        for h in range(2):
            block = sent[(FAR + (0,)).index(4 * s)]
            at = stack(out, at, block.at[h * size + rows : (h + 1) * size])


def place_of(slot):
    return slot // 2 + GROUP // 2 * (slot % 2)


def lay_out(arrays, held, cut, feat, adj, meta):
    rows = adj.shape[1]
    for ref, at, slots in arrays[:2]:
        for slot in slots:
            p = place_of(slot)
            for b in range(cut // held):
                feat[p * held : (p + 1) * held, b * LANES : (b + 1) * LANES] = ref[at : at + held, :]
                at += held
    for ref, at, slots in arrays[2:]:
        for slot in slots:
            p = place_of(slot)
            for b in range(cut // held, feat.shape[1] // LANES):
                feat[p * held : (p + 1) * held, b * LANES : (b + 1) * LANES] = ref[at : at + held, :]
                at += held
            adj[p] = ref[at : at + rows, :]
            at += rows
            meta[p] = ref[at : at + META, :]
            at += META


def spread_of(place, held, slots, adj, picks):
    line = lax.broadcasted_iota(jnp.int32, (held, LANES), 0)
    lane = lax.broadcasted_iota(jnp.int32, (1, LANES), 1) % slots
    owners = [None] * GROUP
    for slot in range(GROUP):
        owners[place_of(slot)] = place ^ slot
    code = jnp.concatenate([line + owner * held for owner in owners], axis=0)
    chosen = jnp.where(code == picks * slots + lane, 1.0, 0.0).astype(BF16)
    return nt(adj, chosen).astype(BF16)


def early_kernel(own, slots, cut, a, far_a, b, far_b, w_first, feat, lifted, spread, adj, meta, w_piece):
    held = own * slots
    rows = adj.shape[1]
    place = lax.axis_index("grp")
    arrays = list(zip((a, far_a, b, far_b), HALF_A + HALF_B))
    lay_out([(ref, 0, at) for ref, at in arrays], held, cut, feat, adj, meta)
    lifted[...] = nn(feat[...], w_first[...]).astype(BF16)
    for p in range(GROUP // 2):
        picks = meta[p, 0:1, :].astype(F32).astype(jnp.int32)
        spread[p * rows : (p + 1) * rows, :] = spread_of(place, held, slots, adj[p], picks)
    each = w_piece.shape[0]
    wide = max(each, LANES)
    per = wide // each
    start = pl.multiple_of((place // per) * wide, wide)
    block = w_first[:, pl.ds(start, wide)].astype(F32).T
    part = block[:each]
    for q in range(1, per):
        part = jnp.where(place % per == q, block[q * each : (q + 1) * each], part)
    w_piece[...] = part.astype(BF16)


def step_kernel(own, slots, cut, rest, pair, *refs):
    sent, refs = refs[: len(FAR) + 1], refs[len(FAR) + 1 :]
    early_feat, early_lifted, early_spread, early_adj, early_meta, w_piece = refs[:6]
    w_first, w_second, output, grad_first, grad_second = refs[6:11]
    hidden, spread, feat, adj, meta, dout, dpre, lifted = refs[11:]
    width = w_first.shape[0]
    held = own * slots
    rows = adj.shape[1]
    place = lax.axis_index("grp")
    first = GROUP // 2

    feat[: first * held, :] = early_feat[...]
    lifted[: first * held, :] = early_lifted[...]
    spread[: first * rows, :] = early_spread[...]
    adj[:first] = early_adj[...]
    meta[:first] = early_meta[...]
    arrays, deep = [], 0
    for size, halves in ((cut, HALF_A), (rest, HALF_B)):
        for group in halves:
            arrays.append((pair, deep, [slot | CORE for slot in group]))
            deep += size * len(group)
    lay_out(arrays, held, cut, feat, adj, meta)
    metas = [meta[p].astype(F32) for p in range(GROUP)]
    picks = jnp.concatenate([m[0:1] for m in metas], axis=0).astype(jnp.int32)
    lane = lax.broadcasted_iota(jnp.int32, (GROUP, LANES), 1) % slots
    count = jnp.zeros((GROUP, LANES), jnp.int32)
    for slot in range(GROUP):
        for i in range(own):
            held_by = metas[place_of(slot)][1 + i : 2 + i].astype(jnp.int32)
            count = jnp.where(picks == (place ^ slot) * own + i, held_by, count)
    masks = (lane < count).astype(F32)

    late = slice(first * held, GROUP * held)
    lifted[late, :] = nn(feat[late, :], w_first[...]).astype(BF16)
    lifted_piece = nt(w_piece[...], feat[...]).astype(BF16)
    for p in range(first, GROUP):
        span = slice(p * rows, (p + 1) * rows)
        spread[span, :] = spread_of(place, held, slots, adj[p], picks[p : p + 1])
    step = min(width, 2 * LANES)
    for c in range(0, width, step):
        half = 0.5 * nn(spread[...], lifted[:, c : c + step])
        hidden[:, c : c + step] = (half + half * jnp.tanh(half)).astype(BF16)
    pre_piece = nt(lifted_piece, spread[...])
    live = jnp.broadcast_to(masks[0:1], (rows, LANES)).T[:, :1]
    agg = nn(adj[0], (hidden[:rows, :].astype(F32) * live).astype(BF16)).astype(BF16)
    output[0] = (nn(agg, w_second[...]) * live).astype(BF16)

    each = grad_first.shape[0]
    size = sent[0].shape[0] // 2
    for slot in range(GROUP):
        p = place_of(slot)
        mask = masks[p : p + 1]
        span = slice(p * rows, (p + 1) * rows)
        s, h = slot // 4, slot // 2 % 2
        if slot % 2:
            at = deep + (2 * s + h) * 2 * each
            source = pair[at : at + 2 * each, :]
        else:
            source = sent[(FAR + (0,)).index(4 * s)][h * size : h * size + 2 * each, :]
        back = nn((source.astype(F32) * mask).astype(BF16), adj[p]) * mask
        dout[:, span] = back[:each].astype(BF16)
        pre = pre_piece[:, span]
        sig = 0.5 + 0.5 * jnp.tanh(0.5 * pre)
        dpre[:, span] = (back[each:] * sig * (1.0 + pre * (1.0 - sig))).astype(BF16)
    grad_second[...] = nn(dout[...], hidden[...])
    moved = nn(dpre[...], spread[...])
    grad_first[...] = nn(moved.astype(BF16), feat[...])


def call(kernel, ins, outs, scratch=(), limit=SMALL, stay=False):
    if stay:
        ins = [pltpu.with_memory_space_constraint(x, pltpu.HBM) for x in ins]
    return pl.pallas_call(
        kernel,
        out_shape=tuple(jax.ShapeDtypeStruct(*out) for out in outs),
        in_specs=[HBM if stay else VMEM] * len(ins),
        out_specs=(VMEM,) * len(outs),
        scratch_shapes=list(scratch),
        compiler_params=pltpu.CompilerParams(vmem_limit_bytes=limit),
    )(*ins)


def whole_body(features, counts, pick_owner, pick_local, adjacency, cotangent, w_first, w_second):
    own, slots, width = features.shape
    rows = adjacency.shape[1]
    held = own * slots
    each = width // GROUP
    total = GROUP * held
    cut = held * (width // LANES * 3 // 4)
    rest = held * (width // LANES) + rows + META - cut
    half = GROUP // 2

    def swap(x, slot):
        return lax.ppermute(x, "grp", [(i, i ^ slot) for i in range(GROUP)])

    piece, near, across = call(
        prepare_kernel,
        (counts, pick_owner, pick_local, features, adjacency, cotangent, w_second),
        [((cut + rest, LANES), BF16)] + [((GROUP * each, rows), BF16)] * 2,
        [pltpu.SMEM(x.shape, jnp.int32) for x in (counts, pick_owner, pick_local)]
        + [pltpu.VMEM(x.shape, BF16) for x in (features, adjacency, cotangent, w_second)]
        + [pltpu.VMEM((width, rows), BF16)] * 2
        + [pltpu.SemaphoreType.DMA((6 + CHUNKS,))],
        stay=True,
    )
    came = swap(piece, Z2)
    across = swap(across, Y)
    a, b, *sent = call(
        split_kernel,
        (piece, came, near, across),
        [((2 * cut, LANES), BF16), ((2 * rest, LANES), BF16)] + [((8 * each, rows), BF16)] * (len(FAR) + 1),
    )
    sent = [swap(x, slot) for x, slot in zip(sent, FAR)] + sent[-1:]
    came_a, came_b = swap(a, Z1), swap(b, Y)
    came_a, came_b, sent[0] = lax.optimization_barrier((came_a, came_b, sent[0]))
    a, b = call(
        join_kernel, (a, came_a, b, came_b), [((4 * cut, LANES), BF16), ((4 * rest, LANES), BF16)]
    )
    far_a, far_b = swap(a, Y), swap(b, Z1)
    (pair,) = call(
        pair_kernel,
        (a, far_a, b, far_b, *sent),
        [((half * (cut + rest) + half * 2 * each, LANES), BF16)],
    )
    pair = swap(pair, CORE)
    early = call(
        functools.partial(early_kernel, own, slots, cut),
        (a, far_a, b, far_b, w_first),
        [
            ((total // 2, width), BF16),
            ((total // 2, width), BF16),
            ((half * rows, total), BF16),
            ((half, rows, rows), BF16),
            ((half, META, LANES), BF16),
            ((each, width), BF16),
        ],
        limit=LIMIT,
    )
    return call(
        functools.partial(step_kernel, own, slots, cut, rest),
        (pair, *sent, *early, w_first, w_second),
        [((1, rows, width), BF16), ((each, width), F32), ((each, width), F32)],
        [
            pltpu.VMEM((GROUP * rows, width), BF16),
            pltpu.VMEM((GROUP * rows, total), BF16),
            pltpu.VMEM((total, width), BF16),
            pltpu.VMEM((GROUP, rows, rows), BF16),
            pltpu.VMEM((GROUP, META, LANES), BF16),
            pltpu.VMEM((each, GROUP * rows), BF16),
            pltpu.VMEM((each, GROUP * rows), BF16),
            pltpu.VMEM((total, width), BF16),
        ],
        LIMIT,
    )


def split_body(features, counts, pick_owner, pick_local, adjacency, cotangent, w_first, w_second):
    owners = pick_owner[0]
    picks = pick_local[0]
    width = w_first.shape[0]
    slots = features.shape[1]
    count_picks = owners.shape[0]
    wanted = owners * features.shape[0] + picks
    feat_piece = lax.all_gather(features, "grp", axis=0, tiled=True)
    count_piece = lax.all_gather(counts, "grp", axis=0, tiled=True)
    live = jnp.take(count_piece, wanted, axis=0)
    rows = count_picks * slots
    inputs = jnp.take(feat_piece, wanted, axis=0).reshape(rows, width)
    mask = (jnp.arange(slots)[None, :] < live[:, None]).reshape(rows, 1).astype(BF16)
    inputs = inputs * mask
    maskf = mask.astype(F32)
    adj = adjacency[0]
    agg_first = nn(adj, inputs).astype(BF16)
    pre = nn(agg_first, w_first)
    hidden = (maskf * jax.nn.silu(pre)).astype(BF16)
    agg_second = nn(adj, hidden).astype(BF16)
    output = (maskf * nn(agg_second, w_second)).astype(BF16)
    dout = cotangent[0] * mask

    def summed(a, b):
        part = lax.dot_general(a, b, (((0,), (0,)), ((), ())), preferred_element_type=F32)
        return lax.psum_scatter(part, "grp", scatter_dimension=0, tiled=True)

    grad_second = summed(dout, agg_second)
    dagg = nt(dout, w_second).astype(BF16)
    back = lax.dot_general(adj, dagg, (((0,), (0,)), ((), ())), preferred_element_type=F32)
    sig = jax.nn.sigmoid(pre)
    dpre = (maskf * back * sig * (1.0 + pre * (1.0 - sig))).astype(BF16)
    grad_first = summed(dpre, agg_first)
    return (output.reshape(1, rows, width), grad_first, grad_second)


def solution(mesh):
    n = mesh.shape["grp"]

    def body(*args):
        rows = args[4].shape[1]
        return whole_body(*args) if n == GROUP and rows == LANES else split_body(*args)

    in_specs = (
        P(("parts", "grp"), None, None),
        P(("parts", "grp")),
        P(("parts", "grp"), None),
        P(("parts", "grp"), None),
        P(("parts", "grp"), None, None),
        P(("parts", "grp"), None, None),
        P(),
        P(),
    )
    out_specs = (
        P(("parts", "grp"), None, None),
        P(("parts", "grp"), None),
        P(("parts", "grp"), None),
    )
    return jax.shard_map(body, mesh=mesh, in_specs=in_specs, out_specs=out_specs, check_vma=False)
```

```python
import functools

import jax
import jax.numpy as jnp
from jax import lax
from jax.experimental import pallas as pl
from jax.experimental.pallas import tpu as pltpu
from jax.sharding import PartitionSpec as P

F32 = jnp.float32
BF16 = jnp.bfloat16
VMEM = pl.BlockSpec(memory_space=pltpu.VMEM)
HBM = pl.BlockSpec(memory_space=pltpu.HBM)
LANES = 128
META = 16
CHUNKS = 4
LIMIT = 24 * 2**20
SMALL = 8 * 2**20
Z2, Z1, Y, CORE = 8, 4, 2, 1
GROUP = 16
FAR = (Z2 | Z1, Z2, 0)
HALF_A = ((0, Z2, Z1, Z1 | Z2), (Y, Y | Z2, Y | Z1, Y | Z1 | Z2))
HALF_B = ((0, Z2, Y, Y | Z2), (Z1, Z1 | Z2, Z1 | Y, Z1 | Y | Z2))


def nn(a, b):
    return jnp.dot(a, b, preferred_element_type=F32)


def nt(a, b):
    return lax.dot_general(a, b, (((1,), (1,)), ((), ())), preferred_element_type=F32)


def prepare_kernel(counts, owner, local, features, adjacency, cotangent, w_second, *refs):
    piece, near, across, count, own_by, own_at, feat, adj, cot, second, turned, back, sems = refs
    own, slots, width = features.shape
    rows = adjacency.shape[1]
    each = width // GROUP
    place = lax.axis_index("grp")
    moves = [(features, feat), (adjacency, adj), (counts, count), (owner, own_by), (local, own_at)]
    moves.append((cotangent, cot))
    some = width // CHUNKS
    for c in range(CHUNKS):
        span = slice(c * some, (c + 1) * some)
        moves.append((w_second.at[span], second.at[span]))
    copies = [pltpu.make_async_copy(a, b, sems.at[i]) for i, (a, b) in enumerate(moves)]
    for copy in copies:
        copy.start()

    held = own * slots
    slot = lax.broadcasted_iota(jnp.int32, (slots, LANES), 0)
    line = lax.broadcasted_iota(jnp.int32, (META, LANES), 0)
    pick = lax.broadcasted_iota(jnp.int32, (META, LANES), 1) // slots
    meta = jnp.zeros((META, LANES), jnp.int32)
    for copy in copies[:5]:
        copy.wait()
    for i in range(own):
        live = slot < count[i]
        for b in range(width // LANES):
            block = feat[i, :, b * LANES : (b + 1) * LANES]
            at = b * held + i * slots
            piece[at : at + slots, :] = jnp.where(live, block, jnp.zeros_like(block))
        meta = jnp.where(line == 1 + i, count[i], meta)
    for k in range(owner.shape[1]):
        meta = jnp.where((line == 0) & (pick == k), own_by[0, k] * own + own_at[0, k], meta)
    at = held * (width // LANES)
    piece[at : at + rows, :] = adj[0]
    piece[at + rows : at + rows + META, :] = meta.astype(F32).astype(BF16)

    copies[5].wait()
    turned[...] = cot[0].astype(F32).T.astype(BF16)
    for c in range(CHUNKS):
        copies[6 + c].wait()
        span = slice(c * some, (c + 1) * some)
        back[span, :] = nt(second[span, :], cot[0]).astype(BF16)
    for h, out in enumerate((near, across)):
        for i in range(out.shape[0] // (2 * each)):
            to = 4 * (i // 2) + 2 * h + i % 2
            span = pl.ds(pl.multiple_of((place ^ to) * each, each), each)
            at = i * 2 * each
            out[at : at + each, :] = turned[span, :]
            out[at + each : at + 2 * each, :] = back[span, :]


def stack(out, at, *blocks):
    for block in blocks:
        out[at : at + block.shape[0], :] = block[...]
        at += block.shape[0]
    return at


def split_kernel(piece, came, near, across, beside, half_b, *sent):
    cut = beside.shape[0] - sent[0].shape[0]
    stack(half_b, 0, piece.at[cut // 2 :], came.at[cut // 2 :])
    at = stack(beside, 0, piece.at[: cut // 2], came.at[: cut // 2])
    size = sent[0].shape[0] // 2
    for slot, (out, at) in {Z1: (beside, at), **{slot: (out, 0) for slot, out in zip(FAR, sent)}}.items():
        span = slice(slot // 4 * size, (slot // 4 + 1) * size)
        stack(out, at, near.at[span], across.at[span])


def join_kernel(beside, came, half_b, came_b, out_a, out_b, both):
    cut = out_a.shape[0] // 2
    stack(out_a, 0, beside.at[:cut], came.at[:cut])
    stack(out_b, 0, half_b, came_b)
    stack(both, 0, out_a, out_b)


def columns_kernel(came, *refs):
    *sent, out = refs
    size = sent[0].shape[0]
    blocks = dict(zip(FAR, sent))
    blocks[Z1] = came.at[came.shape[0] - size :]
    rows = size // 4
    at = 0
    for slot in range(0, GROUP, 4):
        for h in range(2):
            at = stack(out, at, blocks[slot].at[(2 * h + 1) * rows : (2 * h + 2) * rows])


def pair_kernel(far_a, far_b, columns, out):
    stack(out, 0, far_a, far_b, columns)


def place_of(slot):
    return slot // 2 + GROUP // 2 * (slot % 2)


def lay_out(arrays, held, cut, feat, adj, meta):
    rows = adj.shape[1]
    for ref, at, slots in arrays[:2]:
        for slot in slots:
            p = place_of(slot)
            for b in range(cut // held):
                feat[p * held : (p + 1) * held, b * LANES : (b + 1) * LANES] = ref[at : at + held, :]
                at += held
    for ref, at, slots in arrays[2:]:
        for slot in slots:
            p = place_of(slot)
            for b in range(cut // held, feat.shape[1] // LANES):
                feat[p * held : (p + 1) * held, b * LANES : (b + 1) * LANES] = ref[at : at + held, :]
                at += held
            adj[p] = ref[at : at + rows, :]
            at += rows
            meta[p] = ref[at : at + META, :]
            at += META


def spread_of(place, held, slots, adj, picks):
    line = lax.broadcasted_iota(jnp.int32, (held, LANES), 0)
    lane = lax.broadcasted_iota(jnp.int32, (1, LANES), 1) % slots
    owners = [None] * GROUP
    for slot in range(GROUP):
        owners[place_of(slot)] = place ^ slot
    code = jnp.concatenate([line + owner * held for owner in owners], axis=0)
    chosen = jnp.where(code == picks * slots + lane, 1.0, 0.0).astype(BF16)
    return nt(adj, chosen).astype(BF16)


def early_kernel(own, slots, cut, a, far_a, b, far_b, w_first, feat, lifted, spread, adj, meta, w_piece):
    held = own * slots
    rows = adj.shape[1]
    place = lax.axis_index("grp")
    arrays = list(zip((a, far_a, b, far_b), HALF_A + HALF_B))
    lay_out([(ref, 0, at) for ref, at in arrays], held, cut, feat, adj, meta)
    lifted[...] = nn(feat[...], w_first[...]).astype(BF16)
    for p in range(GROUP // 2):
        picks = meta[p, 0:1, :].astype(F32).astype(jnp.int32)
        spread[p * rows : (p + 1) * rows, :] = spread_of(place, held, slots, adj[p], picks)
    each = w_piece.shape[0]
    wide = max(each, LANES)
    per = wide // each
    start = pl.multiple_of((place // per) * wide, wide)
    block = w_first[:, pl.ds(start, wide)].astype(F32).T
    part = block[:each]
    for q in range(1, per):
        part = jnp.where(place % per == q, block[q * each : (q + 1) * each], part)
    w_piece[...] = part.astype(BF16)


def step_kernel(own, slots, cut, rest, core, pair, came, *refs):
    sent, refs = dict(zip(FAR, refs)), refs[len(FAR) :]
    early_feat, early_lifted, early_spread, early_adj, early_meta, w_piece = refs[:6]
    w_first, w_second, output, grad_first, grad_second = refs[6:11]
    hidden, spread, feat, adj, meta, dout, dpre, lifted = refs[11:]
    width = w_first.shape[0]
    held = own * slots
    rows = adj.shape[1]
    place = lax.axis_index("grp")
    first = GROUP // 2

    feat[: first * held, :] = early_feat[...]
    lifted[: first * held, :] = early_lifted[...]
    spread[: first * rows, :] = early_spread[...]
    adj[:first] = early_adj[...]
    meta[:first] = early_meta[...]
    arrays = []
    for size, start, halves in ((cut, 0, HALF_A), (rest, 4 * cut, HALF_B)):
        for ref, group in zip((core, pair), halves):
            arrays.append((ref, start, [slot | CORE for slot in group]))
    deep = 4 * (cut + rest)
    lay_out(arrays, held, cut, feat, adj, meta)
    metas = [meta[p].astype(F32) for p in range(GROUP)]
    picks = jnp.concatenate([m[0:1] for m in metas], axis=0).astype(jnp.int32)
    lane = lax.broadcasted_iota(jnp.int32, (GROUP, LANES), 1) % slots
    count = jnp.zeros((GROUP, LANES), jnp.int32)
    for slot in range(GROUP):
        for i in range(own):
            held_by = metas[place_of(slot)][1 + i : 2 + i].astype(jnp.int32)
            count = jnp.where(picks == (place ^ slot) * own + i, held_by, count)
    masks = (lane < count).astype(F32)

    late = slice(first * held, GROUP * held)
    lifted[late, :] = nn(feat[late, :], w_first[...]).astype(BF16)
    lifted_piece = nt(w_piece[...], feat[...]).astype(BF16)
    for p in range(first, GROUP):
        span = slice(p * rows, (p + 1) * rows)
        spread[span, :] = spread_of(place, held, slots, adj[p], picks[p : p + 1])
    step = min(width, 2 * LANES)
    for c in range(0, width, step):
        half = 0.5 * nn(spread[...], lifted[:, c : c + step])
        hidden[:, c : c + step] = (half + half * jnp.tanh(half)).astype(BF16)
    pre_piece = nt(lifted_piece, spread[...])
    live = jnp.broadcast_to(masks[0:1], (rows, LANES)).T[:, :1]
    agg = nn(adj[0], (hidden[:rows, :].astype(F32) * live).astype(BF16)).astype(BF16)
    output[0] = (nn(agg, w_second[...]) * live).astype(BF16)

    each = grad_first.shape[0]
    size = sent[0].shape[0]
    sent[Z1] = came.at[came.shape[0] - size :]
    for slot in range(GROUP):
        p = place_of(slot)
        mask = masks[p : p + 1]
        span = slice(p * rows, (p + 1) * rows)
        s, h = slot // 4, slot // 2 % 2
        if slot % 2:
            at = deep + (2 * s + h) * 2 * each
            source = pair[at : at + 2 * each, :]
        else:
            source = sent[4 * s][h * size // 2 : h * size // 2 + 2 * each, :]
        back = nn((source.astype(F32) * mask).astype(BF16), adj[p]) * mask
        dout[:, span] = back[:each].astype(BF16)
        pre = pre_piece[:, span]
        sig = 0.5 + 0.5 * jnp.tanh(0.5 * pre)
        dpre[:, span] = (back[each:] * sig * (1.0 + pre * (1.0 - sig))).astype(BF16)
    grad_second[...] = nn(dout[...], hidden[...])
    moved = nn(dpre[...], spread[...])
    grad_first[...] = nn(moved.astype(BF16), feat[...])


def call(kernel, ins, outs, scratch=(), limit=SMALL, stay=False, flops=0):
    if stay:
        ins = [pltpu.with_memory_space_constraint(x, pltpu.HBM) for x in ins]
    return pl.pallas_call(
        kernel,
        out_shape=tuple(jax.ShapeDtypeStruct(*out) for out in outs),
        in_specs=[HBM if stay else VMEM] * len(ins),
        out_specs=(VMEM,) * len(outs),
        scratch_shapes=list(scratch),
        compiler_params=pltpu.CompilerParams(vmem_limit_bytes=limit),
        cost_estimate=pl.CostEstimate(flops=flops, bytes_accessed=0, transcendentals=0),
    )(*ins)


def whole_body(features, counts, pick_owner, pick_local, adjacency, cotangent, w_first, w_second):
    own, slots, width = features.shape
    rows = adjacency.shape[1]
    held = own * slots
    each = width // GROUP
    total = GROUP * held
    cut = held * (width // LANES * 3 // 4)
    rest = held * (width // LANES) + rows + META - cut
    half = GROUP // 2

    def swap(x, slot):
        return lax.ppermute(x, "grp", [(i, i ^ slot) for i in range(GROUP)])

    piece, near, across = call(
        prepare_kernel,
        (counts, pick_owner, pick_local, features, adjacency, cotangent, w_second),
        [((cut + rest, LANES), BF16)] + [((GROUP * each, rows), BF16)] * 2,
        [pltpu.SMEM(x.shape, jnp.int32) for x in (counts, pick_owner, pick_local)]
        + [pltpu.VMEM(x.shape, BF16) for x in (features, adjacency, cotangent, w_second)]
        + [pltpu.VMEM((width, rows), BF16)] * 2
        + [pltpu.SemaphoreType.DMA((6 + CHUNKS,))],
        stay=True,
    )
    came = swap(piece, Z2)
    across = swap(across, Y)
    beside, b, *sent = call(
        split_kernel,
        (piece, came, near, across),
        [((2 * cut + 8 * each, LANES), BF16), ((2 * rest, LANES), BF16)]
        + [((8 * each, rows), BF16)] * len(FAR),
    )
    came, came_b = swap(beside, Z1), swap(b, Y)
    sent = [swap(x, slot) if slot else x for x, slot in zip(sent, FAR)]
    a, b, both = call(
        join_kernel,
        (beside, came, b, came_b),
        [((4 * size, LANES), BF16) for size in (cut, rest, cut + rest)],
    )
    far_a, far_b, core = swap(a, Y), swap(b, Z1), swap(both, CORE)
    (columns,) = call(
        columns_kernel, (came, *sent), [((half * 2 * each, rows), BF16)], flops=8 * 10**9
    )
    far_a, far_b, core = lax.optimization_barrier((far_a, far_b, core))
    (pair,) = call(
        pair_kernel,
        (far_a, far_b, columns),
        [((4 * (cut + rest) + half * 2 * each, LANES), BF16)],
    )
    pair = swap(pair, CORE)
    early = call(
        functools.partial(early_kernel, own, slots, cut),
        (a, far_a, b, far_b, w_first),
        [
            ((total // 2, width), BF16),
            ((total // 2, width), BF16),
            ((half * rows, total), BF16),
            ((half, rows, rows), BF16),
            ((half, META, LANES), BF16),
            ((each, width), BF16),
        ],
        limit=LIMIT,
    )
    return call(
        functools.partial(step_kernel, own, slots, cut, rest),
        (core, pair, came, *sent, *early, w_first, w_second),
        [((1, rows, width), BF16), ((each, width), F32), ((each, width), F32)],
        [
            pltpu.VMEM((GROUP * rows, width), BF16),
            pltpu.VMEM((GROUP * rows, total), BF16),
            pltpu.VMEM((total, width), BF16),
            pltpu.VMEM((GROUP, rows, rows), BF16),
            pltpu.VMEM((GROUP, META, LANES), BF16),
            pltpu.VMEM((each, GROUP * rows), BF16),
            pltpu.VMEM((each, GROUP * rows), BF16),
            pltpu.VMEM((total, width), BF16),
        ],
        LIMIT,
    )


def split_body(features, counts, pick_owner, pick_local, adjacency, cotangent, w_first, w_second):
    owners = pick_owner[0]
    picks = pick_local[0]
    width = w_first.shape[0]
    slots = features.shape[1]
    count_picks = owners.shape[0]
    wanted = owners * features.shape[0] + picks
    feat_piece = lax.all_gather(features, "grp", axis=0, tiled=True)
    count_piece = lax.all_gather(counts, "grp", axis=0, tiled=True)
    live = jnp.take(count_piece, wanted, axis=0)
    rows = count_picks * slots
    inputs = jnp.take(feat_piece, wanted, axis=0).reshape(rows, width)
    mask = (jnp.arange(slots)[None, :] < live[:, None]).reshape(rows, 1).astype(BF16)
    inputs = inputs * mask
    maskf = mask.astype(F32)
    adj = adjacency[0]
    agg_first = nn(adj, inputs).astype(BF16)
    pre = nn(agg_first, w_first)
    hidden = (maskf * jax.nn.silu(pre)).astype(BF16)
    agg_second = nn(adj, hidden).astype(BF16)
    output = (maskf * nn(agg_second, w_second)).astype(BF16)
    dout = cotangent[0] * mask

    def summed(a, b):
        part = lax.dot_general(a, b, (((0,), (0,)), ((), ())), preferred_element_type=F32)
        return lax.psum_scatter(part, "grp", scatter_dimension=0, tiled=True)

    grad_second = summed(dout, agg_second)
    dagg = nt(dout, w_second).astype(BF16)
    back = lax.dot_general(adj, dagg, (((0,), (0,)), ((), ())), preferred_element_type=F32)
    sig = jax.nn.sigmoid(pre)
    dpre = (maskf * back * sig * (1.0 + pre * (1.0 - sig))).astype(BF16)
    grad_first = summed(dpre, agg_first)
    return (output.reshape(1, rows, width), grad_first, grad_second)


def solution(mesh):
    n = mesh.shape["grp"]

    def body(*args):
        rows = args[4].shape[1]
        return whole_body(*args) if n == GROUP and rows == LANES else split_body(*args)

    in_specs = (
        P(("parts", "grp"), None, None),
        P(("parts", "grp")),
        P(("parts", "grp"), None),
        P(("parts", "grp"), None),
        P(("parts", "grp"), None, None),
        P(("parts", "grp"), None, None),
        P(),
        P(),
    )
    out_specs = (
        P(("parts", "grp"), None, None),
        P(("parts", "grp"), None),
        P(("parts", "grp"), None),
    )
    return jax.shard_map(body, mesh=mesh, in_specs=in_specs, out_specs=out_specs, check_vma=False)
```

```python
import functools

import jax
import jax.numpy as jnp
from jax import lax
from jax.experimental import pallas as pl
from jax.experimental.pallas import tpu as pltpu
from jax.sharding import PartitionSpec as P

F32 = jnp.float32
BF16 = jnp.bfloat16
VMEM = pl.BlockSpec(memory_space=pltpu.VMEM)
HBM = pl.BlockSpec(memory_space=pltpu.HBM)
LANES = 128
META = 16
CHUNKS = 4
LIMIT = 16 * 2**20
SMALL = 8 * 2**20
Z2, Z1, Y, CORE = 8, 4, 2, 1
GROUP = 16
HINT = (0, 8 * 10**9, 0, 0, 0, 8 * 10**9, 0)
FAR = (Z2 | Z1, Z2, Z1, 0)
FIRST = (0, 2, 3)
LAST = (1,)
HALF_A = ((0, Z2, Z1, Z1 | Z2), (Y, Y | Z2, Y | Z1, Y | Z1 | Z2))
HALF_B = ((0, Z2, Y, Y | Z2), (Z1, Z1 | Z2, Z1 | Y, Z1 | Y | Z2))


def nn(a, b):
    return jnp.dot(a, b, preferred_element_type=F32)


def nt(a, b):
    return lax.dot_general(a, b, (((1,), (1,)), ((), ())), preferred_element_type=F32)


def start_all(moves, sems):
    copies = [pltpu.make_async_copy(a, b, sems.at[i]) for i, (a, b) in enumerate(moves)]
    for copy in copies:
        copy.start()
    return copies


def pack_kernel(counts, owner, local, features, adjacency, piece, *scratch):
    count, own_by, own_at, feat, adj, sems = scratch
    own, slots, width = features.shape
    rows = adjacency.shape[1]
    held = own * slots
    copies = start_all(zip((features, adjacency, counts, owner, local), (feat, adj, count, own_by, own_at)), sems)
    slot = lax.broadcasted_iota(jnp.int32, (slots, LANES), 0)
    line = lax.broadcasted_iota(jnp.int32, (META, LANES), 0)
    pick = lax.broadcasted_iota(jnp.int32, (META, LANES), 1) // slots
    meta = jnp.zeros((META, LANES), jnp.int32)
    for copy in copies:
        copy.wait()
    for i in range(own):
        live = slot < count[i]
        for b in range(width // LANES):
            block = feat[i, :, b * LANES : (b + 1) * LANES]
            at = b * held + i * slots
            piece[at : at + slots, :] = jnp.where(live, block, jnp.zeros_like(block))
        meta = jnp.where(line == 1 + i, count[i], meta)
    for k in range(owner.shape[1]):
        meta = jnp.where((line == 0) & (pick == k), own_by[0, k] * own + own_at[0, k], meta)
    at = held * (width // LANES)
    piece[at : at + rows, :] = adj[0]
    piece[at + rows : at + rows + META, :] = meta.astype(F32).astype(BF16)


def columns_kernel(cotangent, w_second, near, beside, across, *scratch):
    cot, second, turned, back, sems = scratch
    width = w_second.shape[0]
    each = width // GROUP
    place = lax.axis_index("grp")
    spans = [slice(c * width // CHUNKS, (c + 1) * width // CHUNKS) for c in range(CHUNKS)]
    moves = [(cotangent, cot)] + [(w_second.at[span], second.at[span]) for span in spans]
    copies = start_all(moves, sems)
    copies[0].wait()
    turned[...] = cot[0].astype(F32).T.astype(BF16)
    for span, copy in zip(spans, copies[1:]):
        copy.wait()
        back[span, :] = nt(second[span, :], cot[0]).astype(BF16)
    for out, slots in ((near, (0,)), (beside, (CORE,)), (across, (Y, Y | CORE))):
        at = 0
        for first in slots:
            for slot in range(first, GROUP, 4):
                span = pl.ds(pl.multiple_of((place ^ slot) * each, each), each)
                out[at : at + each, :] = turned[span, :]
                out[at + each : at + 2 * each, :] = back[span, :]
                at += 2 * each


def stack(out, at, *blocks):
    for block in blocks:
        out[at : at + block.shape[0], :] = block[...]
        at += block.shape[0]
    return at


def split_kernel(piece, came, half_a, half_b):
    cut = half_a.shape[0] // 2
    stack(half_a, 0, piece.at[:cut], came.at[:cut])
    stack(half_b, 0, piece.at[cut:], came.at[cut:])


def join_kernel(half_a, came_a, half_b, came_b, out_a, out_b, both):
    stack(out_a, 0, half_a, came_a)
    stack(out_b, 0, half_b, came_b)
    stack(both, 0, out_a, out_b)


def pair_kernel(far_a, far_b, out):
    stack(out, 0, far_a, far_b)


def half_kernel(across, out):
    stack(out, 0, across.at[across.shape[0] // 2 :])


def gather_kernel(*refs):
    stack(refs[-1], 0, *refs[:-1])


def along_kernel(near, beside, across, other, *sent):
    size = sent[0].shape[0] // 4
    for slot, out in zip(FAR, sent):
        span = slice(slot // 4 * size, (slot // 4 + 1) * size)
        stack(out, 0, *[ref.at[span] for ref in (near, beside, across, other)])


def place_of(slot):
    return slot // 2 + GROUP // 2 * (slot % 2)


def lay_out(arrays, held, cut, feat, adj, meta):
    rows = adj.shape[1]
    for ref, at, slots in arrays[:2]:
        for slot in slots:
            p = place_of(slot)
            for b in range(cut // held):
                feat[p * held : (p + 1) * held, b * LANES : (b + 1) * LANES] = ref[at : at + held, :]
                at += held
    for ref, at, slots in arrays[2:]:
        for slot in slots:
            p = place_of(slot)
            for b in range(cut // held, feat.shape[1] // LANES):
                feat[p * held : (p + 1) * held, b * LANES : (b + 1) * LANES] = ref[at : at + held, :]
                at += held
            adj[p] = ref[at : at + rows, :]
            at += rows
            meta[p] = ref[at : at + META, :]
            at += META


def spread_of(place, held, slots, adj, picks):
    line = lax.broadcasted_iota(jnp.int32, (held, LANES), 0)
    lane = lax.broadcasted_iota(jnp.int32, (1, LANES), 1) % slots
    owners = [None] * GROUP
    for slot in range(GROUP):
        owners[place_of(slot)] = place ^ slot
    code = jnp.concatenate([line + owner * held for owner in owners], axis=0)
    chosen = jnp.where(code == picks * slots + lane, 1.0, 0.0).astype(BF16)
    return nt(adj, chosen).astype(BF16)


def early_kernel(own, slots, cut, a, far_a, b, far_b, w_first, feat, lifted, spread, adj, meta, w_piece):
    held = own * slots
    rows = adj.shape[1]
    place = lax.axis_index("grp")
    arrays = list(zip((a, far_a, b, far_b), HALF_A + HALF_B))
    lay_out([(ref, 0, at) for ref, at in arrays], held, cut, feat, adj, meta)
    lifted[...] = nn(feat[...], w_first[...]).astype(BF16)
    for p in range(GROUP // 2):
        picks = meta[p, 0:1, :].astype(F32).astype(jnp.int32)
        spread[p * rows : (p + 1) * rows, :] = spread_of(place, held, slots, adj[p], picks)
    each = w_piece.shape[0]
    wide = max(each, LANES)
    per = wide // each
    start = pl.multiple_of((place // per) * wide, wide)
    block = w_first[:, pl.ds(start, wide)].astype(F32).T
    part = block[:each]
    for q in range(1, per):
        part = jnp.where(place % per == q, block[q * each : (q + 1) * each], part)
    w_piece[...] = part.astype(BF16)


def forward_kernel(own, slots, cut, rest, core, pair, *refs):
    early_feat, early_lifted, early_spread, early_adj, early_meta, w_piece = refs[:6]
    w_first, w_second, output, hidden, spread, feat, adj, keep, pre_piece = refs[6:15]
    meta, lifted = refs[15:]
    width = w_first.shape[0]
    held = own * slots
    rows = adj.shape[1]
    place = lax.axis_index("grp")
    first = GROUP // 2

    feat[: first * held, :] = early_feat[...]
    lifted[: first * held, :] = early_lifted[...]
    spread[: first * rows, :] = early_spread[...]
    adj[:first] = early_adj[...]
    meta[:first] = early_meta[...]
    arrays = []
    for size, start, halves in ((cut, 0, HALF_A), (rest, 4 * cut, HALF_B)):
        for ref, group in zip((core, pair), halves):
            arrays.append((ref, start, [slot | CORE for slot in group]))
    lay_out(arrays, held, cut, feat, adj, meta)
    metas = [meta[p].astype(F32) for p in range(GROUP)]
    picks = jnp.concatenate([m[0:1] for m in metas], axis=0).astype(jnp.int32)
    lane = lax.broadcasted_iota(jnp.int32, (GROUP, LANES), 1) % slots
    count = jnp.zeros((GROUP, LANES), jnp.int32)
    for slot in range(GROUP):
        for i in range(own):
            held_by = metas[place_of(slot)][1 + i : 2 + i].astype(jnp.int32)
            count = jnp.where(picks == (place ^ slot) * own + i, held_by, count)
    masks = (lane < count).astype(F32)
    keep[...] = masks

    late = slice(first * held, GROUP * held)
    lifted[late, :] = nn(feat[late, :], w_first[...]).astype(BF16)
    lifted_piece = nt(w_piece[...], feat[...]).astype(BF16)
    for p in range(first, GROUP):
        span = slice(p * rows, (p + 1) * rows)
        spread[span, :] = spread_of(place, held, slots, adj[p], picks[p : p + 1])
    step = min(width, 2 * LANES)
    for c in range(0, width, step):
        half = 0.5 * nn(spread[...], lifted[:, c : c + step])
        hidden[:, c : c + step] = (half + half * jnp.tanh(half)).astype(BF16)
    pre_piece[...] = nt(lifted_piece, spread[...])
    live = jnp.broadcast_to(masks[0:1], (rows, LANES)).T[:, :1]
    agg = nn(adj[0], (hidden[:rows, :].astype(F32) * live).astype(BF16)).astype(BF16)
    output[0] = (nn(agg, w_second[...]) * live).astype(BF16)


def gradient_kernel(hidden, spread, feat, adj, masks, pre_piece, *refs):
    far, *last = refs[: 1 + len(LAST)]
    grad_first, grad_second, dout, dpre = refs[1 + len(LAST) :]
    each = grad_first.shape[0]
    size = 8 * each
    sent = {FAR[i]: far.at[k * size : (k + 1) * size] for k, i in enumerate(FIRST)}
    sent.update({FAR[i]: ref for i, ref in zip(LAST, last)})
    rows = adj.shape[1]
    for slot in range(GROUP):
        p = place_of(slot)
        mask = masks[p : p + 1, :]
        span = slice(p * rows, (p + 1) * rows)
        at = slot % 4 * 2 * each
        source = sent[slot - slot % 4][at : at + 2 * each, :]
        back = nn((source.astype(F32) * mask).astype(BF16), adj[p]) * mask
        dout[:, span] = back[:each].astype(BF16)
        pre = pre_piece[:, span]
        sig = 0.5 + 0.5 * jnp.tanh(0.5 * pre)
        dpre[:, span] = (back[each:] * sig * (1.0 + pre * (1.0 - sig))).astype(BF16)
    grad_second[...] = nn(dout[...], hidden[...])
    moved = nn(dpre[...], spread[...])
    grad_first[...] = nn(moved.astype(BF16), feat[...])


def call(kernel, ins, outs, scratch=(), limit=SMALL, stay=False, flops=0):
    if stay:
        ins = [pltpu.with_memory_space_constraint(x, pltpu.HBM) for x in ins]
    return pl.pallas_call(
        kernel,
        out_shape=tuple(jax.ShapeDtypeStruct(*out) for out in outs),
        in_specs=[HBM if stay else VMEM] * len(ins),
        out_specs=(VMEM,) * len(outs),
        scratch_shapes=list(scratch),
        compiler_params=pltpu.CompilerParams(vmem_limit_bytes=limit),
        cost_estimate=pl.CostEstimate(flops=flops, bytes_accessed=0, transcendentals=0),
    )(*ins)


def whole_body(features, counts, pick_owner, pick_local, adjacency, cotangent, w_first, w_second):
    own, slots, width = features.shape
    rows = adjacency.shape[1]
    held = own * slots
    each = width // GROUP
    total = GROUP * held
    cut = held * (width // LANES * 3 // 4)
    rest = held * (width // LANES) + rows + META - cut
    half = GROUP // 2

    def swap(x, slot):
        return lax.ppermute(x, "grp", [(i, i ^ slot) for i in range(GROUP)])

    (piece,) = call(
        pack_kernel,
        (counts, pick_owner, pick_local, features, adjacency),
        [((cut + rest, LANES), BF16)],
        [pltpu.SMEM(x.shape, jnp.int32) for x in (counts, pick_owner, pick_local)]
        + [pltpu.VMEM(x.shape, BF16) for x in (features, adjacency)]
        + [pltpu.SemaphoreType.DMA((5,))],
        stay=True,
    )
    came = swap(piece, Z2)
    cotangent, _ = lax.optimization_barrier((cotangent, piece))
    near, beside, across = call(
        columns_kernel,
        (cotangent, w_second),
        [((8 * each, rows), BF16)] * 2 + [((16 * each, rows), BF16)],
        [pltpu.VMEM(x.shape, BF16) for x in (cotangent, w_second)]
        + [pltpu.VMEM((width, rows), BF16)] * 2
        + [pltpu.SemaphoreType.DMA((1 + CHUNKS,))],
        stay=True,
        flops=HINT[0],
    )
    came, across = lax.optimization_barrier((came, across))
    across = swap(across, Y)
    (other,) = call(half_kernel, (across,), [((8 * each, rows), BF16)], flops=HINT[1])
    beside, other = swap(beside, CORE), swap(other, CORE)
    sent = call(along_kernel, (near, beside, across, other), [((8 * each, rows), BF16)] * len(FAR), flops=HINT[2])
    sent = [swap(x, slot) if slot else x for x, slot in zip(sent, FAR)]

    a, b = call(split_kernel, (piece, came), [((2 * size, LANES), BF16) for size in (cut, rest)], flops=HINT[3])
    came_a, came_b = swap(a, Z1), swap(b, Y)
    a, b, both = call(
        join_kernel,
        (a, came_a, b, came_b),
        [((4 * size, LANES), BF16) for size in (cut, rest, cut + rest)],
        flops=HINT[4],
    )
    far_a, far_b, core = swap(a, Y), swap(b, Z1), swap(both, CORE)
    far_a, far_b, core = lax.optimization_barrier((far_a, far_b, core))
    (pair,) = call(pair_kernel, (far_a, far_b), [((4 * (cut + rest), LANES), BF16)])
    pair = swap(pair, CORE)
    (far,) = call(gather_kernel, [sent[i] for i in FIRST], [((8 * each * len(FIRST), rows), BF16)], flops=HINT[5])
    early = call(
        functools.partial(early_kernel, own, slots, cut),
        (a, far_a, b, far_b, w_first),
        [
            ((total // 2, width), BF16),
            ((total // 2, width), BF16),
            ((half * rows, total), BF16),
            ((half, rows, rows), BF16),
            ((half, META, LANES), BF16),
            ((each, width), BF16),
        ],
        limit=LIMIT,
    )
    pair, far = lax.optimization_barrier((pair, far))
    output, *kept = call(
        functools.partial(forward_kernel, own, slots, cut, rest),
        (core, pair, *early, w_first, w_second),
        [
            ((1, rows, width), BF16),
            ((GROUP * rows, width), BF16),
            ((GROUP * rows, total), BF16),
            ((total, width), BF16),
            ((GROUP, rows, rows), BF16),
            ((GROUP, LANES), F32),
            ((each, GROUP * rows), F32),
        ],
        [pltpu.VMEM((GROUP, META, LANES), BF16), pltpu.VMEM((total, width), BF16)],
        LIMIT,
        flops=HINT[6],
    )
    grad_first, grad_second = call(
        gradient_kernel,
        (*kept, far, *[sent[i] for i in LAST]),
        [((each, width), F32)] * 2,
        [pltpu.VMEM((each, GROUP * rows), BF16)] * 2,
        LIMIT,
    )
    return output, grad_first, grad_second


def split_body(features, counts, pick_owner, pick_local, adjacency, cotangent, w_first, w_second):
    owners = pick_owner[0]
    picks = pick_local[0]
    width = w_first.shape[0]
    slots = features.shape[1]
    count_picks = owners.shape[0]
    wanted = owners * features.shape[0] + picks
    feat_piece = lax.all_gather(features, "grp", axis=0, tiled=True)
    count_piece = lax.all_gather(counts, "grp", axis=0, tiled=True)
    live = jnp.take(count_piece, wanted, axis=0)
    rows = count_picks * slots
    inputs = jnp.take(feat_piece, wanted, axis=0).reshape(rows, width)
    mask = (jnp.arange(slots)[None, :] < live[:, None]).reshape(rows, 1).astype(BF16)
    inputs = inputs * mask
    maskf = mask.astype(F32)
    adj = adjacency[0]
    agg_first = nn(adj, inputs).astype(BF16)
    pre = nn(agg_first, w_first)
    hidden = (maskf * jax.nn.silu(pre)).astype(BF16)
    agg_second = nn(adj, hidden).astype(BF16)
    output = (maskf * nn(agg_second, w_second)).astype(BF16)
    dout = cotangent[0] * mask

    def summed(a, b):
        part = lax.dot_general(a, b, (((0,), (0,)), ((), ())), preferred_element_type=F32)
        return lax.psum_scatter(part, "grp", scatter_dimension=0, tiled=True)

    grad_second = summed(dout, agg_second)
    dagg = nt(dout, w_second).astype(BF16)
    back = lax.dot_general(adj, dagg, (((0,), (0,)), ((), ())), preferred_element_type=F32)
    sig = jax.nn.sigmoid(pre)
    dpre = (maskf * back * sig * (1.0 + pre * (1.0 - sig))).astype(BF16)
    grad_first = summed(dpre, agg_first)
    return (output.reshape(1, rows, width), grad_first, grad_second)


def solution(mesh):
    n = mesh.shape["grp"]

    def body(*args):
        rows = args[4].shape[1]
        return whole_body(*args) if n == GROUP and rows == LANES else split_body(*args)

    in_specs = (
        P(("parts", "grp"), None, None),
        P(("parts", "grp")),
        P(("parts", "grp"), None),
        P(("parts", "grp"), None),
        P(("parts", "grp"), None, None),
        P(("parts", "grp"), None, None),
        P(),
        P(),
    )
    out_specs = (
        P(("parts", "grp"), None, None),
        P(("parts", "grp"), None),
        P(("parts", "grp"), None),
    )
    return jax.shard_map(body, mesh=mesh, in_specs=in_specs, out_specs=out_specs, check_vma=False)
```

```python
import functools

import jax
import jax.numpy as jnp
from jax import lax
from jax.experimental import pallas as pl
from jax.experimental.pallas import tpu as pltpu
from jax.sharding import PartitionSpec as P

F32 = jnp.float32
BF16 = jnp.bfloat16
VMEM = pl.BlockSpec(memory_space=pltpu.VMEM)
HBM = pl.BlockSpec(memory_space=pltpu.HBM)
LANES = 128
META = 16
CHUNKS = 8
LIMIT = 24 * 2**20
SMALL = 8 * 2**20
Z2, Z1, Y, CORE = 8, 4, 2, 1
GROUP = 16
FAR = (Z2 | Z1, Z2)
NEAR = tuple(z | c for z in (0, *FAR) for c in (0, CORE))
ACROSS = tuple(Y | slot for slot in NEAR)
BESIDE = (Z1, Z1 | CORE, Z1 | Y, Z1 | Y | CORE)
HALF_A = ((0, Z2, Z1, Z1 | Z2), (Y, Y | Z2, Y | Z1, Y | Z1 | Z2))
HALF_B = ((0, Z2, Y, Y | Z2), (Z1, Z1 | Z2, Z1 | Y, Z1 | Y | Z2))


def nn(a, b):
    return jnp.dot(a, b, preferred_element_type=F32)


def nt(a, b):
    return lax.dot_general(a, b, (((1,), (1,)), ((), ())), preferred_element_type=F32)


def prepare_kernel(counts, owner, local, features, adjacency, cotangent, w_second, *refs):
    piece, near, across, beside, count, own_by, own_at, feat, adj, cot, second, turned, back, sems = refs
    own, slots, width = features.shape
    rows = adjacency.shape[1]
    each = width // GROUP
    place = lax.axis_index("grp")
    moves = [(features, feat), (adjacency, adj), (counts, count), (owner, own_by), (local, own_at)]
    moves.append((cotangent, cot))
    some = width // CHUNKS
    for c in range(CHUNKS):
        span = slice(c * some, (c + 1) * some)
        moves.append((w_second.at[span], second.at[span]))
    copies = [pltpu.make_async_copy(a, b, sems.at[i]) for i, (a, b) in enumerate(moves)]
    for copy in copies:
        copy.start()

    held = own * slots
    slot = lax.broadcasted_iota(jnp.int32, (slots, LANES), 0)
    line = lax.broadcasted_iota(jnp.int32, (META, LANES), 0)
    pick = lax.broadcasted_iota(jnp.int32, (META, LANES), 1) // slots
    meta = jnp.zeros((META, LANES), jnp.int32)
    for copy in copies[:5]:
        copy.wait()
    for i in range(own):
        live = slot < count[i]
        for b in range(width // LANES):
            block = feat[i, :, b * LANES : (b + 1) * LANES]
            at = b * held + i * slots
            piece[at : at + slots, :] = jnp.where(live, block, jnp.zeros_like(block))
        meta = jnp.where(line == 1 + i, count[i], meta)
    for k in range(owner.shape[1]):
        meta = jnp.where((line == 0) & (pick == k), own_by[0, k] * own + own_at[0, k], meta)
    at = held * (width // LANES)
    piece[at : at + rows, :] = adj[0]
    piece[at + rows : at + rows + META, :] = meta.astype(F32).astype(BF16)

    copies[5].wait()
    turned[...] = cot[0].astype(F32).T.astype(BF16)
    for c in range(CHUNKS):
        copies[6 + c].wait()
        span = slice(c * some, (c + 1) * some)
        back[span, :] = nt(second[span, :], cot[0]).astype(BF16)
    for out, slots in ((near, NEAR), (across, ACROSS), (beside, BESIDE)):
        for i, slot in enumerate(slots):
            span = pl.ds(pl.multiple_of((place ^ slot) * each, each), each)
            at = i * 2 * each
            out[at : at + each, :] = turned[span, :]
            out[at + each : at + 2 * each, :] = back[span, :]


def stack(out, at, *blocks):
    for block in blocks:
        out[at : at + block.shape[0], :] = block[...]
        at += block.shape[0]
    return at


def split_kernel(piece, came, near, across, beside, half_a, turn, keep, *sent):
    cut = half_a.shape[0] // 2
    stack(half_a, 0, piece.at[:cut], came.at[:cut])
    two = beside.shape[0] // 2
    stack(turn, 0, piece.at[cut:], came.at[cut:], beside.at[two:])
    stack(keep, 0, near.at[:two], across.at[:two], beside.at[:two])
    for i, out in enumerate(sent, 1):
        span = slice(i * two, (i + 1) * two)
        stack(out, 0, near.at[span], across.at[span])


def join_kernel(half_a, came_a, turn, came_b, out_a, out_b, both):
    size = out_b.shape[0] // 2
    stack(out_a, 0, half_a, came_a)
    stack(out_b, 0, turn.at[:size], came_b.at[:size])
    stack(both, 0, out_a, out_b)


def block_of(slot, rows, keep, came, *sent):
    z, h, b = slot - slot % 4, slot // 2 % 2, slot % 2
    if z in FAR:
        ref, at = sent[FAR.index(z)], 2 * h + b
    elif z == 0 or h == 0:
        ref, at = keep, (4 if z else 2 * h) + b
    else:
        ref, at = came, came.shape[0] // rows - 2 + b
    at = at * rows + ref.shape[0] % rows
    return ref.at[at : at + rows]


def columns_kernel(*refs):
    *refs, out = refs
    rows = out.shape[0] * 2 // GROUP
    at = 0
    for slot in range(1, GROUP, 2):
        at = stack(out, at, block_of(slot, rows, *refs))


def pair_kernel(far_a, far_b, columns, out):
    stack(out, 0, far_a, far_b, columns)


def place_of(slot):
    return slot // 2 + GROUP // 2 * (slot % 2)


def lay_out(arrays, held, cut, feat, adj, meta):
    rows = adj.shape[1]
    for ref, at, slots in arrays[:2]:
        for slot in slots:
            p = place_of(slot)
            for b in range(cut // held):
                feat[p * held : (p + 1) * held, b * LANES : (b + 1) * LANES] = ref[at : at + held, :]
                at += held
    for ref, at, slots in arrays[2:]:
        for slot in slots:
            p = place_of(slot)
            for b in range(cut // held, feat.shape[1] // LANES):
                feat[p * held : (p + 1) * held, b * LANES : (b + 1) * LANES] = ref[at : at + held, :]
                at += held
            adj[p] = ref[at : at + rows, :]
            at += rows
            meta[p] = ref[at : at + META, :]
            at += META


def spread_of(place, held, slots, adj, picks):
    line = lax.broadcasted_iota(jnp.int32, (held, LANES), 0)
    lane = lax.broadcasted_iota(jnp.int32, (1, LANES), 1) % slots
    owners = [None] * GROUP
    for slot in range(GROUP):
        owners[place_of(slot)] = place ^ slot
    code = jnp.concatenate([line + owner * held for owner in owners], axis=0)
    chosen = jnp.where(code == picks * slots + lane, 1.0, 0.0).astype(BF16)
    return nt(adj, chosen).astype(BF16)


def early_kernel(own, slots, cut, a, far_a, b, far_b, w_first, feat, lifted, spread, adj, meta, w_piece):
    held = own * slots
    rows = adj.shape[1]
    place = lax.axis_index("grp")
    arrays = list(zip((a, far_a, b, far_b), HALF_A + HALF_B))
    lay_out([(ref, 0, at) for ref, at in arrays], held, cut, feat, adj, meta)
    lifted[...] = nn(feat[...], w_first[...]).astype(BF16)
    for p in range(GROUP // 2):
        picks = meta[p, 0:1, :].astype(F32).astype(jnp.int32)
        spread[p * rows : (p + 1) * rows, :] = spread_of(place, held, slots, adj[p], picks)
    each = w_piece.shape[0]
    wide = max(each, LANES)
    per = wide // each
    start = pl.multiple_of((place // per) * wide, wide)
    block = w_first[:, pl.ds(start, wide)].astype(F32).T
    part = block[:each]
    for q in range(1, per):
        part = jnp.where(place % per == q, block[q * each : (q + 1) * each], part)
    w_piece[...] = part.astype(BF16)


def step_kernel(own, slots, cut, rest, core, pair, *refs):
    blocks, refs = refs[: 2 + len(FAR)], refs[2 + len(FAR) :]
    early_feat, early_lifted, early_spread, early_adj, early_meta, w_piece = refs[:6]
    w_first, w_second, output, grad_first, grad_second = refs[6:11]
    hidden, spread, feat, adj, meta, dout, dpre, lifted = refs[11:]
    width = w_first.shape[0]
    held = own * slots
    rows = adj.shape[1]
    place = lax.axis_index("grp")
    first = GROUP // 2

    feat[: first * held, :] = early_feat[...]
    lifted[: first * held, :] = early_lifted[...]
    spread[: first * rows, :] = early_spread[...]
    adj[:first] = early_adj[...]
    meta[:first] = early_meta[...]
    arrays = []
    for size, start, halves in ((cut, 0, HALF_A), (rest, 4 * cut, HALF_B)):
        for ref, group in zip((core, pair), halves):
            arrays.append((ref, start, [slot | CORE for slot in group]))
    deep = 4 * (cut + rest)
    lay_out(arrays, held, cut, feat, adj, meta)
    metas = [meta[p].astype(F32) for p in range(GROUP)]
    picks = jnp.concatenate([m[0:1] for m in metas], axis=0).astype(jnp.int32)
    lane = lax.broadcasted_iota(jnp.int32, (GROUP, LANES), 1) % slots
    count = jnp.zeros((GROUP, LANES), jnp.int32)
    for slot in range(GROUP):
        for i in range(own):
            held_by = metas[place_of(slot)][1 + i : 2 + i].astype(jnp.int32)
            count = jnp.where(picks == (place ^ slot) * own + i, held_by, count)
    masks = (lane < count).astype(F32)

    late = slice(first * held, GROUP * held)
    lifted[late, :] = nn(feat[late, :], w_first[...]).astype(BF16)
    lifted_piece = nt(w_piece[...], feat[...]).astype(BF16)
    for p in range(first, GROUP):
        span = slice(p * rows, (p + 1) * rows)
        spread[span, :] = spread_of(place, held, slots, adj[p], picks[p : p + 1])
    step = min(width, 2 * LANES)
    for c in range(0, width, step):
        half = 0.5 * nn(spread[...], lifted[:, c : c + step])
        hidden[:, c : c + step] = (half + half * jnp.tanh(half)).astype(BF16)
    pre_piece = nt(lifted_piece, spread[...])
    live = jnp.broadcast_to(masks[0:1], (rows, LANES)).T[:, :1]
    agg = nn(adj[0], (hidden[:rows, :].astype(F32) * live).astype(BF16)).astype(BF16)
    output[0] = (nn(agg, w_second[...]) * live).astype(BF16)

    each = grad_first.shape[0]
    for slot in range(GROUP):
        p = place_of(slot)
        mask = masks[p : p + 1]
        span = slice(p * rows, (p + 1) * rows)
        if slot % 2:
            at = deep + slot // 2 * 2 * each
            source = pair[at : at + 2 * each, :]
        else:
            source = block_of(slot, 2 * each, *blocks)[...]
        back = nn((source.astype(F32) * mask).astype(BF16), adj[p]) * mask
        dout[:, span] = back[:each].astype(BF16)
        pre = pre_piece[:, span]
        sig = 0.5 + 0.5 * jnp.tanh(0.5 * pre)
        dpre[:, span] = (back[each:] * sig * (1.0 + pre * (1.0 - sig))).astype(BF16)
    grad_second[...] = nn(dout[...], hidden[...])
    moved = nn(dpre[...], spread[...])
    grad_first[...] = nn(moved.astype(BF16), feat[...])


def call(kernel, ins, outs, scratch=(), limit=SMALL, stay=False, flops=0):
    if stay:
        ins = [pltpu.with_memory_space_constraint(x, pltpu.HBM) for x in ins]
    return pl.pallas_call(
        kernel,
        out_shape=tuple(jax.ShapeDtypeStruct(*out) for out in outs),
        in_specs=[HBM if stay else VMEM] * len(ins),
        out_specs=(VMEM,) * len(outs),
        scratch_shapes=list(scratch),
        compiler_params=pltpu.CompilerParams(vmem_limit_bytes=limit),
        cost_estimate=pl.CostEstimate(flops=flops, bytes_accessed=0, transcendentals=0),
    )(*ins)


def whole_body(features, counts, pick_owner, pick_local, adjacency, cotangent, w_first, w_second):
    own, slots, width = features.shape
    rows = adjacency.shape[1]
    held = own * slots
    each = width // GROUP
    total = GROUP * held
    cut = held * (width // LANES * 3 // 4)
    rest = held * (width // LANES) + rows + META - cut
    half = GROUP // 2

    def swap(x, slot):
        return lax.ppermute(x, "grp", [(i, i ^ slot) for i in range(GROUP)])

    piece, near, across, beside = call(
        prepare_kernel,
        (counts, pick_owner, pick_local, features, adjacency, cotangent, w_second),
        [((cut + rest, LANES), BF16)]
        + [((len(x) * 2 * each, rows), BF16) for x in (NEAR, ACROSS, BESIDE)],
        [pltpu.SMEM(x.shape, jnp.int32) for x in (counts, pick_owner, pick_local)]
        + [pltpu.VMEM(x.shape, BF16) for x in (features, adjacency, cotangent, w_second)]
        + [pltpu.VMEM((width, rows), BF16)] * 2
        + [pltpu.SemaphoreType.DMA((6 + CHUNKS,))],
        stay=True,
    )
    came, across, beside = swap(piece, Z2), swap(across, Y), swap(beside, Z1)
    a, turn, keep, *sent = call(
        split_kernel,
        (piece, came, near, across, beside),
        [((x, LANES), BF16) for x in (2 * cut, 2 * rest + 4 * each, 12 * each)]
        + [((8 * each, rows), BF16)] * len(FAR),
    )
    came_a, came_b = swap(a, Z1), swap(turn, Y)
    sent = [swap(x, slot) for x, slot in zip(sent, FAR)]
    a, b, both = call(
        join_kernel,
        (a, came_a, turn, came_b),
        [((4 * size, LANES), BF16) for size in (cut, rest, cut + rest)],
    )
    far_a, far_b, core = swap(a, Y), swap(b, Z1), swap(both, CORE)
    (columns,) = call(
        columns_kernel, (keep, came_b, *sent), [((half * 2 * each, rows), BF16)], flops=8 * 10**9
    )
    far_a, far_b, core = lax.optimization_barrier((far_a, far_b, core))
    (pair,) = call(
        pair_kernel,
        (far_a, far_b, columns),
        [((4 * (cut + rest) + half * 2 * each, LANES), BF16)],
    )
    pair = swap(pair, CORE)
    early = call(
        functools.partial(early_kernel, own, slots, cut),
        (a, far_a, b, far_b, w_first),
        [
            ((total // 2, width), BF16),
            ((total // 2, width), BF16),
            ((half * rows, total), BF16),
            ((half, rows, rows), BF16),
            ((half, META, LANES), BF16),
            ((each, width), BF16),
        ],
        limit=LIMIT,
    )
    return call(
        functools.partial(step_kernel, own, slots, cut, rest),
        (core, pair, keep, came_b, *sent, *early, w_first, w_second),
        [((1, rows, width), BF16), ((each, width), F32), ((each, width), F32)],
        [
            pltpu.VMEM((GROUP * rows, width), BF16),
            pltpu.VMEM((GROUP * rows, total), BF16),
            pltpu.VMEM((total, width), BF16),
            pltpu.VMEM((GROUP, rows, rows), BF16),
            pltpu.VMEM((GROUP, META, LANES), BF16),
            pltpu.VMEM((each, GROUP * rows), BF16),
            pltpu.VMEM((each, GROUP * rows), BF16),
            pltpu.VMEM((total, width), BF16),
        ],
        LIMIT,
    )


def split_body(features, counts, pick_owner, pick_local, adjacency, cotangent, w_first, w_second):
    owners = pick_owner[0]
    picks = pick_local[0]
    width = w_first.shape[0]
    slots = features.shape[1]
    count_picks = owners.shape[0]
    wanted = owners * features.shape[0] + picks
    feat_piece = lax.all_gather(features, "grp", axis=0, tiled=True)
    count_piece = lax.all_gather(counts, "grp", axis=0, tiled=True)
    live = jnp.take(count_piece, wanted, axis=0)
    rows = count_picks * slots
    inputs = jnp.take(feat_piece, wanted, axis=0).reshape(rows, width)
    mask = (jnp.arange(slots)[None, :] < live[:, None]).reshape(rows, 1).astype(BF16)
    inputs = inputs * mask
    maskf = mask.astype(F32)
    adj = adjacency[0]
    agg_first = nn(adj, inputs).astype(BF16)
    pre = nn(agg_first, w_first)
    hidden = (maskf * jax.nn.silu(pre)).astype(BF16)
    agg_second = nn(adj, hidden).astype(BF16)
    output = (maskf * nn(agg_second, w_second)).astype(BF16)
    dout = cotangent[0] * mask

    def summed(a, b):
        part = lax.dot_general(a, b, (((0,), (0,)), ((), ())), preferred_element_type=F32)
        return lax.psum_scatter(part, "grp", scatter_dimension=0, tiled=True)

    grad_second = summed(dout, agg_second)
    dagg = nt(dout, w_second).astype(BF16)
    back = lax.dot_general(adj, dagg, (((0,), (0,)), ((), ())), preferred_element_type=F32)
    sig = jax.nn.sigmoid(pre)
    dpre = (maskf * back * sig * (1.0 + pre * (1.0 - sig))).astype(BF16)
    grad_first = summed(dpre, agg_first)
    return (output.reshape(1, rows, width), grad_first, grad_second)


def solution(mesh):
    n = mesh.shape["grp"]

    def body(*args):
        rows = args[4].shape[1]
        return whole_body(*args) if n == GROUP and rows == LANES else split_body(*args)

    in_specs = (
        P(("parts", "grp"), None, None),
        P(("parts", "grp")),
        P(("parts", "grp"), None),
        P(("parts", "grp"), None),
        P(("parts", "grp"), None, None),
        P(("parts", "grp"), None, None),
        P(),
        P(),
    )
    out_specs = (
        P(("parts", "grp"), None, None),
        P(("parts", "grp"), None),
        P(("parts", "grp"), None),
    )
    return jax.shard_map(body, mesh=mesh, in_specs=in_specs, out_specs=out_specs, check_vma=False)
```

```python
import functools

import jax
import jax.numpy as jnp
from jax import lax
from jax.experimental import pallas as pl
from jax.experimental.pallas import tpu as pltpu
from jax.sharding import PartitionSpec as P

F32 = jnp.float32
BF16 = jnp.bfloat16
VMEM = pl.BlockSpec(memory_space=pltpu.VMEM)
HBM = pl.BlockSpec(memory_space=pltpu.HBM)
LANES = 128
META = 16
CHUNKS = 4
LIMIT = 24 * 2**20
SMALL = 8 * 2**20
Z2, Z1, Y, CORE = 8, 4, 2, 1
GROUP = 16
HINT = (0, 8 * 10**9)
PLACES = tuple(range(0, GROUP, 2))
HALF_A = ((0, Z2, Z1, Z1 | Z2), (Y, Y | Z2, Y | Z1, Y | Z1 | Z2))
HALF_B = ((0, Z2, Y, Y | Z2), (Z1, Z1 | Z2, Z1 | Y, Z1 | Y | Z2))


def nn(a, b):
    return jnp.dot(a, b, preferred_element_type=F32)


def nt(a, b):
    return lax.dot_general(a, b, (((1,), (1,)), ((), ())), preferred_element_type=F32)


def start_all(moves, sems):
    copies = [pltpu.make_async_copy(a, b, sems.at[i]) for i, (a, b) in enumerate(moves)]
    for copy in copies:
        copy.start()
    return copies


def pack_kernel(counts, owner, local, features, adjacency, piece, *scratch):
    count, own_by, own_at, feat, adj, sems = scratch
    own, slots, width = features.shape
    rows = adjacency.shape[1]
    held = own * slots
    copies = start_all(zip((features, adjacency, counts, owner, local), (feat, adj, count, own_by, own_at)), sems)
    slot = lax.broadcasted_iota(jnp.int32, (slots, LANES), 0)
    line = lax.broadcasted_iota(jnp.int32, (META, LANES), 0)
    pick = lax.broadcasted_iota(jnp.int32, (META, LANES), 1) // slots
    meta = jnp.zeros((META, LANES), jnp.int32)
    for copy in copies:
        copy.wait()
    for i in range(own):
        live = slot < count[i]
        for b in range(width // LANES):
            block = feat[i, :, b * LANES : (b + 1) * LANES]
            at = b * held + i * slots
            piece[at : at + slots, :] = jnp.where(live, block, jnp.zeros_like(block))
        meta = jnp.where(line == 1 + i, count[i], meta)
    for k in range(owner.shape[1]):
        meta = jnp.where((line == 0) & (pick == k), own_by[0, k] * own + own_at[0, k], meta)
    at = held * (width // LANES)
    piece[at : at + rows, :] = adj[0]
    piece[at + rows : at + rows + META, :] = meta.astype(F32).astype(BF16)


def columns_kernel(cotangent, w_second, *refs):
    outs, (cot, second, turned, back, sems) = refs[: len(PLACES)], refs[len(PLACES) :]
    width = w_second.shape[0]
    each = width // GROUP
    place = lax.axis_index("grp")
    spans = [slice(c * width // CHUNKS, (c + 1) * width // CHUNKS) for c in range(CHUNKS)]
    moves = [(cotangent, cot)] + [(w_second.at[span], second.at[span]) for span in spans]
    copies = start_all(moves, sems)
    copies[0].wait()
    turned[...] = cot[0].astype(F32).T.astype(BF16)
    for span, copy in zip(spans, copies[1:]):
        copy.wait()
        back[span, :] = nt(second[span, :], cot[0]).astype(BF16)
    for out, slot in zip(outs, PLACES):
        for core in range(2):
            span = pl.ds(pl.multiple_of((place ^ (slot | core)) * each, each), each)
            at = core * 2 * each
            out[at : at + each, :] = turned[span, :]
            out[at + each : at + 2 * each, :] = back[span, :]


def stack(out, at, *blocks):
    for block in blocks:
        out[at : at + block.shape[0], :] = block[...]
        at += block.shape[0]
    return at


def split_kernel(piece, came, half_a, half_b):
    cut = half_a.shape[0] // 2
    stack(half_a, 0, piece.at[:cut], came.at[:cut])
    stack(half_b, 0, piece.at[cut:], came.at[cut:])


def join_kernel(half_a, came_a, half_b, came_b, out_a, out_b, both):
    stack(out_a, 0, half_a, came_a)
    stack(out_b, 0, half_b, came_b)
    stack(both, 0, out_a, out_b)


def other_kernel(*refs):
    *blocks, out = refs
    rows = out.shape[0] // len(PLACES)
    stack(out, 0, *[ref.at[rows:] for ref in blocks])


def pair_kernel(far_a, far_b, columns, out):
    stack(out, 0, far_a, far_b, columns)


def place_of(slot):
    return slot // 2 + GROUP // 2 * (slot % 2)


def lay_out(arrays, held, cut, feat, adj, meta):
    rows = adj.shape[1]
    for ref, at, slots in arrays[:2]:
        for slot in slots:
            p = place_of(slot)
            for b in range(cut // held):
                feat[p * held : (p + 1) * held, b * LANES : (b + 1) * LANES] = ref[at : at + held, :]
                at += held
    for ref, at, slots in arrays[2:]:
        for slot in slots:
            p = place_of(slot)
            for b in range(cut // held, feat.shape[1] // LANES):
                feat[p * held : (p + 1) * held, b * LANES : (b + 1) * LANES] = ref[at : at + held, :]
                at += held
            adj[p] = ref[at : at + rows, :]
            at += rows
            meta[p] = ref[at : at + META, :]
            at += META


def spread_of(place, held, slots, adj, picks):
    line = lax.broadcasted_iota(jnp.int32, (held, LANES), 0)
    lane = lax.broadcasted_iota(jnp.int32, (1, LANES), 1) % slots
    owners = [None] * GROUP
    for slot in range(GROUP):
        owners[place_of(slot)] = place ^ slot
    code = jnp.concatenate([line + owner * held for owner in owners], axis=0)
    chosen = jnp.where(code == picks * slots + lane, 1.0, 0.0).astype(BF16)
    return nt(adj, chosen).astype(BF16)


def early_kernel(own, slots, cut, a, far_a, b, far_b, w_first, feat, lifted, spread, adj, meta, w_piece):
    held = own * slots
    rows = adj.shape[1]
    place = lax.axis_index("grp")
    arrays = list(zip((a, far_a, b, far_b), HALF_A + HALF_B))
    lay_out([(ref, 0, at) for ref, at in arrays], held, cut, feat, adj, meta)
    lifted[...] = nn(feat[...], w_first[...]).astype(BF16)
    for p in range(GROUP // 2):
        picks = meta[p, 0:1, :].astype(F32).astype(jnp.int32)
        spread[p * rows : (p + 1) * rows, :] = spread_of(place, held, slots, adj[p], picks)
    each = w_piece.shape[0]
    wide = max(each, LANES)
    per = wide // each
    start = pl.multiple_of((place // per) * wide, wide)
    block = w_first[:, pl.ds(start, wide)].astype(F32).T
    part = block[:each]
    for q in range(1, per):
        part = jnp.where(place % per == q, block[q * each : (q + 1) * each], part)
    w_piece[...] = part.astype(BF16)


def step_kernel(own, slots, cut, rest, core, pair, *refs):
    blocks, refs = refs[: len(PLACES)], refs[len(PLACES) :]
    early_feat, early_lifted, early_spread, early_adj, early_meta, w_piece = refs[:6]
    w_first, w_second, output, grad_first, grad_second = refs[6:11]
    hidden, spread, feat, adj, meta, dout, dpre, lifted = refs[11:]
    width = w_first.shape[0]
    held = own * slots
    rows = adj.shape[1]
    place = lax.axis_index("grp")
    first = GROUP // 2

    feat[: first * held, :] = early_feat[...]
    lifted[: first * held, :] = early_lifted[...]
    spread[: first * rows, :] = early_spread[...]
    adj[:first] = early_adj[...]
    meta[:first] = early_meta[...]
    arrays = []
    for size, start, halves in ((cut, 0, HALF_A), (rest, 4 * cut, HALF_B)):
        for ref, group in zip((core, pair), halves):
            arrays.append((ref, start, [slot | CORE for slot in group]))
    deep = 4 * (cut + rest)
    lay_out(arrays, held, cut, feat, adj, meta)
    metas = [meta[p].astype(F32) for p in range(GROUP)]
    picks = jnp.concatenate([m[0:1] for m in metas], axis=0).astype(jnp.int32)
    lane = lax.broadcasted_iota(jnp.int32, (GROUP, LANES), 1) % slots
    count = jnp.zeros((GROUP, LANES), jnp.int32)
    for slot in range(GROUP):
        for i in range(own):
            held_by = metas[place_of(slot)][1 + i : 2 + i].astype(jnp.int32)
            count = jnp.where(picks == (place ^ slot) * own + i, held_by, count)
    masks = (lane < count).astype(F32)

    late = slice(first * held, GROUP * held)
    lifted[late, :] = nn(feat[late, :], w_first[...]).astype(BF16)
    lifted_piece = nt(w_piece[...], feat[...]).astype(BF16)
    for p in range(first, GROUP):
        span = slice(p * rows, (p + 1) * rows)
        spread[span, :] = spread_of(place, held, slots, adj[p], picks[p : p + 1])
    step = min(width, 2 * LANES)
    for c in range(0, width, step):
        half = 0.5 * nn(spread[...], lifted[:, c : c + step])
        hidden[:, c : c + step] = (half + half * jnp.tanh(half)).astype(BF16)
    pre_piece = nt(lifted_piece, spread[...])
    live = jnp.broadcast_to(masks[0:1], (rows, LANES)).T[:, :1]
    agg = nn(adj[0], (hidden[:rows, :].astype(F32) * live).astype(BF16)).astype(BF16)
    output[0] = (nn(agg, w_second[...]) * live).astype(BF16)

    each = grad_first.shape[0]
    for slot in range(GROUP):
        p = place_of(slot)
        mask = masks[p : p + 1]
        span = slice(p * rows, (p + 1) * rows)
        if slot % 2:
            at = deep + slot // 2 * 2 * each
            source = pair[at : at + 2 * each, :]
        else:
            source = blocks[slot // 2][: 2 * each, :]
        back = nn((source.astype(F32) * mask).astype(BF16), adj[p]) * mask
        dout[:, span] = back[:each].astype(BF16)
        pre = pre_piece[:, span]
        sig = 0.5 + 0.5 * jnp.tanh(0.5 * pre)
        dpre[:, span] = (back[each:] * sig * (1.0 + pre * (1.0 - sig))).astype(BF16)
    grad_second[...] = nn(dout[...], hidden[...])
    moved = nn(dpre[...], spread[...])
    grad_first[...] = nn(moved.astype(BF16), feat[...])


def call(kernel, ins, outs, scratch=(), limit=SMALL, stay=False, flops=0):
    if stay:
        ins = [pltpu.with_memory_space_constraint(x, pltpu.HBM) for x in ins]
    return pl.pallas_call(
        kernel,
        out_shape=tuple(jax.ShapeDtypeStruct(*out) for out in outs),
        in_specs=[HBM if stay else VMEM] * len(ins),
        out_specs=(VMEM,) * len(outs),
        scratch_shapes=list(scratch),
        compiler_params=pltpu.CompilerParams(vmem_limit_bytes=limit),
        cost_estimate=pl.CostEstimate(flops=flops, bytes_accessed=0, transcendentals=0),
    )(*ins)


def whole_body(features, counts, pick_owner, pick_local, adjacency, cotangent, w_first, w_second):
    own, slots, width = features.shape
    rows = adjacency.shape[1]
    held = own * slots
    each = width // GROUP
    total = GROUP * held
    cut = held * (width // LANES * 3 // 4)
    rest = held * (width // LANES) + rows + META - cut
    half = GROUP // 2

    def swap(x, slot):
        return lax.ppermute(x, "grp", [(i, i ^ slot) for i in range(GROUP)])

    (piece,) = call(
        pack_kernel,
        (counts, pick_owner, pick_local, features, adjacency),
        [((cut + rest, LANES), BF16)],
        [pltpu.SMEM(x.shape, jnp.int32) for x in (counts, pick_owner, pick_local)]
        + [pltpu.VMEM(x.shape, BF16) for x in (features, adjacency)]
        + [pltpu.SemaphoreType.DMA((5,))],
        stay=True,
    )
    came = swap(piece, Z2)
    cotangent, _ = lax.optimization_barrier((cotangent, piece))
    columns = list(call(
        columns_kernel,
        (cotangent, w_second),
        [((4 * each, rows), BF16)] * len(PLACES),
        [pltpu.VMEM(x.shape, BF16) for x in (cotangent, w_second)]
        + [pltpu.VMEM((width, rows), BF16)] * 2
        + [pltpu.SemaphoreType.DMA((1 + CHUNKS,))],
        stay=True,
    ))
    came, columns[0] = lax.optimization_barrier((came, columns[0]))
    columns = [swap(x, slot) if slot else x for x, slot in zip(columns, PLACES)]
    a, b = call(split_kernel, (piece, came), [((2 * size, LANES), BF16) for size in (cut, rest)])
    came_a, came_b = swap(a, Z1), swap(b, Y)
    a, b, both = call(
        join_kernel,
        (a, came_a, b, came_b),
        [((4 * size, LANES), BF16) for size in (cut, rest, cut + rest)],
        flops=HINT[0],
    )
    far_a, far_b, core = swap(a, Y), swap(b, Z1), swap(both, CORE)
    (others,) = call(other_kernel, columns, [((half * 2 * each, rows), BF16)], flops=HINT[1])
    far_a, far_b, core = lax.optimization_barrier((far_a, far_b, core))
    (pair,) = call(
        pair_kernel,
        (far_a, far_b, others),
        [((4 * (cut + rest) + half * 2 * each, LANES), BF16)],
    )
    pair = swap(pair, CORE)
    early = call(
        functools.partial(early_kernel, own, slots, cut),
        (a, far_a, b, far_b, w_first),
        [
            ((total // 2, width), BF16),
            ((total // 2, width), BF16),
            ((half * rows, total), BF16),
            ((half, rows, rows), BF16),
            ((half, META, LANES), BF16),
            ((each, width), BF16),
        ],
        limit=LIMIT,
    )
    return call(
        functools.partial(step_kernel, own, slots, cut, rest),
        (core, pair, *columns, *early, w_first, w_second),
        [((1, rows, width), BF16), ((each, width), F32), ((each, width), F32)],
        [
            pltpu.VMEM((GROUP * rows, width), BF16),
            pltpu.VMEM((GROUP * rows, total), BF16),
            pltpu.VMEM((total, width), BF16),
            pltpu.VMEM((GROUP, rows, rows), BF16),
            pltpu.VMEM((GROUP, META, LANES), BF16),
            pltpu.VMEM((each, GROUP * rows), BF16),
            pltpu.VMEM((each, GROUP * rows), BF16),
            pltpu.VMEM((total, width), BF16),
        ],
        LIMIT,
    )


def split_body(features, counts, pick_owner, pick_local, adjacency, cotangent, w_first, w_second):
    owners = pick_owner[0]
    picks = pick_local[0]
    width = w_first.shape[0]
    slots = features.shape[1]
    count_picks = owners.shape[0]
    wanted = owners * features.shape[0] + picks
    feat_piece = lax.all_gather(features, "grp", axis=0, tiled=True)
    count_piece = lax.all_gather(counts, "grp", axis=0, tiled=True)
    live = jnp.take(count_piece, wanted, axis=0)
    rows = count_picks * slots
    inputs = jnp.take(feat_piece, wanted, axis=0).reshape(rows, width)
    mask = (jnp.arange(slots)[None, :] < live[:, None]).reshape(rows, 1).astype(BF16)
    inputs = inputs * mask
    maskf = mask.astype(F32)
    adj = adjacency[0]
    agg_first = nn(adj, inputs).astype(BF16)
    pre = nn(agg_first, w_first)
    hidden = (maskf * jax.nn.silu(pre)).astype(BF16)
    agg_second = nn(adj, hidden).astype(BF16)
    output = (maskf * nn(agg_second, w_second)).astype(BF16)
    dout = cotangent[0] * mask

    def summed(a, b):
        part = lax.dot_general(a, b, (((0,), (0,)), ((), ())), preferred_element_type=F32)
        return lax.psum_scatter(part, "grp", scatter_dimension=0, tiled=True)

    grad_second = summed(dout, agg_second)
    dagg = nt(dout, w_second).astype(BF16)
    back = lax.dot_general(adj, dagg, (((0,), (0,)), ((), ())), preferred_element_type=F32)
    sig = jax.nn.sigmoid(pre)
    dpre = (maskf * back * sig * (1.0 + pre * (1.0 - sig))).astype(BF16)
    grad_first = summed(dpre, agg_first)
    return (output.reshape(1, rows, width), grad_first, grad_second)


def solution(mesh):
    n = mesh.shape["grp"]

    def body(*args):
        rows = args[4].shape[1]
        return whole_body(*args) if n == GROUP and rows == LANES else split_body(*args)

    in_specs = (
        P(("parts", "grp"), None, None),
        P(("parts", "grp")),
        P(("parts", "grp"), None),
        P(("parts", "grp"), None),
        P(("parts", "grp"), None, None),
        P(("parts", "grp"), None, None),
        P(),
        P(),
    )
    out_specs = (
        P(("parts", "grp"), None, None),
        P(("parts", "grp"), None),
        P(("parts", "grp"), None),
    )
    return jax.shard_map(body, mesh=mesh, in_specs=in_specs, out_specs=out_specs, check_vma=False)
```

```python
import functools

import jax
import jax.numpy as jnp
from jax import lax
from jax.experimental import pallas as pl
from jax.experimental.pallas import tpu as pltpu
from jax.sharding import PartitionSpec as P

F32 = jnp.float32
BF16 = jnp.bfloat16
VMEM = pl.BlockSpec(memory_space=pltpu.VMEM)
HBM = pl.BlockSpec(memory_space=pltpu.HBM)
LANES = 128
META = 16
CHUNKS = 4
LIMIT = 24 * 2**20
SMALL = 8 * 2**20
Z2, Z1, Y, CORE = 8, 4, 2, 1
GROUP = 16
HINT = (0, 8 * 10**9)
SENT = ((0, CORE), (Y, Y | CORE)) + tuple(
    tuple(z | slot for slot in range(4)) for z in (Z1, Z2 | Z1, Z2)
)
HALF_A = ((0, Z2, Z1, Z1 | Z2), (Y, Y | Z2, Y | Z1, Y | Z1 | Z2))
HALF_B = ((0, Z2, Y, Y | Z2), (Z1, Z1 | Z2, Z1 | Y, Z1 | Y | Z2))


def nn(a, b):
    return jnp.dot(a, b, preferred_element_type=F32)


def nt(a, b):
    return lax.dot_general(a, b, (((1,), (1,)), ((), ())), preferred_element_type=F32)


def start_all(moves, sems):
    copies = [pltpu.make_async_copy(a, b, sems.at[i]) for i, (a, b) in enumerate(moves)]
    for copy in copies:
        copy.start()
    return copies


def pack_kernel(counts, owner, local, features, adjacency, piece, *scratch):
    count, own_by, own_at, feat, adj, sems = scratch
    own, slots, width = features.shape
    rows = adjacency.shape[1]
    held = own * slots
    copies = start_all(zip((features, adjacency, counts, owner, local), (feat, adj, count, own_by, own_at)), sems)
    slot = lax.broadcasted_iota(jnp.int32, (slots, LANES), 0)
    line = lax.broadcasted_iota(jnp.int32, (META, LANES), 0)
    pick = lax.broadcasted_iota(jnp.int32, (META, LANES), 1) // slots
    meta = jnp.zeros((META, LANES), jnp.int32)
    for copy in copies:
        copy.wait()
    for i in range(own):
        live = slot < count[i]
        for b in range(width // LANES):
            block = feat[i, :, b * LANES : (b + 1) * LANES]
            at = b * held + i * slots
            piece[at : at + slots, :] = jnp.where(live, block, jnp.zeros_like(block))
        meta = jnp.where(line == 1 + i, count[i], meta)
    for k in range(owner.shape[1]):
        meta = jnp.where((line == 0) & (pick == k), own_by[0, k] * own + own_at[0, k], meta)
    at = held * (width // LANES)
    piece[at : at + rows, :] = adj[0]
    piece[at + rows : at + rows + META, :] = meta.astype(F32).astype(BF16)


def columns_kernel(cotangent, w_second, *refs):
    outs, (cot, second, turned, back, sems) = refs[: len(SENT)], refs[len(SENT) :]
    width = w_second.shape[0]
    each = width // GROUP
    place = lax.axis_index("grp")
    spans = [slice(c * width // CHUNKS, (c + 1) * width // CHUNKS) for c in range(CHUNKS)]
    moves = [(cotangent, cot)] + [(w_second.at[span], second.at[span]) for span in spans]
    copies = start_all(moves, sems)
    copies[0].wait()
    turned[...] = cot[0].astype(F32).T.astype(BF16)
    for span, copy in zip(spans, copies[1:]):
        copy.wait()
        back[span, :] = nt(second[span, :], cot[0]).astype(BF16)
    for out, slots in zip(outs, SENT):
        for i, slot in enumerate(slots):
            span = pl.ds(pl.multiple_of((place ^ slot) * each, each), each)
            at = i * 2 * each
            out[at : at + each, :] = turned[span, :]
            out[at + each : at + 2 * each, :] = back[span, :]


def stack(out, at, *blocks):
    for block in blocks:
        out[at : at + block.shape[0], :] = block[...]
        at += block.shape[0]
    return at


def split_kernel(piece, came, columns_y, columns_z, half_a, half_b):
    cut = (half_a.shape[0] - columns_z.shape[0]) // 2
    stack(half_a, 0, piece.at[:cut], came.at[:cut], columns_z)
    stack(half_b, 0, piece.at[cut:], came.at[cut:], columns_y)


def join_kernel(half_a, came_a, half_b, came_b, out_a, out_b, both):
    size, last = out_b.shape[0] // 2, half_a.shape[0] - (both.shape[0] - out_b.shape[0]) // 2
    cut = half_a.shape[0] - last
    stack(out_a, 0, half_a.at[:cut], came_a.at[:cut], came_a.at[cut + last // 2 :])
    stack(out_b, 0, half_b.at[:size], came_b.at[:size])
    stack(both, 0, out_a.at[: 2 * cut], out_b)


def turn_kernel(one, two, out):
    half = out.shape[0] // 2
    stack(out, 0, one.at[half:], two.at[half:])


def block_of(slot, rows, own, came_a, came_b, far_a, one, two, turn):
    ref, at = {
        0: (own, 0),
        Y: (came_b, came_b.shape[0] - 2 * rows),
        Z1: (came_a, came_a.shape[0] - 4 * rows),
        Z1 | Y: (far_a, far_a.shape[0] - 2 * rows),
        Z2 | Z1: (one, 0),
        Z2: (two, 0),
        Z2 | Z1 | Y: (turn, 0),
        Z2 | Y: (turn, 2 * rows),
    }[slot - slot % 2]
    at += slot % 2 * rows
    return ref.at[at : at + rows]


def other_kernel(*refs):
    *refs, out = refs
    rows = out.shape[0] * 2 // GROUP
    stack(out, 0, *[block_of(slot, rows, *refs) for slot in range(1, GROUP, 2)])


def pair_kernel(far_a, far_b, columns, out):
    stack(out, 0, far_a.at[: out.shape[0] - far_b.shape[0] - columns.shape[0]], far_b, columns)


def place_of(slot):
    return slot // 2 + GROUP // 2 * (slot % 2)


def lay_out(arrays, held, cut, feat, adj, meta):
    rows = adj.shape[1]
    for ref, at, slots in arrays[:2]:
        for slot in slots:
            p = place_of(slot)
            for b in range(cut // held):
                feat[p * held : (p + 1) * held, b * LANES : (b + 1) * LANES] = ref[at : at + held, :]
                at += held
    for ref, at, slots in arrays[2:]:
        for slot in slots:
            p = place_of(slot)
            for b in range(cut // held, feat.shape[1] // LANES):
                feat[p * held : (p + 1) * held, b * LANES : (b + 1) * LANES] = ref[at : at + held, :]
                at += held
            adj[p] = ref[at : at + rows, :]
            at += rows
            meta[p] = ref[at : at + META, :]
            at += META


def spread_of(place, held, slots, adj, picks):
    line = lax.broadcasted_iota(jnp.int32, (held, LANES), 0)
    lane = lax.broadcasted_iota(jnp.int32, (1, LANES), 1) % slots
    owners = [None] * GROUP
    for slot in range(GROUP):
        owners[place_of(slot)] = place ^ slot
    code = jnp.concatenate([line + owner * held for owner in owners], axis=0)
    chosen = jnp.where(code == picks * slots + lane, 1.0, 0.0).astype(BF16)
    return nt(adj, chosen).astype(BF16)


def early_kernel(own, slots, cut, a, far_a, b, far_b, w_first, feat, lifted, spread, adj, meta, w_piece):
    held = own * slots
    rows = adj.shape[1]
    place = lax.axis_index("grp")
    arrays = list(zip((a, far_a, b, far_b), HALF_A + HALF_B))
    lay_out([(ref, 0, at) for ref, at in arrays], held, cut, feat, adj, meta)
    lifted[...] = nn(feat[...], w_first[...]).astype(BF16)
    for p in range(GROUP // 2):
        picks = meta[p, 0:1, :].astype(F32).astype(jnp.int32)
        spread[p * rows : (p + 1) * rows, :] = spread_of(place, held, slots, adj[p], picks)
    each = w_piece.shape[0]
    wide = max(each, LANES)
    per = wide // each
    start = pl.multiple_of((place // per) * wide, wide)
    block = w_first[:, pl.ds(start, wide)].astype(F32).T
    part = block[:each]
    for q in range(1, per):
        part = jnp.where(place % per == q, block[q * each : (q + 1) * each], part)
    w_piece[...] = part.astype(BF16)


def step_kernel(own, slots, cut, rest, core, pair, *refs):
    blocks, refs = refs[:7], refs[7:]
    early_feat, early_lifted, early_spread, early_adj, early_meta, w_piece = refs[:6]
    w_first, w_second, output, grad_first, grad_second = refs[6:11]
    hidden, spread, feat, adj, meta, dout, dpre, lifted = refs[11:]
    width = w_first.shape[0]
    held = own * slots
    rows = adj.shape[1]
    place = lax.axis_index("grp")
    first = GROUP // 2

    feat[: first * held, :] = early_feat[...]
    lifted[: first * held, :] = early_lifted[...]
    spread[: first * rows, :] = early_spread[...]
    adj[:first] = early_adj[...]
    meta[:first] = early_meta[...]
    arrays = []
    for size, start, halves in ((cut, 0, HALF_A), (rest, 4 * cut, HALF_B)):
        for ref, group in zip((core, pair), halves):
            arrays.append((ref, start, [slot | CORE for slot in group]))
    deep = 4 * (cut + rest)
    lay_out(arrays, held, cut, feat, adj, meta)
    metas = [meta[p].astype(F32) for p in range(GROUP)]
    picks = jnp.concatenate([m[0:1] for m in metas], axis=0).astype(jnp.int32)
    lane = lax.broadcasted_iota(jnp.int32, (GROUP, LANES), 1) % slots
    count = jnp.zeros((GROUP, LANES), jnp.int32)
    for slot in range(GROUP):
        for i in range(own):
            held_by = metas[place_of(slot)][1 + i : 2 + i].astype(jnp.int32)
            count = jnp.where(picks == (place ^ slot) * own + i, held_by, count)
    masks = (lane < count).astype(F32)

    late = slice(first * held, GROUP * held)
    lifted[late, :] = nn(feat[late, :], w_first[...]).astype(BF16)
    lifted_piece = nt(w_piece[...], feat[...]).astype(BF16)
    for p in range(first, GROUP):
        span = slice(p * rows, (p + 1) * rows)
        spread[span, :] = spread_of(place, held, slots, adj[p], picks[p : p + 1])
    step = min(width, 2 * LANES)
    for c in range(0, width, step):
        half = 0.5 * nn(spread[...], lifted[:, c : c + step])
        hidden[:, c : c + step] = (half + half * jnp.tanh(half)).astype(BF16)
    pre_piece = nt(lifted_piece, spread[...])
    live = jnp.broadcast_to(masks[0:1], (rows, LANES)).T[:, :1]
    agg = nn(adj[0], (hidden[:rows, :].astype(F32) * live).astype(BF16)).astype(BF16)
    output[0] = (nn(agg, w_second[...]) * live).astype(BF16)

    each = grad_first.shape[0]
    for slot in range(GROUP):
        p = place_of(slot)
        mask = masks[p : p + 1]
        span = slice(p * rows, (p + 1) * rows)
        if slot % 2:
            at = deep + slot // 2 * 2 * each
            source = pair[at : at + 2 * each, :]
        else:
            source = block_of(slot, 2 * each, *blocks)[...]
        back = nn((source.astype(F32) * mask).astype(BF16), adj[p]) * mask
        dout[:, span] = back[:each].astype(BF16)
        pre = pre_piece[:, span]
        sig = 0.5 + 0.5 * jnp.tanh(0.5 * pre)
        dpre[:, span] = (back[each:] * sig * (1.0 + pre * (1.0 - sig))).astype(BF16)
    grad_second[...] = nn(dout[...], hidden[...])
    moved = nn(dpre[...], spread[...])
    grad_first[...] = nn(moved.astype(BF16), feat[...])


def call(kernel, ins, outs, scratch=(), limit=SMALL, stay=False, flops=0):
    if stay:
        ins = [pltpu.with_memory_space_constraint(x, pltpu.HBM) for x in ins]
    return pl.pallas_call(
        kernel,
        out_shape=tuple(jax.ShapeDtypeStruct(*out) for out in outs),
        in_specs=[HBM if stay else VMEM] * len(ins),
        out_specs=(VMEM,) * len(outs),
        scratch_shapes=list(scratch),
        compiler_params=pltpu.CompilerParams(vmem_limit_bytes=limit),
        cost_estimate=pl.CostEstimate(flops=flops, bytes_accessed=0, transcendentals=0),
    )(*ins)


def whole_body(features, counts, pick_owner, pick_local, adjacency, cotangent, w_first, w_second):
    own, slots, width = features.shape
    rows = adjacency.shape[1]
    held = own * slots
    each = width // GROUP
    total = GROUP * held
    cut = held * (width // LANES * 3 // 4)
    rest = held * (width // LANES) + rows + META - cut
    half = GROUP // 2

    def swap(x, slot):
        return lax.ppermute(x, "grp", [(i, i ^ slot) for i in range(GROUP)])

    (piece,) = call(
        pack_kernel,
        (counts, pick_owner, pick_local, features, adjacency),
        [((cut + rest, LANES), BF16)],
        [pltpu.SMEM(x.shape, jnp.int32) for x in (counts, pick_owner, pick_local)]
        + [pltpu.VMEM(x.shape, BF16) for x in (features, adjacency)]
        + [pltpu.SemaphoreType.DMA((5,))],
        stay=True,
    )
    came = swap(piece, Z2)
    cotangent, _ = lax.optimization_barrier((cotangent, piece))
    own_columns, columns_y, columns_z, one, two = call(
        columns_kernel,
        (cotangent, w_second),
        [((len(x) * 2 * each, rows), BF16) for x in SENT],
        [pltpu.VMEM(x.shape, BF16) for x in (cotangent, w_second)]
        + [pltpu.VMEM((width, rows), BF16)] * 2
        + [pltpu.SemaphoreType.DMA((1 + CHUNKS,))],
        stay=True,
    )
    one, two = swap(one, Z2 | Z1), swap(two, Z2)
    a, b = call(
        split_kernel,
        (piece, came, columns_y, columns_z),
        [((2 * cut + 8 * each, LANES), BF16), ((2 * rest + 4 * each, LANES), BF16)],
    )
    came_a, came_b = swap(a, Z1), swap(b, Y)
    a, b, both = call(
        join_kernel,
        (a, came_a, b, came_b),
        [((4 * cut + 4 * each, LANES), BF16)] + [((4 * size, LANES), BF16) for size in (rest, cut + rest)],
        flops=HINT[0],
    )
    far_a, far_b, core = swap(a, Y), swap(b, Z1), swap(both, CORE)
    (turn,) = call(turn_kernel, (one, two), [((8 * each, rows), BF16)], flops=HINT[1])
    turn = swap(turn, Y)
    blocks = (own_columns, came_a, came_b, far_a, one, two, turn)
    (others,) = call(other_kernel, blocks, [((half * 2 * each, rows), BF16)])
    far_a, far_b, core = lax.optimization_barrier((far_a, far_b, core))
    (pair,) = call(
        pair_kernel,
        (far_a, far_b, others),
        [((4 * (cut + rest) + half * 2 * each, LANES), BF16)],
    )
    pair = swap(pair, CORE)
    early = call(
        functools.partial(early_kernel, own, slots, cut),
        (a, far_a, b, far_b, w_first),
        [
            ((total // 2, width), BF16),
            ((total // 2, width), BF16),
            ((half * rows, total), BF16),
            ((half, rows, rows), BF16),
            ((half, META, LANES), BF16),
            ((each, width), BF16),
        ],
        limit=LIMIT,
    )
    return call(
        functools.partial(step_kernel, own, slots, cut, rest),
        (core, pair, *blocks, *early, w_first, w_second),
        [((1, rows, width), BF16), ((each, width), F32), ((each, width), F32)],
        [
            pltpu.VMEM((GROUP * rows, width), BF16),
            pltpu.VMEM((GROUP * rows, total), BF16),
            pltpu.VMEM((total, width), BF16),
            pltpu.VMEM((GROUP, rows, rows), BF16),
            pltpu.VMEM((GROUP, META, LANES), BF16),
            pltpu.VMEM((each, GROUP * rows), BF16),
            pltpu.VMEM((each, GROUP * rows), BF16),
            pltpu.VMEM((total, width), BF16),
        ],
        LIMIT,
    )


def split_body(features, counts, pick_owner, pick_local, adjacency, cotangent, w_first, w_second):
    owners = pick_owner[0]
    picks = pick_local[0]
    width = w_first.shape[0]
    slots = features.shape[1]
    count_picks = owners.shape[0]
    wanted = owners * features.shape[0] + picks
    feat_piece = lax.all_gather(features, "grp", axis=0, tiled=True)
    count_piece = lax.all_gather(counts, "grp", axis=0, tiled=True)
    live = jnp.take(count_piece, wanted, axis=0)
    rows = count_picks * slots
    inputs = jnp.take(feat_piece, wanted, axis=0).reshape(rows, width)
    mask = (jnp.arange(slots)[None, :] < live[:, None]).reshape(rows, 1).astype(BF16)
    inputs = inputs * mask
    maskf = mask.astype(F32)
    adj = adjacency[0]
    agg_first = nn(adj, inputs).astype(BF16)
    pre = nn(agg_first, w_first)
    hidden = (maskf * jax.nn.silu(pre)).astype(BF16)
    agg_second = nn(adj, hidden).astype(BF16)
    output = (maskf * nn(agg_second, w_second)).astype(BF16)
    dout = cotangent[0] * mask

    def summed(a, b):
        part = lax.dot_general(a, b, (((0,), (0,)), ((), ())), preferred_element_type=F32)
        return lax.psum_scatter(part, "grp", scatter_dimension=0, tiled=True)

    grad_second = summed(dout, agg_second)
    dagg = nt(dout, w_second).astype(BF16)
    back = lax.dot_general(adj, dagg, (((0,), (0,)), ((), ())), preferred_element_type=F32)
    sig = jax.nn.sigmoid(pre)
    dpre = (maskf * back * sig * (1.0 + pre * (1.0 - sig))).astype(BF16)
    grad_first = summed(dpre, agg_first)
    return (output.reshape(1, rows, width), grad_first, grad_second)


def solution(mesh):
    n = mesh.shape["grp"]

    def body(*args):
        rows = args[4].shape[1]
        return whole_body(*args) if n == GROUP and rows == LANES else split_body(*args)

    in_specs = (
        P(("parts", "grp"), None, None),
        P(("parts", "grp")),
        P(("parts", "grp"), None),
        P(("parts", "grp"), None),
        P(("parts", "grp"), None, None),
        P(("parts", "grp"), None, None),
        P(),
        P(),
    )
    out_specs = (
        P(("parts", "grp"), None, None),
        P(("parts", "grp"), None),
        P(("parts", "grp"), None),
    )
    return jax.shard_map(body, mesh=mesh, in_specs=in_specs, out_specs=out_specs, check_vma=False)
```

```python
import functools

import jax
import jax.numpy as jnp
from jax import lax
from jax.experimental import pallas as pl
from jax.experimental.pallas import tpu as pltpu
from jax.sharding import PartitionSpec as P

F32 = jnp.float32
BF16 = jnp.bfloat16
VMEM = pl.BlockSpec(memory_space=pltpu.VMEM)
HBM = pl.BlockSpec(memory_space=pltpu.HBM)
LANES = 128
META = 16
CHUNKS = 4
LIMIT = 24 * 2**20
SMALL = 8 * 2**20
Z2, Z1, Y, CORE = 8, 4, 2, 1
GROUP = 16
HINT = (0, 8 * 10**9)
SENT = ((0, CORE), (Y, Y | CORE)) + tuple(
    tuple(z | slot for slot in range(4)) for z in (Z1, Z2 | Z1, Z2)
)
HALF_A = ((0, Z2, Z1, Z1 | Z2), (Y, Y | Z2, Y | Z1, Y | Z1 | Z2))
HALF_B = ((0, Z2, Y, Y | Z2), (Z1, Z1 | Z2, Z1 | Y, Z1 | Y | Z2))


def nn(a, b):
    return jnp.dot(a, b, preferred_element_type=F32)


def nt(a, b):
    return lax.dot_general(a, b, (((1,), (1,)), ((), ())), preferred_element_type=F32)


def start_all(moves, sems):
    copies = [pltpu.make_async_copy(a, b, sems.at[i]) for i, (a, b) in enumerate(moves)]
    for copy in copies:
        copy.start()
    return copies


def pack_kernel(counts, owner, local, features, adjacency, piece, *scratch):
    count, own_by, own_at, feat, adj, sems = scratch
    own, slots, width = features.shape
    rows = adjacency.shape[1]
    held = own * slots
    copies = start_all(zip((features, adjacency, counts, owner, local), (feat, adj, count, own_by, own_at)), sems)
    slot = lax.broadcasted_iota(jnp.int32, (slots, LANES), 0)
    line = lax.broadcasted_iota(jnp.int32, (META, LANES), 0)
    pick = lax.broadcasted_iota(jnp.int32, (META, LANES), 1) // slots
    meta = jnp.zeros((META, LANES), jnp.int32)
    for copy in copies:
        copy.wait()
    for i in range(own):
        live = slot < count[i]
        for b in range(width // LANES):
            block = feat[i, :, b * LANES : (b + 1) * LANES]
            at = b * held + i * slots
            piece[at : at + slots, :] = jnp.where(live, block, jnp.zeros_like(block))
        meta = jnp.where(line == 1 + i, count[i], meta)
    for k in range(owner.shape[1]):
        meta = jnp.where((line == 0) & (pick == k), own_by[0, k] * own + own_at[0, k], meta)
    at = held * (width // LANES)
    piece[at : at + rows, :] = adj[0]
    piece[at + rows : at + rows + META, :] = meta.astype(F32).astype(BF16)


def columns_kernel(cotangent, w_second, *refs):
    outs, (cot, second, turned, back, sems) = refs[: len(SENT)], refs[len(SENT) :]
    width = w_second.shape[0]
    each = width // GROUP
    place = lax.axis_index("grp")
    spans = [slice(c * width // CHUNKS, (c + 1) * width // CHUNKS) for c in range(CHUNKS)]
    moves = [(cotangent, cot)] + [(w_second.at[span], second.at[span]) for span in spans]
    copies = start_all(moves, sems)
    copies[0].wait()
    turned[...] = cot[0].astype(F32).T.astype(BF16)
    for span, copy in zip(spans, copies[1:]):
        copy.wait()
        back[span, :] = nt(second[span, :], cot[0]).astype(BF16)
    for out, slots in zip(outs, SENT):
        for i, slot in enumerate(slots):
            span = pl.ds(pl.multiple_of((place ^ slot) * each, each), each)
            at = i * 2 * each
            out[at : at + each, :] = turned[span, :]
            out[at + each : at + 2 * each, :] = back[span, :]


def stack(out, at, *blocks):
    for block in blocks:
        out[at : at + block.shape[0], :] = block[...]
        at += block.shape[0]
    return at


def split_kernel(piece, came, columns_y, columns_z, half_a, half_b):
    cut = (half_a.shape[0] - columns_z.shape[0]) // 2
    stack(half_a, 0, piece.at[:cut], came.at[:cut], columns_z)
    stack(half_b, 0, piece.at[cut:], came.at[cut:], columns_y)


def join_kernel(half_a, came_a, half_b, came_b, out_a, out_b, both):
    size, last = out_b.shape[0] // 2, half_a.shape[0] - (both.shape[0] - out_b.shape[0]) // 2
    cut = half_a.shape[0] - last
    stack(out_a, 0, half_a.at[:cut], came_a.at[:cut], came_a.at[cut + last // 2 :])
    stack(out_b, 0, half_b.at[:size], came_b.at[:size])
    stack(both, 0, out_a.at[: 2 * cut], out_b)


def turn_kernel(one, two, out):
    half = out.shape[0] // 2
    stack(out, 0, one.at[half:], two.at[half:])


def block_of(slot, rows, own, came_a, came_b, far_a, one, two, turn):
    ref, at = {
        0: (own, 0),
        Y: (came_b, came_b.shape[0] - 2 * rows),
        Z1: (came_a, came_a.shape[0] - 4 * rows),
        Z1 | Y: (far_a, far_a.shape[0] - 2 * rows),
        Z2 | Z1: (one, 0),
        Z2: (two, 0),
        Z2 | Z1 | Y: (turn, 0),
        Z2 | Y: (turn, 2 * rows),
    }[slot - slot % 2]
    at += slot % 2 * rows
    return ref.at[at : at + rows]


def other_kernel(*refs):
    *refs, out = refs
    rows = out.shape[0] * 2 // GROUP
    stack(out, 0, *[block_of(slot, rows, *refs) for slot in range(1, GROUP, 2)])


def pair_kernel(far_a, far_b, columns, out):
    stack(out, 0, far_a.at[: out.shape[0] - far_b.shape[0] - columns.shape[0]], far_b, columns)


def place_of(slot):
    return slot // 2 + GROUP // 2 * (slot % 2)


def lay_out(arrays, held, cut, feat, adj, meta):
    rows = adj.shape[1]
    for ref, at, slots in arrays[:2]:
        for slot in slots:
            p = place_of(slot)
            for b in range(cut // held):
                feat[p * held : (p + 1) * held, b * LANES : (b + 1) * LANES] = ref[at : at + held, :]
                at += held
    for ref, at, slots in arrays[2:]:
        for slot in slots:
            p = place_of(slot)
            for b in range(cut // held, feat.shape[1] // LANES):
                feat[p * held : (p + 1) * held, b * LANES : (b + 1) * LANES] = ref[at : at + held, :]
                at += held
            adj[p] = ref[at : at + rows, :]
            at += rows
            meta[p] = ref[at : at + META, :]
            at += META


def spread_of(place, held, slots, adj, picks):
    line = lax.broadcasted_iota(jnp.int32, (held, LANES), 0)
    lane = lax.broadcasted_iota(jnp.int32, (1, LANES), 1) % slots
    owners = [None] * GROUP
    for slot in range(GROUP):
        owners[place_of(slot)] = place ^ slot
    code = jnp.concatenate([line + owner * held for owner in owners], axis=0)
    chosen = jnp.where(code == picks * slots + lane, 1.0, 0.0).astype(BF16)
    return nt(adj, chosen).astype(BF16)


def early_kernel(own, slots, cut, a, far_a, b, far_b, w_first, feat, lifted, spread, adj, meta, w_piece):
    held = own * slots
    rows = adj.shape[1]
    place = lax.axis_index("grp")
    arrays = list(zip((a, far_a, b, far_b), HALF_A + HALF_B))
    lay_out([(ref, 0, at) for ref, at in arrays], held, cut, feat, adj, meta)
    lifted[...] = nn(feat[...], w_first[...]).astype(BF16)
    for p in range(GROUP // 2):
        picks = meta[p, 0:1, :].astype(F32).astype(jnp.int32)
        spread[p * rows : (p + 1) * rows, :] = spread_of(place, held, slots, adj[p], picks)
    each = w_piece.shape[0]
    wide = max(each, LANES)
    per = wide // each
    start = pl.multiple_of((place // per) * wide, wide)
    block = w_first[:, pl.ds(start, wide)].astype(F32).T
    part = block[:each]
    for q in range(1, per):
        part = jnp.where(place % per == q, block[q * each : (q + 1) * each], part)
    w_piece[...] = part.astype(BF16)


def step_kernel(own, slots, cut, rest, core, pair, *refs):
    blocks, refs = refs[:7], refs[7:]
    early_feat, early_lifted, early_spread, early_adj, early_meta, w_piece = refs[:6]
    w_first, w_second, output, grad_first, grad_second = refs[6:11]
    hidden, spread, feat, adj, meta, dout, dpre, lifted, result, grads, second, sems = refs[11:]
    width = w_first.shape[0]
    held = own * slots
    rows = adj.shape[1]
    place = lax.axis_index("grp")
    first = GROUP // 2

    feat[: first * held, :] = early_feat[...]
    lifted[: first * held, :] = early_lifted[...]
    spread[: first * rows, :] = early_spread[...]
    adj[:first] = early_adj[...]
    meta[:first] = early_meta[...]
    arrays = []
    for size, start, halves in ((cut, 0, HALF_A), (rest, 4 * cut, HALF_B)):
        for ref, group in zip((core, pair), halves):
            arrays.append((ref, start, [slot | CORE for slot in group]))
    deep = 4 * (cut + rest)
    lay_out(arrays, held, cut, feat, adj, meta)
    metas = [meta[p].astype(F32) for p in range(GROUP)]
    picks = jnp.concatenate([m[0:1] for m in metas], axis=0).astype(jnp.int32)
    lane = lax.broadcasted_iota(jnp.int32, (GROUP, LANES), 1) % slots
    count = jnp.zeros((GROUP, LANES), jnp.int32)
    for slot in range(GROUP):
        for i in range(own):
            held_by = metas[place_of(slot)][1 + i : 2 + i].astype(jnp.int32)
            count = jnp.where(picks == (place ^ slot) * own + i, held_by, count)
    masks = (lane < count).astype(F32)

    late = slice(first * held, GROUP * held)
    lifted[late, :] = nn(feat[late, :], w_first[...]).astype(BF16)
    for p in range(first, GROUP):
        span = slice(p * rows, (p + 1) * rows)
        spread[span, :] = spread_of(place, held, slots, adj[p], picks[p : p + 1])
    lifted_piece = nt(w_piece[...], feat[...]).astype(BF16)
    pre_piece = nt(lifted_piece, spread[...])
    each = grad_first.shape[0]
    for slot in range(GROUP):
        p = place_of(slot)
        mask = masks[p : p + 1]
        span = slice(p * rows, (p + 1) * rows)
        if slot % 2:
            at = deep + slot // 2 * 2 * each
            source = pair[at : at + 2 * each, :]
        else:
            source = block_of(slot, 2 * each, *blocks)[...]
        back = nn((source.astype(F32) * mask).astype(BF16), adj[p]) * mask
        dout[:, span] = back[:each].astype(BF16)
        pre = pre_piece[:, span]
        sig = 0.5 + 0.5 * jnp.tanh(0.5 * pre)
        dpre[:, span] = (back[each:] * sig * (1.0 + pre * (1.0 - sig))).astype(BF16)

    chunk = min(width, 2 * LANES)
    for c in range(0, width, chunk):
        span = slice(c, c + chunk)
        half = 0.5 * nn(spread[...], lifted[:, span])
        hidden[:, span] = (half + half * jnp.tanh(half)).astype(BF16)
        if c:
            done = slice(c - chunk, c)
            second[:, done] = nn(dout[...], hidden[:, done])
        else:
            moved = nn(dpre[...], spread[...])
            grads[...] = nn(moved.astype(BF16), feat[...])
            first_out = pltpu.make_async_copy(grads, grad_first, sems.at[0])
            first_out.start()
    live = jnp.broadcast_to(masks[0:1], (rows, LANES)).T[:, :1]
    agg = nn(adj[0], (hidden[:rows, :].astype(F32) * live).astype(BF16)).astype(BF16)
    result[0] = (nn(agg, w_second[...]) * live).astype(BF16)
    output_out = pltpu.make_async_copy(result, output, sems.at[1])
    output_out.start()
    second[:, span] = nn(dout[...], hidden[:, span])
    second_out = pltpu.make_async_copy(second, grad_second, sems.at[2])
    second_out.start()
    for copy in (first_out, output_out, second_out):
        copy.wait()


def call(kernel, ins, outs, scratch=(), limit=SMALL, stay=False, leave=False, flops=0):
    if stay:
        ins = [pltpu.with_memory_space_constraint(x, pltpu.HBM) for x in ins]
    return pl.pallas_call(
        kernel,
        out_shape=tuple(jax.ShapeDtypeStruct(*out) for out in outs),
        in_specs=[HBM if stay else VMEM] * len(ins),
        out_specs=(HBM if leave else VMEM,) * len(outs),
        scratch_shapes=list(scratch),
        compiler_params=pltpu.CompilerParams(vmem_limit_bytes=limit),
        cost_estimate=pl.CostEstimate(flops=flops, bytes_accessed=0, transcendentals=0),
    )(*ins)


def whole_body(features, counts, pick_owner, pick_local, adjacency, cotangent, w_first, w_second):
    own, slots, width = features.shape
    rows = adjacency.shape[1]
    held = own * slots
    each = width // GROUP
    total = GROUP * held
    cut = held * (width // LANES // 2)
    rest = held * (width // LANES) + rows + META - cut
    half = GROUP // 2

    def swap(x, slot):
        return lax.ppermute(x, "grp", [(i, i ^ slot) for i in range(GROUP)])

    (piece,) = call(
        pack_kernel,
        (counts, pick_owner, pick_local, features, adjacency),
        [((cut + rest, LANES), BF16)],
        [pltpu.SMEM(x.shape, jnp.int32) for x in (counts, pick_owner, pick_local)]
        + [pltpu.VMEM(x.shape, BF16) for x in (features, adjacency)]
        + [pltpu.SemaphoreType.DMA((5,))],
        stay=True,
    )
    came = swap(piece, Z2)
    cotangent, _ = lax.optimization_barrier((cotangent, piece))
    own_columns, columns_y, columns_z, one, two = call(
        columns_kernel,
        (cotangent, w_second),
        [((len(x) * 2 * each, rows), BF16) for x in SENT],
        [pltpu.VMEM(x.shape, BF16) for x in (cotangent, w_second)]
        + [pltpu.VMEM((width, rows), BF16)] * 2
        + [pltpu.SemaphoreType.DMA((1 + CHUNKS,))],
        stay=True,
    )
    one, two = swap(one, Z2 | Z1), swap(two, Z2)
    a, b = call(
        split_kernel,
        (piece, came, columns_y, columns_z),
        [((2 * cut + 8 * each, LANES), BF16), ((2 * rest + 4 * each, LANES), BF16)],
    )
    came_a, came_b = swap(a, Z1), swap(b, Y)
    a, b, both = call(
        join_kernel,
        (a, came_a, b, came_b),
        [((4 * cut + 4 * each, LANES), BF16)] + [((4 * size, LANES), BF16) for size in (rest, cut + rest)],
        flops=HINT[0],
    )
    far_b, far_a, core = swap(b, Z1), swap(a, Y), swap(both, CORE)
    (turn,) = call(turn_kernel, (one, two), [((8 * each, rows), BF16)], flops=HINT[1])
    turn = swap(turn, Y)
    blocks = (own_columns, came_a, came_b, far_a, one, two, turn)
    (others,) = call(other_kernel, blocks, [((half * 2 * each, rows), BF16)])
    far_a, far_b, core = lax.optimization_barrier((far_a, far_b, core))
    (pair,) = call(
        pair_kernel,
        (far_a, far_b, others),
        [((4 * (cut + rest) + half * 2 * each, LANES), BF16)],
    )
    pair = swap(pair, CORE)
    early = call(
        functools.partial(early_kernel, own, slots, cut),
        (a, far_a, b, far_b, w_first),
        [
            ((total // 2, width), BF16),
            ((total // 2, width), BF16),
            ((half * rows, total), BF16),
            ((half, rows, rows), BF16),
            ((half, META, LANES), BF16),
            ((each, width), BF16),
        ],
        limit=LIMIT,
    )
    return call(
        functools.partial(step_kernel, own, slots, cut, rest),
        (core, pair, *blocks, *early, w_first, w_second),
        [((1, rows, width), BF16), ((each, width), F32), ((each, width), F32)],
        [
            pltpu.VMEM((GROUP * rows, width), BF16),
            pltpu.VMEM((GROUP * rows, total), BF16),
            pltpu.VMEM((total, width), BF16),
            pltpu.VMEM((GROUP, rows, rows), BF16),
            pltpu.VMEM((GROUP, META, LANES), BF16),
            pltpu.VMEM((each, GROUP * rows), BF16),
            pltpu.VMEM((each, GROUP * rows), BF16),
            pltpu.VMEM((total, width), BF16),
            pltpu.VMEM((1, rows, width), BF16),
            pltpu.VMEM((each, width), F32),
            pltpu.VMEM((each, width), F32),
            pltpu.SemaphoreType.DMA((3,)),
        ],
        LIMIT,
        leave=True,
    )


def split_body(features, counts, pick_owner, pick_local, adjacency, cotangent, w_first, w_second):
    owners = pick_owner[0]
    picks = pick_local[0]
    width = w_first.shape[0]
    slots = features.shape[1]
    count_picks = owners.shape[0]
    wanted = owners * features.shape[0] + picks
    feat_piece = lax.all_gather(features, "grp", axis=0, tiled=True)
    count_piece = lax.all_gather(counts, "grp", axis=0, tiled=True)
    live = jnp.take(count_piece, wanted, axis=0)
    rows = count_picks * slots
    inputs = jnp.take(feat_piece, wanted, axis=0).reshape(rows, width)
    mask = (jnp.arange(slots)[None, :] < live[:, None]).reshape(rows, 1).astype(BF16)
    inputs = inputs * mask
    maskf = mask.astype(F32)
    adj = adjacency[0]
    agg_first = nn(adj, inputs).astype(BF16)
    pre = nn(agg_first, w_first)
    hidden = (maskf * jax.nn.silu(pre)).astype(BF16)
    agg_second = nn(adj, hidden).astype(BF16)
    output = (maskf * nn(agg_second, w_second)).astype(BF16)
    dout = cotangent[0] * mask

    def summed(a, b):
        part = lax.dot_general(a, b, (((0,), (0,)), ((), ())), preferred_element_type=F32)
        return lax.psum_scatter(part, "grp", scatter_dimension=0, tiled=True)

    grad_second = summed(dout, agg_second)
    dagg = nt(dout, w_second).astype(BF16)
    back = lax.dot_general(adj, dagg, (((0,), (0,)), ((), ())), preferred_element_type=F32)
    sig = jax.nn.sigmoid(pre)
    dpre = (maskf * back * sig * (1.0 + pre * (1.0 - sig))).astype(BF16)
    grad_first = summed(dpre, agg_first)
    return (output.reshape(1, rows, width), grad_first, grad_second)


def solution(mesh):
    n = mesh.shape["grp"]

    def body(*args):
        rows = args[4].shape[1]
        return whole_body(*args) if n == GROUP and rows == LANES else split_body(*args)

    in_specs = (
        P(("parts", "grp"), None, None),
        P(("parts", "grp")),
        P(("parts", "grp"), None),
        P(("parts", "grp"), None),
        P(("parts", "grp"), None, None),
        P(("parts", "grp"), None, None),
        P(),
        P(),
    )
    out_specs = (
        P(("parts", "grp"), None, None),
        P(("parts", "grp"), None),
        P(("parts", "grp"), None),
    )
    return jax.shard_map(body, mesh=mesh, in_specs=in_specs, out_specs=out_specs, check_vma=False)
```

```python
import functools

import jax
import jax.numpy as jnp
from jax import lax
from jax.experimental import pallas as pl
from jax.experimental.pallas import tpu as pltpu
from jax.sharding import PartitionSpec as P

F32 = jnp.float32
BF16 = jnp.bfloat16
VMEM = pl.BlockSpec(memory_space=pltpu.VMEM)
HBM = pl.BlockSpec(memory_space=pltpu.HBM)
LANES = 128
META = 16
CHUNKS = 4
LIMIT = 24 * 2**20
SMALL = 8 * 2**20
Z2, Z1, Y, CORE = 8, 4, 2, 1
GROUP = 16
HINT = (0, 8 * 10**9)
SENT = (
    ((0, CORE), (Y, Y | CORE), (Z1, Z1 | CORE, Z1 | Y, Z1 | Y | CORE))
    + tuple((z, z | CORE) for z in (Z2 | Z1, Z2))
    + tuple((z | Y, z | Y | CORE) for z in (Z2 | Z1, Z2))
)
HALF_A = ((0, Z2, Z1, Z1 | Z2), (Y, Y | Z2, Y | Z1, Y | Z1 | Z2))
HALF_B = ((0, Z2, Y, Y | Z2), (Z1, Z1 | Z2, Z1 | Y, Z1 | Y | Z2))


def nn(a, b):
    return jnp.dot(a, b, preferred_element_type=F32)


def nt(a, b):
    return lax.dot_general(a, b, (((1,), (1,)), ((), ())), preferred_element_type=F32)


def start_all(moves, sems):
    copies = [pltpu.make_async_copy(a, b, sems.at[i]) for i, (a, b) in enumerate(moves)]
    for copy in copies:
        copy.start()
    return copies


def pack_kernel(counts, owner, local, features, adjacency, piece, *scratch):
    count, own_by, own_at, feat, adj, sems = scratch
    own, slots, width = features.shape
    rows = adjacency.shape[1]
    held = own * slots
    copies = start_all(zip((features, adjacency, counts, owner, local), (feat, adj, count, own_by, own_at)), sems)
    slot = lax.broadcasted_iota(jnp.int32, (slots, LANES), 0)
    line = lax.broadcasted_iota(jnp.int32, (META, LANES), 0)
    pick = lax.broadcasted_iota(jnp.int32, (META, LANES), 1) // slots
    meta = jnp.zeros((META, LANES), jnp.int32)
    for copy in copies:
        copy.wait()
    for i in range(own):
        live = slot < count[i]
        for b in range(width // LANES):
            block = feat[i, :, b * LANES : (b + 1) * LANES]
            at = b * held + i * slots
            piece[at : at + slots, :] = jnp.where(live, block, jnp.zeros_like(block))
        meta = jnp.where(line == 1 + i, count[i], meta)
    for k in range(owner.shape[1]):
        meta = jnp.where((line == 0) & (pick == k), own_by[0, k] * own + own_at[0, k], meta)
    at = held * (width // LANES)
    piece[at : at + rows, :] = adj[0]
    piece[at + rows : at + rows + META, :] = meta.astype(F32).astype(BF16)


def columns_kernel(cotangent, w_second, *refs):
    outs, (cot, second, turned, back, sems) = refs[: len(SENT)], refs[len(SENT) :]
    width = w_second.shape[0]
    each = width // GROUP
    place = lax.axis_index("grp")
    spans = [slice(c * width // CHUNKS, (c + 1) * width // CHUNKS) for c in range(CHUNKS)]
    moves = [(cotangent, cot)] + [(w_second.at[span], second.at[span]) for span in spans]
    copies = start_all(moves, sems)
    copies[0].wait()
    turned[...] = cot[0].astype(F32).T.astype(BF16)
    for span, copy in zip(spans, copies[1:]):
        copy.wait()
        back[span, :] = nt(second[span, :], cot[0]).astype(BF16)
    for out, slots in zip(outs, SENT):
        for i, slot in enumerate(slots):
            span = pl.ds(pl.multiple_of((place ^ slot) * each, each), each)
            at = i * 2 * each
            out[at : at + each, :] = turned[span, :]
            out[at + each : at + 2 * each, :] = back[span, :]


def stack(out, at, *blocks):
    for block in blocks:
        out[at : at + block.shape[0], :] = block[...]
        at += block.shape[0]
    return at


def split_kernel(piece, came, columns_y, columns_z, *refs):
    near_one, near_two, across_one, across_two, half_a, half_b, one, two = refs
    stack(one, 0, near_one, across_one)
    stack(two, 0, near_two, across_two)
    cut = (half_a.shape[0] - columns_z.shape[0]) // 2
    stack(half_a, 0, piece.at[:cut], came.at[:cut], columns_z)
    stack(half_b, 0, piece.at[cut:], came.at[cut:], columns_y)


def join_kernel(half_a, came_a, half_b, came_b, out_a, out_b, both):
    size, last = out_b.shape[0] // 2, half_a.shape[0] - (both.shape[0] - out_b.shape[0]) // 2
    cut = half_a.shape[0] - last
    stack(out_a, 0, half_a.at[:cut], came_a.at[:cut], came_a.at[cut + last // 2 :])
    stack(out_b, 0, half_b.at[:size], came_b.at[:size])
    stack(both, 0, out_a.at[: 2 * cut], out_b)


def block_of(slot, rows, own, came_a, came_b, far_a, one, two):
    ref, at = {
        0: (own, 0),
        Y: (came_b, came_b.shape[0] - 2 * rows),
        Z1: (came_a, came_a.shape[0] - 4 * rows),
        Z1 | Y: (far_a, far_a.shape[0] - 2 * rows),
        Z2 | Z1: (one, 0),
        Z2: (two, 0),
        Z2 | Z1 | Y: (one, 2 * rows),
        Z2 | Y: (two, 2 * rows),
    }[slot - slot % 2]
    at += slot % 2 * rows
    return ref.at[at : at + rows]


def far_kernel(one, two, out):
    rows = out.shape[0] // 4
    odd = [slice(k * rows, (k + 1) * rows) for k in (1, 3)]
    stack(out, 0, *[ref.at[span] for ref in (two, one) for span in odd])


def other_kernel(own, came_a, came_b, far_a, late, out):
    rows = late.shape[0] // 4
    near = [block_of(slot, rows, own, came_a, came_b, far_a, None, None) for slot in range(1, Z2, 2)]
    stack(out, 0, *near, late)


def pair_kernel(far_a, far_b, columns, out):
    stack(out, 0, far_a.at[: out.shape[0] - far_b.shape[0] - columns.shape[0]], far_b, columns)


def place_of(slot):
    return slot // 2 + GROUP // 2 * (slot % 2)


def lay_out(arrays, held, cut, feat, adj, meta):
    rows = adj.shape[1]
    for ref, at, slots in arrays[:2]:
        for slot in slots:
            p = place_of(slot)
            for b in range(cut // held):
                feat[p * held : (p + 1) * held, b * LANES : (b + 1) * LANES] = ref[at : at + held, :]
                at += held
    for ref, at, slots in arrays[2:]:
        for slot in slots:
            p = place_of(slot)
            for b in range(cut // held, feat.shape[1] // LANES):
                feat[p * held : (p + 1) * held, b * LANES : (b + 1) * LANES] = ref[at : at + held, :]
                at += held
            adj[p] = ref[at : at + rows, :]
            at += rows
            meta[p] = ref[at : at + META, :]
            at += META


def spread_of(place, held, slots, adj, picks):
    line = lax.broadcasted_iota(jnp.int32, (held, LANES), 0)
    lane = lax.broadcasted_iota(jnp.int32, (1, LANES), 1) % slots
    owners = [None] * GROUP
    for slot in range(GROUP):
        owners[place_of(slot)] = place ^ slot
    code = jnp.concatenate([line + owner * held for owner in owners], axis=0)
    chosen = jnp.where(code == picks * slots + lane, 1.0, 0.0).astype(BF16)
    return nt(adj, chosen).astype(BF16)


def early_kernel(own, slots, cut, a, far_a, b, far_b, w_first, feat, lifted, spread, adj, meta, w_piece):
    held = own * slots
    rows = adj.shape[1]
    place = lax.axis_index("grp")
    arrays = list(zip((a, far_a, b, far_b), HALF_A + HALF_B))
    lay_out([(ref, 0, at) for ref, at in arrays], held, cut, feat, adj, meta)
    lifted[...] = nn(feat[...], w_first[...]).astype(BF16)
    for p in range(GROUP // 2):
        picks = meta[p, 0:1, :].astype(F32).astype(jnp.int32)
        spread[p * rows : (p + 1) * rows, :] = spread_of(place, held, slots, adj[p], picks)
    each = w_piece.shape[0]
    wide = max(each, LANES)
    per = wide // each
    start = pl.multiple_of((place // per) * wide, wide)
    block = w_first[:, pl.ds(start, wide)].astype(F32).T
    part = block[:each]
    for q in range(1, per):
        part = jnp.where(place % per == q, block[q * each : (q + 1) * each], part)
    w_piece[...] = part.astype(BF16)


def step_kernel(own, slots, cut, rest, core, pair, *refs):
    blocks, refs = refs[:6], refs[6:]
    early_feat, early_lifted, early_spread, early_adj, early_meta, w_piece = refs[:6]
    w_first, w_second, output, grad_first, grad_second = refs[6:11]
    hidden, spread, feat, adj, meta, dout, dpre, lifted, result, grads, second, sems = refs[11:]
    width = w_first.shape[0]
    held = own * slots
    rows = adj.shape[1]
    place = lax.axis_index("grp")
    first = GROUP // 2

    feat[: first * held, :] = early_feat[...]
    lifted[: first * held, :] = early_lifted[...]
    spread[: first * rows, :] = early_spread[...]
    adj[:first] = early_adj[...]
    meta[:first] = early_meta[...]
    arrays = []
    for size, start, halves in ((cut, 0, HALF_A), (rest, 4 * cut, HALF_B)):
        for ref, group in zip((core, pair), halves):
            arrays.append((ref, start, [slot | CORE for slot in group]))
    deep = 4 * (cut + rest)
    lay_out(arrays, held, cut, feat, adj, meta)
    metas = [meta[p].astype(F32) for p in range(GROUP)]
    picks = jnp.concatenate([m[0:1] for m in metas], axis=0).astype(jnp.int32)
    lane = lax.broadcasted_iota(jnp.int32, (GROUP, LANES), 1) % slots
    count = jnp.zeros((GROUP, LANES), jnp.int32)
    for slot in range(GROUP):
        for i in range(own):
            held_by = metas[place_of(slot)][1 + i : 2 + i].astype(jnp.int32)
            count = jnp.where(picks == (place ^ slot) * own + i, held_by, count)
    masks = (lane < count).astype(F32)

    late = slice(first * held, GROUP * held)
    lifted[late, :] = nn(feat[late, :], w_first[...]).astype(BF16)
    for p in range(first, GROUP):
        span = slice(p * rows, (p + 1) * rows)
        spread[span, :] = spread_of(place, held, slots, adj[p], picks[p : p + 1])
    lifted_piece = nt(w_piece[...], feat[...]).astype(BF16)
    pre_piece = nt(lifted_piece, spread[...])
    each = grad_first.shape[0]
    for slot in range(GROUP):
        p = place_of(slot)
        mask = masks[p : p + 1]
        span = slice(p * rows, (p + 1) * rows)
        if slot % 2:
            at = deep + slot // 2 * 2 * each
            source = pair[at : at + 2 * each, :]
        else:
            source = block_of(slot, 2 * each, *blocks)[...]
        back = nn((source.astype(F32) * mask).astype(BF16), adj[p]) * mask
        dout[:, span] = back[:each].astype(BF16)
        pre = pre_piece[:, span]
        sig = 0.5 + 0.5 * jnp.tanh(0.5 * pre)
        dpre[:, span] = (back[each:] * sig * (1.0 + pre * (1.0 - sig))).astype(BF16)

    chunk = min(width, 2 * LANES)
    for c in range(0, width, chunk):
        span = slice(c, c + chunk)
        half = 0.5 * nn(spread[...], lifted[:, span])
        hidden[:, span] = (half + half * jnp.tanh(half)).astype(BF16)
        if c:
            done = slice(c - chunk, c)
            second[:, done] = nn(dout[...], hidden[:, done])
        else:
            moved = nn(dpre[...], spread[...])
            grads[...] = nn(moved.astype(BF16), feat[...])
            first_out = pltpu.make_async_copy(grads, grad_first, sems.at[0])
            first_out.start()
    live = jnp.broadcast_to(masks[0:1], (rows, LANES)).T[:, :1]
    agg = nn(adj[0], (hidden[:rows, :].astype(F32) * live).astype(BF16)).astype(BF16)
    result[0] = (nn(agg, w_second[...]) * live).astype(BF16)
    output_out = pltpu.make_async_copy(result, output, sems.at[1])
    output_out.start()
    second[:, span] = nn(dout[...], hidden[:, span])
    second_out = pltpu.make_async_copy(second, grad_second, sems.at[2])
    second_out.start()
    for copy in (first_out, output_out, second_out):
        copy.wait()


def call(kernel, ins, outs, scratch=(), limit=SMALL, stay=False, leave=False, flops=0):
    if stay:
        ins = [pltpu.with_memory_space_constraint(x, pltpu.HBM) for x in ins]
    return pl.pallas_call(
        kernel,
        out_shape=tuple(jax.ShapeDtypeStruct(*out) for out in outs),
        in_specs=[HBM if stay else VMEM] * len(ins),
        out_specs=(HBM if leave else VMEM,) * len(outs),
        scratch_shapes=list(scratch),
        compiler_params=pltpu.CompilerParams(vmem_limit_bytes=limit),
        cost_estimate=pl.CostEstimate(flops=flops, bytes_accessed=0, transcendentals=0),
    )(*ins)


def whole_body(features, counts, pick_owner, pick_local, adjacency, cotangent, w_first, w_second):
    own, slots, width = features.shape
    rows = adjacency.shape[1]
    held = own * slots
    each = width // GROUP
    total = GROUP * held
    cut = held * (width // LANES // 2)
    rest = held * (width // LANES) + rows + META - cut
    half = GROUP // 2

    def swap(x, slot):
        return lax.ppermute(x, "grp", [(i, i ^ slot) for i in range(GROUP)])

    (piece,) = call(
        pack_kernel,
        (counts, pick_owner, pick_local, features, adjacency),
        [((cut + rest, LANES), BF16)],
        [pltpu.SMEM(x.shape, jnp.int32) for x in (counts, pick_owner, pick_local)]
        + [pltpu.VMEM(x.shape, BF16) for x in (features, adjacency)]
        + [pltpu.SemaphoreType.DMA((5,))],
        stay=True,
    )
    came = swap(piece, Z2)
    cotangent, _ = lax.optimization_barrier((cotangent, piece))
    own_columns, columns_y, columns_z, *parts = call(
        columns_kernel,
        (cotangent, w_second),
        [((len(x) * 2 * each, rows), BF16) for x in SENT],
        [pltpu.VMEM(x.shape, BF16) for x in (cotangent, w_second)]
        + [pltpu.VMEM((width, rows), BF16)] * 2
        + [pltpu.SemaphoreType.DMA((1 + CHUNKS,))],
        stay=True,
    )
    parts[2:] = [swap(x, Y) for x in parts[2:]]
    a, b, one, two = call(
        split_kernel,
        (piece, came, columns_y, columns_z, *parts),
        [((2 * cut + 8 * each, LANES), BF16), ((2 * rest + 4 * each, LANES), BF16)]
        + [((8 * each, rows), BF16)] * 2,
    )
    one, two = swap(one, Z2 | Z1), swap(two, Z2)
    came_a, came_b = swap(a, Z1), swap(b, Y)
    a, b, both = call(
        join_kernel,
        (a, came_a, b, came_b),
        [((4 * cut + 4 * each, LANES), BF16)] + [((4 * size, LANES), BF16) for size in (rest, cut + rest)],
        flops=HINT[0],
    )
    far_b, far_a, core = swap(b, Z1), swap(a, Y), swap(both, CORE)
    blocks = (own_columns, came_a, came_b, far_a, one, two)
    (late,) = call(far_kernel, (one, two), [((8 * each, rows), BF16)], flops=HINT[1])
    (others,) = call(other_kernel, (*blocks[:4], late), [((half * 2 * each, rows), BF16)])
    far_a, far_b, core = lax.optimization_barrier((far_a, far_b, core))
    (pair,) = call(
        pair_kernel,
        (far_a, far_b, others),
        [((4 * (cut + rest) + half * 2 * each, LANES), BF16)],
    )
    pair = swap(pair, CORE)
    early = call(
        functools.partial(early_kernel, own, slots, cut),
        (a, far_a, b, far_b, w_first),
        [
            ((total // 2, width), BF16),
            ((total // 2, width), BF16),
            ((half * rows, total), BF16),
            ((half, rows, rows), BF16),
            ((half, META, LANES), BF16),
            ((each, width), BF16),
        ],
        limit=LIMIT,
    )
    return call(
        functools.partial(step_kernel, own, slots, cut, rest),
        (core, pair, *blocks, *early, w_first, w_second),
        [((1, rows, width), BF16), ((each, width), F32), ((each, width), F32)],
        [
            pltpu.VMEM((GROUP * rows, width), BF16),
            pltpu.VMEM((GROUP * rows, total), BF16),
            pltpu.VMEM((total, width), BF16),
            pltpu.VMEM((GROUP, rows, rows), BF16),
            pltpu.VMEM((GROUP, META, LANES), BF16),
            pltpu.VMEM((each, GROUP * rows), BF16),
            pltpu.VMEM((each, GROUP * rows), BF16),
            pltpu.VMEM((total, width), BF16),
            pltpu.VMEM((1, rows, width), BF16),
            pltpu.VMEM((each, width), F32),
            pltpu.VMEM((each, width), F32),
            pltpu.SemaphoreType.DMA((3,)),
        ],
        LIMIT,
        leave=True,
    )


def split_body(features, counts, pick_owner, pick_local, adjacency, cotangent, w_first, w_second):
    owners = pick_owner[0]
    picks = pick_local[0]
    width = w_first.shape[0]
    slots = features.shape[1]
    count_picks = owners.shape[0]
    wanted = owners * features.shape[0] + picks
    feat_piece = lax.all_gather(features, "grp", axis=0, tiled=True)
    count_piece = lax.all_gather(counts, "grp", axis=0, tiled=True)
    live = jnp.take(count_piece, wanted, axis=0)
    rows = count_picks * slots
    inputs = jnp.take(feat_piece, wanted, axis=0).reshape(rows, width)
    mask = (jnp.arange(slots)[None, :] < live[:, None]).reshape(rows, 1).astype(BF16)
    inputs = inputs * mask
    maskf = mask.astype(F32)
    adj = adjacency[0]
    agg_first = nn(adj, inputs).astype(BF16)
    pre = nn(agg_first, w_first)
    hidden = (maskf * jax.nn.silu(pre)).astype(BF16)
    agg_second = nn(adj, hidden).astype(BF16)
    output = (maskf * nn(agg_second, w_second)).astype(BF16)
    dout = cotangent[0] * mask

    def summed(a, b):
        part = lax.dot_general(a, b, (((0,), (0,)), ((), ())), preferred_element_type=F32)
        return lax.psum_scatter(part, "grp", scatter_dimension=0, tiled=True)

    grad_second = summed(dout, agg_second)
    dagg = nt(dout, w_second).astype(BF16)
    back = lax.dot_general(adj, dagg, (((0,), (0,)), ((), ())), preferred_element_type=F32)
    sig = jax.nn.sigmoid(pre)
    dpre = (maskf * back * sig * (1.0 + pre * (1.0 - sig))).astype(BF16)
    grad_first = summed(dpre, agg_first)
    return (output.reshape(1, rows, width), grad_first, grad_second)


def solution(mesh):
    n = mesh.shape["grp"]

    def body(*args):
        rows = args[4].shape[1]
        return whole_body(*args) if n == GROUP and rows == LANES else split_body(*args)

    in_specs = (
        P(("parts", "grp"), None, None),
        P(("parts", "grp")),
        P(("parts", "grp"), None),
        P(("parts", "grp"), None),
        P(("parts", "grp"), None, None),
        P(("parts", "grp"), None, None),
        P(),
        P(),
    )
    out_specs = (
        P(("parts", "grp"), None, None),
        P(("parts", "grp"), None),
        P(("parts", "grp"), None),
    )
    return jax.shard_map(body, mesh=mesh, in_specs=in_specs, out_specs=out_specs, check_vma=False)
```

```python
import functools

import jax
import jax.numpy as jnp
from jax import lax
from jax.experimental import pallas as pl
from jax.experimental.pallas import tpu as pltpu
from jax.sharding import PartitionSpec as P

F32 = jnp.float32
BF16 = jnp.bfloat16
VMEM = pl.BlockSpec(memory_space=pltpu.VMEM)
HBM = pl.BlockSpec(memory_space=pltpu.HBM)
LANES = 128
META = 16
LIMIT = 24 * 2**20
SMALL = 8 * 2**20
Z2, Z1, Y, CORE = 8, 4, 2, 1
GROUP = 16
FAR = (Z2 | Z1, Z2, 0)
HALF_A = ((0, Z2, Z1, Z1 | Z2), (Y, Y | Z2, Y | Z1, Y | Z1 | Z2))
HALF_B = ((0, Z2, Y, Y | Z2), (Z1, Z1 | Z2, Z1 | Y, Z1 | Y | Z2))


def nn(a, b):
    return jnp.dot(a, b, preferred_element_type=F32)


def nt(a, b):
    return lax.dot_general(a, b, (((1,), (1,)), ((), ())), preferred_element_type=F32)


def start_all(moves, sems):
    copies = [pltpu.make_async_copy(a, b, sems.at[i]) for i, (a, b) in enumerate(moves)]
    for copy in copies:
        copy.start()
    return copies


def pack_kernel(counts, owner, local, features, adjacency, piece, *scratch):
    count, own_by, own_at, feat, adj, sems = scratch
    own, slots, width = features.shape
    rows = adjacency.shape[1]
    held = own * slots
    copies = start_all(zip((features, adjacency, counts, owner, local), (feat, adj, count, own_by, own_at)), sems)
    slot = lax.broadcasted_iota(jnp.int32, (slots, LANES), 0)
    line = lax.broadcasted_iota(jnp.int32, (META, LANES), 0)
    pick = lax.broadcasted_iota(jnp.int32, (META, LANES), 1) // slots
    meta = jnp.zeros((META, LANES), jnp.int32)
    for copy in copies:
        copy.wait()
    for i in range(own):
        live = slot < count[i]
        for b in range(width // LANES):
            block = feat[i, :, b * LANES : (b + 1) * LANES]
            at = b * held + i * slots
            piece[at : at + slots, :] = jnp.where(live, block, jnp.zeros_like(block))
        meta = jnp.where(line == 1 + i, count[i], meta)
    for k in range(owner.shape[1]):
        meta = jnp.where((line == 0) & (pick == k), own_by[0, k] * own + own_at[0, k], meta)
    at = held * (width // LANES)
    piece[at : at + rows, :] = adj[0]
    piece[at + rows : at + rows + META, :] = meta.astype(F32).astype(BF16)


def product_kernel(cotangent, w_second, near, across, turned, back):
    each = w_second.shape[0] // GROUP
    place = lax.axis_index("grp")
    cot = cotangent[0]
    turned[...] = cot.astype(F32).T.astype(BF16)
    back[...] = nt(w_second[...], cot).astype(BF16)
    for h, out in enumerate((near, across)):
        for i in range(out.shape[0] // (2 * each)):
            to = 4 * (i // 2) + 2 * h + i % 2
            span = pl.ds(pl.multiple_of((place ^ to) * each, each), each)
            at = i * 2 * each
            out[at : at + each, :] = turned[span, :]
            out[at + each : at + 2 * each, :] = back[span, :]


def stack(out, at, *blocks):
    for block in blocks:
        out[at : at + block.shape[0], :] = block[...]
        at += block.shape[0]
    return at


def split_kernel(piece, came, near, across, beside, half_b, *sent):
    cut = beside.shape[0] - sent[0].shape[0]
    stack(half_b, 0, piece.at[cut // 2 :], came.at[cut // 2 :])
    at = stack(beside, 0, piece.at[: cut // 2], came.at[: cut // 2])
    size = sent[0].shape[0] // 2
    for slot, (out, at) in {Z1: (beside, at), **{slot: (out, 0) for slot, out in zip(FAR, sent)}}.items():
        span = slice(slot // 4 * size, (slot // 4 + 1) * size)
        stack(out, at, near.at[span], across.at[span])


def join_kernel(beside, came, half_b, came_b, out_a, out_b, both):
    cut = out_a.shape[0] // 2
    stack(out_a, 0, beside.at[:cut], came.at[:cut])
    stack(out_b, 0, half_b, came_b)
    stack(both, 0, out_a, out_b)


def columns_kernel(came, *refs):
    *sent, out = refs
    size = sent[0].shape[0]
    blocks = dict(zip(FAR, sent))
    blocks[Z1] = came.at[came.shape[0] - size :]
    rows = size // 4
    at = 0
    for slot in range(0, GROUP, 4):
        for h in range(2):
            at = stack(out, at, blocks[slot].at[(2 * h + 1) * rows : (2 * h + 2) * rows])


def pair_kernel(far_a, far_b, columns, out):
    stack(out, 0, far_a, far_b, columns)


def place_of(slot):
    return slot // 2 + GROUP // 2 * (slot % 2)


def lay_out(arrays, held, cut, feat, adj, meta):
    rows = adj.shape[1]
    for ref, at, slots in arrays[:2]:
        for slot in slots:
            p = place_of(slot)
            for b in range(cut // held):
                feat[p * held : (p + 1) * held, b * LANES : (b + 1) * LANES] = ref[at : at + held, :]
                at += held
    for ref, at, slots in arrays[2:]:
        for slot in slots:
            p = place_of(slot)
            for b in range(cut // held, feat.shape[1] // LANES):
                feat[p * held : (p + 1) * held, b * LANES : (b + 1) * LANES] = ref[at : at + held, :]
                at += held
            adj[p] = ref[at : at + rows, :]
            at += rows
            meta[p] = ref[at : at + META, :]
            at += META


def spread_of(place, held, slots, adj, picks):
    line = lax.broadcasted_iota(jnp.int32, (held, LANES), 0)
    lane = lax.broadcasted_iota(jnp.int32, (1, LANES), 1) % slots
    owners = [None] * GROUP
    for slot in range(GROUP):
        owners[place_of(slot)] = place ^ slot
    code = jnp.concatenate([line + owner * held for owner in owners], axis=0)
    chosen = jnp.where(code == picks * slots + lane, 1.0, 0.0).astype(BF16)
    return nt(adj, chosen).astype(BF16)


def early_kernel(own, slots, cut, a, far_a, b, far_b, w_first, feat, lifted, spread, adj, meta, w_piece):
    held = own * slots
    rows = adj.shape[1]
    place = lax.axis_index("grp")
    arrays = list(zip((a, far_a, b, far_b), HALF_A + HALF_B))
    lay_out([(ref, 0, at) for ref, at in arrays], held, cut, feat, adj, meta)
    lifted[...] = nn(feat[...], w_first[...]).astype(BF16)
    for p in range(GROUP // 2):
        picks = meta[p, 0:1, :].astype(F32).astype(jnp.int32)
        spread[p * rows : (p + 1) * rows, :] = spread_of(place, held, slots, adj[p], picks)
    each = w_piece.shape[0]
    wide = max(each, LANES)
    per = wide // each
    start = pl.multiple_of((place // per) * wide, wide)
    block = w_first[:, pl.ds(start, wide)].astype(F32).T
    part = block[:each]
    for q in range(1, per):
        part = jnp.where(place % per == q, block[q * each : (q + 1) * each], part)
    w_piece[...] = part.astype(BF16)


def step_kernel(own, slots, cut, rest, core, pair, came, *refs):
    sent, refs = dict(zip(FAR, refs)), refs[len(FAR) :]
    early_feat, early_lifted, early_spread, early_adj, early_meta, w_piece = refs[:6]
    w_first, w_second, output, grad_first, grad_second = refs[6:11]
    hidden, spread, feat, adj, meta, dout, dpre, lifted, result, grads, second, sems = refs[11:]
    width = w_first.shape[0]
    held = own * slots
    rows = adj.shape[1]
    place = lax.axis_index("grp")
    first = GROUP // 2

    feat[: first * held, :] = early_feat[...]
    lifted[: first * held, :] = early_lifted[...]
    spread[: first * rows, :] = early_spread[...]
    adj[:first] = early_adj[...]
    meta[:first] = early_meta[...]
    arrays = []
    for size, start, halves in ((cut, 0, HALF_A), (rest, 4 * cut, HALF_B)):
        for ref, group in zip((core, pair), halves):
            arrays.append((ref, start, [slot | CORE for slot in group]))
    deep = 4 * (cut + rest)
    lay_out(arrays, held, cut, feat, adj, meta)
    metas = [meta[p].astype(F32) for p in range(GROUP)]
    picks = jnp.concatenate([m[0:1] for m in metas], axis=0).astype(jnp.int32)
    lane = lax.broadcasted_iota(jnp.int32, (GROUP, LANES), 1) % slots
    count = jnp.zeros((GROUP, LANES), jnp.int32)
    for slot in range(GROUP):
        for i in range(own):
            held_by = metas[place_of(slot)][1 + i : 2 + i].astype(jnp.int32)
            count = jnp.where(picks == (place ^ slot) * own + i, held_by, count)
    masks = (lane < count).astype(F32)

    late = slice(first * held, GROUP * held)
    lifted[late, :] = nn(feat[late, :], w_first[...]).astype(BF16)
    for p in range(first, GROUP):
        span = slice(p * rows, (p + 1) * rows)
        spread[span, :] = spread_of(place, held, slots, adj[p], picks[p : p + 1])
    lifted_piece = nt(w_piece[...], feat[...]).astype(BF16)
    pre_piece = nt(lifted_piece, spread[...])
    each = grad_first.shape[0]
    size = sent[0].shape[0]
    sent[Z1] = came.at[came.shape[0] - size :]
    for slot in range(GROUP):
        p = place_of(slot)
        mask = masks[p : p + 1]
        span = slice(p * rows, (p + 1) * rows)
        if slot % 2:
            at = deep + slot // 2 * 2 * each
            source = pair[at : at + 2 * each, :]
        else:
            at = slot // 2 % 2 * size // 2
            source = sent[slot - slot % 4][at : at + 2 * each, :]
        back = nn((source.astype(F32) * mask).astype(BF16), adj[p]) * mask
        dout[:, span] = back[:each].astype(BF16)
        pre = pre_piece[:, span]
        sig = 0.5 + 0.5 * jnp.tanh(0.5 * pre)
        dpre[:, span] = (back[each:] * sig * (1.0 + pre * (1.0 - sig))).astype(BF16)

    chunk = min(width, 2 * LANES)
    for c in range(0, width, chunk):
        span = slice(c, c + chunk)
        half = 0.5 * nn(spread[...], lifted[:, span])
        hidden[:, span] = (half + half * jnp.tanh(half)).astype(BF16)
        if c:
            done = slice(c - chunk, c)
            second[:, done] = nn(dout[...], hidden[:, done])
        else:
            moved = nn(dpre[...], spread[...])
            grads[...] = nn(moved.astype(BF16), feat[...])
            first_out = pltpu.make_async_copy(grads, grad_first, sems.at[0])
            first_out.start()
    live = jnp.broadcast_to(masks[0:1], (rows, LANES)).T[:, :1]
    agg = nn(adj[0], (hidden[:rows, :].astype(F32) * live).astype(BF16)).astype(BF16)
    result[0] = (nn(agg, w_second[...]) * live).astype(BF16)
    output_out = pltpu.make_async_copy(result, output, sems.at[1])
    output_out.start()
    second[:, span] = nn(dout[...], hidden[:, span])
    second_out = pltpu.make_async_copy(second, grad_second, sems.at[2])
    second_out.start()
    for copy in (first_out, output_out, second_out):
        copy.wait()


def call(kernel, ins, outs, scratch=(), limit=SMALL, stay=False, leave=False, flops=0):
    if stay:
        ins = [pltpu.with_memory_space_constraint(x, pltpu.HBM) for x in ins]
    return pl.pallas_call(
        kernel,
        out_shape=tuple(jax.ShapeDtypeStruct(*out) for out in outs),
        in_specs=[HBM if stay else VMEM] * len(ins),
        out_specs=(HBM if leave else VMEM,) * len(outs),
        scratch_shapes=list(scratch),
        compiler_params=pltpu.CompilerParams(vmem_limit_bytes=limit),
        cost_estimate=pl.CostEstimate(flops=flops, bytes_accessed=0, transcendentals=0),
    )(*ins)


def whole_body(features, counts, pick_owner, pick_local, adjacency, cotangent, w_first, w_second):
    own, slots, width = features.shape
    rows = adjacency.shape[1]
    held = own * slots
    each = width // GROUP
    total = GROUP * held
    cut = held * (width // LANES * 3 // 4)
    rest = held * (width // LANES) + rows + META - cut
    half = GROUP // 2

    def swap(x, slot):
        return lax.ppermute(x, "grp", [(i, i ^ slot) for i in range(GROUP)])

    (piece,) = call(
        pack_kernel,
        (counts, pick_owner, pick_local, features, adjacency),
        [((cut + rest, LANES), BF16)],
        [pltpu.SMEM(x.shape, jnp.int32) for x in (counts, pick_owner, pick_local)]
        + [pltpu.VMEM(x.shape, BF16) for x in (features, adjacency)]
        + [pltpu.SemaphoreType.DMA((5,))],
        stay=True,
        flops=10**10,
    )
    cotangent, _ = lax.optimization_barrier((cotangent, piece))
    near, across = call(
        product_kernel,
        (cotangent, w_second),
        [((GROUP * each, rows), BF16)] * 2,
        [pltpu.VMEM((width, rows), BF16)] * 2,
    )
    came = swap(piece, Z2)
    across = swap(across, Y)
    beside, b, *sent = call(
        split_kernel,
        (piece, came, near, across),
        [((2 * cut + 8 * each, LANES), BF16), ((2 * rest, LANES), BF16)]
        + [((8 * each, rows), BF16)] * len(FAR),
    )
    came, came_b = swap(beside, Z1), swap(b, Y)
    sent = [swap(x, slot) if slot else x for x, slot in zip(sent, FAR)]
    a, b, both = call(
        join_kernel,
        (beside, came, b, came_b),
        [((4 * size, LANES), BF16) for size in (cut, rest, cut + rest)],
    )
    far_a, far_b, core = swap(a, Y), swap(b, Z1), swap(both, CORE)
    (columns,) = call(
        columns_kernel, (came, *sent), [((half * 2 * each, rows), BF16)], flops=8 * 10**9
    )
    far_a, far_b, core = lax.optimization_barrier((far_a, far_b, core))
    (pair,) = call(
        pair_kernel,
        (far_a, far_b, columns),
        [((4 * (cut + rest) + half * 2 * each, LANES), BF16)],
    )
    pair = swap(pair, CORE)
    early = call(
        functools.partial(early_kernel, own, slots, cut),
        (a, far_a, b, far_b, w_first),
        [
            ((total // 2, width), BF16),
            ((total // 2, width), BF16),
            ((half * rows, total), BF16),
            ((half, rows, rows), BF16),
            ((half, META, LANES), BF16),
            ((each, width), BF16),
        ],
        limit=LIMIT,
    )
    return call(
        functools.partial(step_kernel, own, slots, cut, rest),
        (core, pair, came, *sent, *early, w_first, w_second),
        [((1, rows, width), BF16), ((each, width), F32), ((each, width), F32)],
        [
            pltpu.VMEM((GROUP * rows, width), BF16),
            pltpu.VMEM((GROUP * rows, total), BF16),
            pltpu.VMEM((total, width), BF16),
            pltpu.VMEM((GROUP, rows, rows), BF16),
            pltpu.VMEM((GROUP, META, LANES), BF16),
            pltpu.VMEM((each, GROUP * rows), BF16),
            pltpu.VMEM((each, GROUP * rows), BF16),
            pltpu.VMEM((total, width), BF16),
            pltpu.VMEM((1, rows, width), BF16),
            pltpu.VMEM((each, width), F32),
            pltpu.VMEM((each, width), F32),
            pltpu.SemaphoreType.DMA((3,)),
        ],
        LIMIT,
        leave=True,
    )


def split_body(features, counts, pick_owner, pick_local, adjacency, cotangent, w_first, w_second):
    owners = pick_owner[0]
    picks = pick_local[0]
    width = w_first.shape[0]
    slots = features.shape[1]
    count_picks = owners.shape[0]
    wanted = owners * features.shape[0] + picks
    feat_piece = lax.all_gather(features, "grp", axis=0, tiled=True)
    count_piece = lax.all_gather(counts, "grp", axis=0, tiled=True)
    live = jnp.take(count_piece, wanted, axis=0)
    rows = count_picks * slots
    inputs = jnp.take(feat_piece, wanted, axis=0).reshape(rows, width)
    mask = (jnp.arange(slots)[None, :] < live[:, None]).reshape(rows, 1).astype(BF16)
    inputs = inputs * mask
    maskf = mask.astype(F32)
    adj = adjacency[0]
    agg_first = nn(adj, inputs).astype(BF16)
    pre = nn(agg_first, w_first)
    hidden = (maskf * jax.nn.silu(pre)).astype(BF16)
    agg_second = nn(adj, hidden).astype(BF16)
    output = (maskf * nn(agg_second, w_second)).astype(BF16)
    dout = cotangent[0] * mask

    def summed(a, b):
        part = lax.dot_general(a, b, (((0,), (0,)), ((), ())), preferred_element_type=F32)
        return lax.psum_scatter(part, "grp", scatter_dimension=0, tiled=True)

    grad_second = summed(dout, agg_second)
    dagg = nt(dout, w_second).astype(BF16)
    back = lax.dot_general(adj, dagg, (((0,), (0,)), ((), ())), preferred_element_type=F32)
    sig = jax.nn.sigmoid(pre)
    dpre = (maskf * back * sig * (1.0 + pre * (1.0 - sig))).astype(BF16)
    grad_first = summed(dpre, agg_first)
    return (output.reshape(1, rows, width), grad_first, grad_second)


def solution(mesh):
    n = mesh.shape["grp"]

    def body(*args):
        rows = args[4].shape[1]
        return whole_body(*args) if n == GROUP and rows == LANES else split_body(*args)

    in_specs = (
        P(("parts", "grp"), None, None),
        P(("parts", "grp")),
        P(("parts", "grp"), None),
        P(("parts", "grp"), None),
        P(("parts", "grp"), None, None),
        P(("parts", "grp"), None, None),
        P(),
        P(),
    )
    out_specs = (
        P(("parts", "grp"), None, None),
        P(("parts", "grp"), None),
        P(("parts", "grp"), None),
    )
    return jax.shard_map(body, mesh=mesh, in_specs=in_specs, out_specs=out_specs, check_vma=False)
```

```python
import functools

import jax
import jax.numpy as jnp
from jax import lax
from jax.experimental import pallas as pl
from jax.experimental.pallas import tpu as pltpu
from jax.sharding import PartitionSpec as P

F32 = jnp.float32
BF16 = jnp.bfloat16
VMEM = pl.BlockSpec(memory_space=pltpu.VMEM)
HBM = pl.BlockSpec(memory_space=pltpu.HBM)
LANES = 128
META = 16
LIMIT = 24 * 2**20
SMALL = 8 * 2**20
Z2, Z1, Y, CORE = 8, 4, 2, 1
GROUP = 16
FAR = (Z2 | Z1, Z2, 0)
HALF_A = ((0, Z2, Z1, Z1 | Z2), (Y, Y | Z2, Y | Z1, Y | Z1 | Z2))
HALF_B = ((0, Z2, Y, Y | Z2), (Z1, Z1 | Z2, Z1 | Y, Z1 | Y | Z2))


def nn(a, b):
    return jnp.dot(a, b, preferred_element_type=F32)


def nt(a, b):
    return lax.dot_general(a, b, (((1,), (1,)), ((), ())), preferred_element_type=F32)


def start_all(moves, sems):
    copies = [pltpu.make_async_copy(a, b, sems.at[i]) for i, (a, b) in enumerate(moves)]
    for copy in copies:
        copy.start()
    return copies


def pack_kernel(counts, owner, local, features, adjacency, piece, *scratch):
    count, own_by, own_at, feat, adj, sems = scratch
    own, slots, width = features.shape
    rows = adjacency.shape[1]
    held = own * slots
    copies = start_all(zip((features, adjacency, counts, owner, local), (feat, adj, count, own_by, own_at)), sems)
    slot = lax.broadcasted_iota(jnp.int32, (slots, LANES), 0)
    line = lax.broadcasted_iota(jnp.int32, (META, LANES), 0)
    pick = lax.broadcasted_iota(jnp.int32, (META, LANES), 1) // slots
    meta = jnp.zeros((META, LANES), jnp.int32)
    for copy in copies:
        copy.wait()
    for i in range(own):
        live = slot < count[i]
        for b in range(width // LANES):
            block = feat[i, :, b * LANES : (b + 1) * LANES]
            at = b * held + i * slots
            piece[at : at + slots, :] = jnp.where(live, block, jnp.zeros_like(block))
        meta = jnp.where(line == 1 + i, count[i], meta)
    for k in range(owner.shape[1]):
        meta = jnp.where((line == 0) & (pick == k), own_by[0, k] * own + own_at[0, k], meta)
    at = held * (width // LANES)
    piece[at : at + rows, :] = adj[0]
    piece[at + rows : at + rows + META, :] = meta.astype(F32).astype(BF16)


def product_kernel(cotangent, w_second, near, across, turned, back):
    each = w_second.shape[0] // GROUP
    place = lax.axis_index("grp")
    cot = cotangent[0]
    turned[...] = cot.astype(F32).T.astype(BF16)
    back[...] = nt(w_second[...], cot).astype(BF16)
    for h, out in enumerate((near, across)):
        for i in range(out.shape[0] // (2 * each)):
            to = 4 * (i // 2) + 2 * h + i % 2
            span = pl.ds(pl.multiple_of((place ^ to) * each, each), each)
            at = i * 2 * each
            out[at : at + each, :] = turned[span, :]
            out[at + each : at + 2 * each, :] = back[span, :]


def stack(out, at, *blocks):
    for block in blocks:
        out[at : at + block.shape[0], :] = block[...]
        at += block.shape[0]
    return at


def split_kernel(piece, came, near, across, beside, half_b, *sent):
    cut = beside.shape[0] - sent[0].shape[0]
    stack(half_b, 0, piece.at[cut // 2 :], came.at[cut // 2 :])
    at = stack(beside, 0, piece.at[: cut // 2], came.at[: cut // 2])
    size = sent[0].shape[0] // 2
    for slot, (out, at) in {Z1: (beside, at), **{slot: (out, 0) for slot, out in zip(FAR, sent)}}.items():
        span = slice(slot // 4 * size, (slot // 4 + 1) * size)
        stack(out, at, near.at[span], across.at[span])


def join_kernel(beside, came, half_b, came_b, out_a, out_b, both):
    cut = out_a.shape[0] // 2
    stack(out_a, 0, beside.at[:cut], came.at[:cut])
    stack(out_b, 0, half_b, came_b)
    stack(both, 0, out_a, out_b)


def columns_kernel(came, *refs):
    *sent, out = refs
    size = sent[0].shape[0]
    blocks = dict(zip(FAR, sent))
    blocks[Z1] = came.at[came.shape[0] - size :]
    rows = size // 4
    at = 0
    for slot in range(0, GROUP, 4):
        for h in range(2):
            at = stack(out, at, blocks[slot].at[(2 * h + 1) * rows : (2 * h + 2) * rows])


def pair_kernel(far_a, far_b, columns, out):
    stack(out, 0, far_a, far_b, columns)


def place_of(slot):
    return slot // 2 + GROUP // 2 * (slot % 2)


def lay_out(arrays, held, cut, feat, adj, meta):
    rows = adj.shape[1]
    for ref, at, slots in arrays[:2]:
        for slot in slots:
            p = place_of(slot)
            for b in range(cut // held):
                feat[p * held : (p + 1) * held, b * LANES : (b + 1) * LANES] = ref[at : at + held, :]
                at += held
    for ref, at, slots in arrays[2:]:
        for slot in slots:
            p = place_of(slot)
            for b in range(cut // held, feat.shape[1] // LANES):
                feat[p * held : (p + 1) * held, b * LANES : (b + 1) * LANES] = ref[at : at + held, :]
                at += held
            adj[p] = ref[at : at + rows, :]
            at += rows
            meta[p] = ref[at : at + META, :]
            at += META


def spread_of(place, held, slots, adj, picks):
    line = lax.broadcasted_iota(jnp.int32, (held, LANES), 0)
    lane = lax.broadcasted_iota(jnp.int32, (1, LANES), 1) % slots
    owners = [None] * GROUP
    for slot in range(GROUP):
        owners[place_of(slot)] = place ^ slot
    code = jnp.concatenate([line + owner * held for owner in owners], axis=0)
    chosen = jnp.where(code == picks * slots + lane, 1.0, 0.0).astype(BF16)
    return nt(adj, chosen).astype(BF16)


def early_kernel(own, slots, cut, a, far_a, b, far_b, w_first, feat, lifted, spread, adj, meta, w_piece):
    held = own * slots
    rows = adj.shape[1]
    place = lax.axis_index("grp")
    arrays = list(zip((a, far_a, b, far_b), HALF_A + HALF_B))
    lay_out([(ref, 0, at) for ref, at in arrays], held, cut, feat, adj, meta)
    lifted[...] = nn(feat[...], w_first[...]).astype(BF16)
    for p in range(GROUP // 2):
        picks = meta[p, 0:1, :].astype(F32).astype(jnp.int32)
        spread[p * rows : (p + 1) * rows, :] = spread_of(place, held, slots, adj[p], picks)
    each = w_piece.shape[0]
    wide = max(each, LANES)
    per = wide // each
    start = pl.multiple_of((place // per) * wide, wide)
    block = w_first[:, pl.ds(start, wide)].astype(F32).T
    part = block[:each]
    for q in range(1, per):
        part = jnp.where(place % per == q, block[q * each : (q + 1) * each], part)
    w_piece[...] = part.astype(BF16)


def step_kernel(own, slots, cut, rest, core, pair, came, *refs):
    sent, refs = dict(zip(FAR, refs)), refs[len(FAR) :]
    early_feat, early_lifted, early_spread, early_adj, early_meta, w_piece = refs[:6]
    w_first, w_second, output, grad_first, grad_second = refs[6:11]
    hidden, spread, feat, adj, meta, dout, dpre, lifted, result, grads, second, sems = refs[11:]
    width = w_first.shape[0]
    held = own * slots
    rows = adj.shape[1]
    place = lax.axis_index("grp")
    first = GROUP // 2

    feat[: first * held, :] = early_feat[...]
    lifted[: first * held, :] = early_lifted[...]
    spread[: first * rows, :] = early_spread[...]
    adj[:first] = early_adj[...]
    meta[:first] = early_meta[...]
    arrays = []
    for size, start, halves in ((cut, 0, HALF_A), (rest, 4 * cut, HALF_B)):
        for ref, group in zip((core, pair), halves):
            arrays.append((ref, start, [slot | CORE for slot in group]))
    deep = 4 * (cut + rest)
    lay_out(arrays, held, cut, feat, adj, meta)
    metas = [meta[p].astype(F32) for p in range(GROUP)]
    picks = jnp.concatenate([m[0:1] for m in metas], axis=0).astype(jnp.int32)
    lane = lax.broadcasted_iota(jnp.int32, (GROUP, LANES), 1) % slots
    count = jnp.zeros((GROUP, LANES), jnp.int32)
    for slot in range(GROUP):
        for i in range(own):
            held_by = metas[place_of(slot)][1 + i : 2 + i].astype(jnp.int32)
            count = jnp.where(picks == (place ^ slot) * own + i, held_by, count)
    masks = (lane < count).astype(F32)

    late = slice(first * held, GROUP * held)
    lifted[late, :] = nn(feat[late, :], w_first[...]).astype(BF16)
    for p in range(first, GROUP):
        span = slice(p * rows, (p + 1) * rows)
        spread[span, :] = spread_of(place, held, slots, adj[p], picks[p : p + 1])
    lifted_piece = nt(w_piece[...], feat[...]).astype(BF16)
    pre_piece = nt(lifted_piece, spread[...])
    each = grad_first.shape[0]
    size = sent[0].shape[0]
    sent[Z1] = came.at[came.shape[0] - size :]
    for slot in range(GROUP):
        p = place_of(slot)
        mask = masks[p : p + 1]
        span = slice(p * rows, (p + 1) * rows)
        if slot % 2:
            at = deep + slot // 2 * 2 * each
            source = pair[at : at + 2 * each, :]
        else:
            at = slot // 2 % 2 * size // 2
            source = sent[slot - slot % 4][at : at + 2 * each, :]
        back = nn((source.astype(F32) * mask).astype(BF16), adj[p]) * mask
        dout[:, span] = back[:each].astype(BF16)
        pre = pre_piece[:, span]
        sig = 0.5 + 0.5 * jnp.tanh(0.5 * pre)
        dpre[:, span] = (back[each:] * sig * (1.0 + pre * (1.0 - sig))).astype(BF16)

    chunk = min(width, 2 * LANES)
    for c in range(0, width, chunk):
        span = slice(c, c + chunk)
        half = 0.5 * nn(spread[...], lifted[:, span])
        hidden[:, span] = (half + half * jnp.tanh(half)).astype(BF16)
        if c:
            done = slice(c - chunk, c)
            second[:, done] = nn(dout[...], hidden[:, done])
        else:
            moved = nn(dpre[...], spread[...])
            grads[...] = nn(moved.astype(BF16), feat[...])
            first_out = pltpu.make_async_copy(grads, grad_first, sems.at[0])
            first_out.start()
    live = jnp.broadcast_to(masks[0:1], (rows, LANES)).T[:, :1]
    agg = nn(adj[0], (hidden[:rows, :].astype(F32) * live).astype(BF16)).astype(BF16)
    result[0] = (nn(agg, w_second[...]) * live).astype(BF16)
    output_out = pltpu.make_async_copy(result, output, sems.at[1])
    output_out.start()
    second[:, span] = nn(dout[...], hidden[:, span])
    second_out = pltpu.make_async_copy(second, grad_second, sems.at[2])
    second_out.start()
    for copy in (first_out, output_out, second_out):
        copy.wait()


def call(kernel, ins, outs, scratch=(), limit=SMALL, stay=False, leave=False, flops=0):
    if stay:
        ins = [pltpu.with_memory_space_constraint(x, pltpu.HBM) for x in ins]
    return pl.pallas_call(
        kernel,
        out_shape=tuple(jax.ShapeDtypeStruct(*out) for out in outs),
        in_specs=[HBM if stay else VMEM] * len(ins),
        out_specs=(HBM if leave else VMEM,) * len(outs),
        scratch_shapes=list(scratch),
        compiler_params=pltpu.CompilerParams(vmem_limit_bytes=limit),
        cost_estimate=pl.CostEstimate(flops=flops, bytes_accessed=0, transcendentals=0),
    )(*ins)


def whole_body(features, counts, pick_owner, pick_local, adjacency, cotangent, w_first, w_second):
    own, slots, width = features.shape
    rows = adjacency.shape[1]
    held = own * slots
    each = width // GROUP
    total = GROUP * held
    cut = held * (width // LANES)
    rest = held * (width // LANES) + rows + META - cut
    half = GROUP // 2

    def swap(x, slot):
        return lax.ppermute(x, "grp", [(i, i ^ slot) for i in range(GROUP)])

    (piece,) = call(
        pack_kernel,
        (counts, pick_owner, pick_local, features, adjacency),
        [((cut + rest, LANES), BF16)],
        [pltpu.SMEM(x.shape, jnp.int32) for x in (counts, pick_owner, pick_local)]
        + [pltpu.VMEM(x.shape, BF16) for x in (features, adjacency)]
        + [pltpu.SemaphoreType.DMA((5,))],
        stay=True,
        flops=10**10,
    )
    cotangent, _ = lax.optimization_barrier((cotangent, piece))
    near, across = call(
        product_kernel,
        (cotangent, w_second),
        [((GROUP * each, rows), BF16)] * 2,
        [pltpu.VMEM((width, rows), BF16)] * 2,
    )
    came = swap(piece, Z2)
    across = swap(across, Y)
    beside, b, *sent = call(
        split_kernel,
        (piece, came, near, across),
        [((2 * cut + 8 * each, LANES), BF16), ((2 * rest, LANES), BF16)]
        + [((8 * each, rows), BF16)] * len(FAR),
    )
    came, came_b = swap(beside, Z1), swap(b, Y)
    sent = [swap(x, slot) if slot else x for x, slot in zip(sent, FAR)]
    a, b, both = call(
        join_kernel,
        (beside, came, b, came_b),
        [((4 * size, LANES), BF16) for size in (cut, rest, cut + rest)],
    )
    core, far_b, far_a = swap(both, CORE), swap(b, Z1), swap(a, Y)
    (columns,) = call(
        columns_kernel, (came, *sent), [((half * 2 * each, rows), BF16)], flops=8 * 10**9
    )
    far_a, far_b, core = lax.optimization_barrier((far_a, far_b, core))
    (pair,) = call(
        pair_kernel,
        (far_a, far_b, columns),
        [((4 * (cut + rest) + half * 2 * each, LANES), BF16)],
    )
    pair = swap(pair, CORE)
    early = call(
        functools.partial(early_kernel, own, slots, cut),
        (a, far_a, b, far_b, w_first),
        [
            ((total // 2, width), BF16),
            ((total // 2, width), BF16),
            ((half * rows, total), BF16),
            ((half, rows, rows), BF16),
            ((half, META, LANES), BF16),
            ((each, width), BF16),
        ],
        limit=LIMIT,
    )
    return call(
        functools.partial(step_kernel, own, slots, cut, rest),
        (core, pair, came, *sent, *early, w_first, w_second),
        [((1, rows, width), BF16), ((each, width), F32), ((each, width), F32)],
        [
            pltpu.VMEM((GROUP * rows, width), BF16),
            pltpu.VMEM((GROUP * rows, total), BF16),
            pltpu.VMEM((total, width), BF16),
            pltpu.VMEM((GROUP, rows, rows), BF16),
            pltpu.VMEM((GROUP, META, LANES), BF16),
            pltpu.VMEM((each, GROUP * rows), BF16),
            pltpu.VMEM((each, GROUP * rows), BF16),
            pltpu.VMEM((total, width), BF16),
            pltpu.VMEM((1, rows, width), BF16),
            pltpu.VMEM((each, width), F32),
            pltpu.VMEM((each, width), F32),
            pltpu.SemaphoreType.DMA((3,)),
        ],
        LIMIT,
        leave=True,
    )


def split_body(features, counts, pick_owner, pick_local, adjacency, cotangent, w_first, w_second):
    owners = pick_owner[0]
    picks = pick_local[0]
    width = w_first.shape[0]
    slots = features.shape[1]
    count_picks = owners.shape[0]
    wanted = owners * features.shape[0] + picks
    feat_piece = lax.all_gather(features, "grp", axis=0, tiled=True)
    count_piece = lax.all_gather(counts, "grp", axis=0, tiled=True)
    live = jnp.take(count_piece, wanted, axis=0)
    rows = count_picks * slots
    inputs = jnp.take(feat_piece, wanted, axis=0).reshape(rows, width)
    mask = (jnp.arange(slots)[None, :] < live[:, None]).reshape(rows, 1).astype(BF16)
    inputs = inputs * mask
    maskf = mask.astype(F32)
    adj = adjacency[0]
    agg_first = nn(adj, inputs).astype(BF16)
    pre = nn(agg_first, w_first)
    hidden = (maskf * jax.nn.silu(pre)).astype(BF16)
    agg_second = nn(adj, hidden).astype(BF16)
    output = (maskf * nn(agg_second, w_second)).astype(BF16)
    dout = cotangent[0] * mask

    def summed(a, b):
        part = lax.dot_general(a, b, (((0,), (0,)), ((), ())), preferred_element_type=F32)
        return lax.psum_scatter(part, "grp", scatter_dimension=0, tiled=True)

    grad_second = summed(dout, agg_second)
    dagg = nt(dout, w_second).astype(BF16)
    back = lax.dot_general(adj, dagg, (((0,), (0,)), ((), ())), preferred_element_type=F32)
    sig = jax.nn.sigmoid(pre)
    dpre = (maskf * back * sig * (1.0 + pre * (1.0 - sig))).astype(BF16)
    grad_first = summed(dpre, agg_first)
    return (output.reshape(1, rows, width), grad_first, grad_second)


def solution(mesh):
    n = mesh.shape["grp"]

    def body(*args):
        rows = args[4].shape[1]
        return whole_body(*args) if n == GROUP and rows == LANES else split_body(*args)

    in_specs = (
        P(("parts", "grp"), None, None),
        P(("parts", "grp")),
        P(("parts", "grp"), None),
        P(("parts", "grp"), None),
        P(("parts", "grp"), None, None),
        P(("parts", "grp"), None, None),
        P(),
        P(),
    )
    out_specs = (
        P(("parts", "grp"), None, None),
        P(("parts", "grp"), None),
        P(("parts", "grp"), None),
    )
    return jax.shard_map(body, mesh=mesh, in_specs=in_specs, out_specs=out_specs, check_vma=False)
```

```python
import functools

import jax
import jax.numpy as jnp
from jax import lax
from jax.experimental import pallas as pl
from jax.experimental.pallas import tpu as pltpu
from jax.sharding import PartitionSpec as P

F32 = jnp.float32
BF16 = jnp.bfloat16
VMEM = pl.BlockSpec(memory_space=pltpu.VMEM)
HBM = pl.BlockSpec(memory_space=pltpu.HBM)
LANES = 128
META = 16
LIMIT = 24 * 2**20
SMALL = 8 * 2**20
Z2, Z1, Y, CORE = 8, 4, 2, 1
GROUP = 16
FAR = (Z2 | Z1, Z2)
NEAR = tuple(z | c for z in (0, *FAR) for c in (0, CORE))
ACROSS = tuple(Y | slot for slot in NEAR)
BESIDE = (Z1, Z1 | CORE, Z1 | Y, Z1 | Y | CORE)
HALF_A = ((0, Z2, Z1, Z1 | Z2), (Y, Y | Z2, Y | Z1, Y | Z1 | Z2))
HALF_B = ((0, Z2, Y, Y | Z2), (Z1, Z1 | Z2, Z1 | Y, Z1 | Y | Z2))


def nn(a, b):
    return jnp.dot(a, b, preferred_element_type=F32)


def nt(a, b):
    return lax.dot_general(a, b, (((1,), (1,)), ((), ())), preferred_element_type=F32)


def start_all(moves, sems):
    copies = [pltpu.make_async_copy(a, b, sems.at[i]) for i, (a, b) in enumerate(moves)]
    for copy in copies:
        copy.start()
    return copies


def pack_kernel(counts, owner, local, features, adjacency, piece, *scratch):
    count, own_by, own_at, feat, adj, sems = scratch
    own, slots, width = features.shape
    rows = adjacency.shape[1]
    held = own * slots
    copies = start_all(zip((features, adjacency, counts, owner, local), (feat, adj, count, own_by, own_at)), sems)
    slot = lax.broadcasted_iota(jnp.int32, (slots, LANES), 0)
    line = lax.broadcasted_iota(jnp.int32, (META, LANES), 0)
    pick = lax.broadcasted_iota(jnp.int32, (META, LANES), 1) // slots
    meta = jnp.zeros((META, LANES), jnp.int32)
    for copy in copies:
        copy.wait()
    for i in range(own):
        live = slot < count[i]
        for b in range(width // LANES):
            block = feat[i, :, b * LANES : (b + 1) * LANES]
            at = b * held + i * slots
            piece[at : at + slots, :] = jnp.where(live, block, jnp.zeros_like(block))
        meta = jnp.where(line == 1 + i, count[i], meta)
    for k in range(owner.shape[1]):
        meta = jnp.where((line == 0) & (pick == k), own_by[0, k] * own + own_at[0, k], meta)
    at = held * (width // LANES)
    piece[at : at + rows, :] = adj[0]
    piece[at + rows : at + rows + META, :] = meta.astype(F32).astype(BF16)


def product_kernel(cotangent, w_second, near, across, beside, turned, back):
    each = w_second.shape[0] // GROUP
    place = lax.axis_index("grp")
    cot = cotangent[0]
    turned[...] = cot.astype(F32).T.astype(BF16)
    back[...] = nt(w_second[...], cot).astype(BF16)
    for out, slots in ((near, NEAR), (across, ACROSS), (beside, BESIDE)):
        for i, slot in enumerate(slots):
            span = pl.ds(pl.multiple_of((place ^ slot) * each, each), each)
            at = i * 2 * each
            out[at : at + each, :] = turned[span, :]
            out[at + each : at + 2 * each, :] = back[span, :]


def stack(out, at, *blocks):
    for block in blocks:
        out[at : at + block.shape[0], :] = block[...]
        at += block.shape[0]
    return at


def split_kernel(piece, came, near, across, beside, half_a, turn, keep, *sent):
    cut = half_a.shape[0] // 2
    stack(half_a, 0, piece.at[:cut], came.at[:cut])
    two = beside.shape[0] // 2
    stack(turn, 0, piece.at[cut:], came.at[cut:], beside.at[two:])
    stack(keep, 0, near.at[:two], across.at[:two], beside.at[:two])
    for i, out in enumerate(sent, 1):
        span = slice(i * two, (i + 1) * two)
        stack(out, 0, near.at[span], across.at[span])


def join_kernel(half_a, came_a, turn, came_b, out_a, out_b, both):
    size = out_b.shape[0] // 2
    stack(out_a, 0, half_a, came_a)
    stack(out_b, 0, turn.at[:size], came_b.at[:size])
    stack(both, 0, out_a, out_b)


def block_of(slot, rows, keep, came, *sent):
    z, h, b = slot - slot % 4, slot // 2 % 2, slot % 2
    if z in FAR:
        ref, at = sent[FAR.index(z)], 2 * h + b
    elif z == 0 or h == 0:
        ref, at = keep, (4 if z else 2 * h) + b
    else:
        ref, at = came, b
    at *= rows
    if ref is came:
        at += came.shape[0] - 2 * rows
    return ref.at[at : at + rows]


def columns_kernel(*refs):
    *refs, out = refs
    rows = out.shape[0] * 2 // GROUP
    at = 0
    for slot in range(1, GROUP, 2):
        at = stack(out, at, block_of(slot, rows, *refs))


def pair_kernel(far_a, far_b, columns, out):
    stack(out, 0, far_a, far_b, columns)


def place_of(slot):
    return slot // 2 + GROUP // 2 * (slot % 2)


def lay_out(arrays, held, cut, feat, adj, meta):
    rows = adj.shape[1]
    for ref, at, slots in arrays[:2]:
        for slot in slots:
            p = place_of(slot)
            for b in range(cut // held):
                feat[p * held : (p + 1) * held, b * LANES : (b + 1) * LANES] = ref[at : at + held, :]
                at += held
    for ref, at, slots in arrays[2:]:
        for slot in slots:
            p = place_of(slot)
            for b in range(cut // held, feat.shape[1] // LANES):
                feat[p * held : (p + 1) * held, b * LANES : (b + 1) * LANES] = ref[at : at + held, :]
                at += held
            adj[p] = ref[at : at + rows, :]
            at += rows
            meta[p] = ref[at : at + META, :]
            at += META


def spread_of(place, held, slots, adj, picks):
    line = lax.broadcasted_iota(jnp.int32, (held, LANES), 0)
    lane = lax.broadcasted_iota(jnp.int32, (1, LANES), 1) % slots
    owners = [None] * GROUP
    for slot in range(GROUP):
        owners[place_of(slot)] = place ^ slot
    code = jnp.concatenate([line + owner * held for owner in owners], axis=0)
    chosen = jnp.where(code == picks * slots + lane, 1.0, 0.0).astype(BF16)
    return nt(adj, chosen).astype(BF16)


def early_kernel(own, slots, cut, a, far_a, b, far_b, w_first, feat, lifted, spread, adj, meta, w_piece):
    held = own * slots
    rows = adj.shape[1]
    place = lax.axis_index("grp")
    arrays = list(zip((a, far_a, b, far_b), HALF_A + HALF_B))
    lay_out([(ref, 0, at) for ref, at in arrays], held, cut, feat, adj, meta)
    lifted[...] = nn(feat[...], w_first[...]).astype(BF16)
    for p in range(GROUP // 2):
        picks = meta[p, 0:1, :].astype(F32).astype(jnp.int32)
        spread[p * rows : (p + 1) * rows, :] = spread_of(place, held, slots, adj[p], picks)
    each = w_piece.shape[0]
    wide = max(each, LANES)
    per = wide // each
    start = pl.multiple_of((place // per) * wide, wide)
    block = w_first[:, pl.ds(start, wide)].astype(F32).T
    part = block[:each]
    for q in range(1, per):
        part = jnp.where(place % per == q, block[q * each : (q + 1) * each], part)
    w_piece[...] = part.astype(BF16)


def step_kernel(own, slots, cut, rest, core, pair, *refs):
    blocks, refs = refs[: 2 + len(FAR)], refs[2 + len(FAR) :]
    early_feat, early_lifted, early_spread, early_adj, early_meta, w_piece = refs[:6]
    w_first, w_second, output, grad_first, grad_second = refs[6:11]
    hidden, spread, feat, adj, meta, dout, dpre, lifted, result, grads, second, sems = refs[11:]
    width = w_first.shape[0]
    held = own * slots
    rows = adj.shape[1]
    place = lax.axis_index("grp")
    first = GROUP // 2

    feat[: first * held, :] = early_feat[...]
    lifted[: first * held, :] = early_lifted[...]
    spread[: first * rows, :] = early_spread[...]
    adj[:first] = early_adj[...]
    meta[:first] = early_meta[...]
    arrays = []
    for size, start, halves in ((cut, 0, HALF_A), (rest, 4 * cut, HALF_B)):
        for ref, group in zip((core, pair), halves):
            arrays.append((ref, start, [slot | CORE for slot in group]))
    deep = 4 * (cut + rest)
    lay_out(arrays, held, cut, feat, adj, meta)
    metas = [meta[p].astype(F32) for p in range(GROUP)]
    picks = jnp.concatenate([m[0:1] for m in metas], axis=0).astype(jnp.int32)
    lane = lax.broadcasted_iota(jnp.int32, (GROUP, LANES), 1) % slots
    count = jnp.zeros((GROUP, LANES), jnp.int32)
    for slot in range(GROUP):
        for i in range(own):
            held_by = metas[place_of(slot)][1 + i : 2 + i].astype(jnp.int32)
            count = jnp.where(picks == (place ^ slot) * own + i, held_by, count)
    masks = (lane < count).astype(F32)

    late = slice(first * held, GROUP * held)
    lifted[late, :] = nn(feat[late, :], w_first[...]).astype(BF16)
    for p in range(first, GROUP):
        span = slice(p * rows, (p + 1) * rows)
        spread[span, :] = spread_of(place, held, slots, adj[p], picks[p : p + 1])
    lifted_piece = nt(w_piece[...], feat[...]).astype(BF16)
    pre_piece = nt(lifted_piece, spread[...])
    each = grad_first.shape[0]
    for slot in range(GROUP):
        p = place_of(slot)
        mask = masks[p : p + 1]
        span = slice(p * rows, (p + 1) * rows)
        if slot % 2:
            at = deep + slot // 2 * 2 * each
            source = pair[at : at + 2 * each, :]
        else:
            source = block_of(slot, 2 * each, *blocks)[...]
        back = nn((source.astype(F32) * mask).astype(BF16), adj[p]) * mask
        dout[:, span] = back[:each].astype(BF16)
        pre = pre_piece[:, span]
        sig = 0.5 + 0.5 * jnp.tanh(0.5 * pre)
        dpre[:, span] = (back[each:] * sig * (1.0 + pre * (1.0 - sig))).astype(BF16)

    chunk = min(width, 2 * LANES)
    for c in range(0, width, chunk):
        span = slice(c, c + chunk)
        half = 0.5 * nn(spread[...], lifted[:, span])
        hidden[:, span] = (half + half * jnp.tanh(half)).astype(BF16)
        if c:
            done = slice(c - chunk, c)
            second[:, done] = nn(dout[...], hidden[:, done])
        else:
            moved = nn(dpre[...], spread[...])
            grads[...] = nn(moved.astype(BF16), feat[...])
            first_out = pltpu.make_async_copy(grads, grad_first, sems.at[0])
            first_out.start()
    live = jnp.broadcast_to(masks[0:1], (rows, LANES)).T[:, :1]
    agg = nn(adj[0], (hidden[:rows, :].astype(F32) * live).astype(BF16)).astype(BF16)
    result[0] = (nn(agg, w_second[...]) * live).astype(BF16)
    output_out = pltpu.make_async_copy(result, output, sems.at[1])
    output_out.start()
    second[:, span] = nn(dout[...], hidden[:, span])
    second_out = pltpu.make_async_copy(second, grad_second, sems.at[2])
    second_out.start()
    for copy in (first_out, output_out, second_out):
        copy.wait()


def call(kernel, ins, outs, scratch=(), limit=SMALL, stay=False, leave=False, flops=0):
    if stay:
        ins = [pltpu.with_memory_space_constraint(x, pltpu.HBM) for x in ins]
    return pl.pallas_call(
        kernel,
        out_shape=tuple(jax.ShapeDtypeStruct(*out) for out in outs),
        in_specs=[HBM if stay else VMEM] * len(ins),
        out_specs=(HBM if leave else VMEM,) * len(outs),
        scratch_shapes=list(scratch),
        compiler_params=pltpu.CompilerParams(vmem_limit_bytes=limit),
        cost_estimate=pl.CostEstimate(flops=flops, bytes_accessed=0, transcendentals=0),
    )(*ins)


def whole_body(features, counts, pick_owner, pick_local, adjacency, cotangent, w_first, w_second):
    own, slots, width = features.shape
    rows = adjacency.shape[1]
    held = own * slots
    each = width // GROUP
    total = GROUP * held
    cut = held * (width // LANES)
    rest = held * (width // LANES) + rows + META - cut
    half = GROUP // 2

    def swap(x, slot):
        return lax.ppermute(x, "grp", [(i, i ^ slot) for i in range(GROUP)])

    (piece,) = call(
        pack_kernel,
        (counts, pick_owner, pick_local, features, adjacency),
        [((cut + rest, LANES), BF16)],
        [pltpu.SMEM(x.shape, jnp.int32) for x in (counts, pick_owner, pick_local)]
        + [pltpu.VMEM(x.shape, BF16) for x in (features, adjacency)]
        + [pltpu.SemaphoreType.DMA((5,))],
        stay=True,
        flops=10**10,
    )
    cotangent, _ = lax.optimization_barrier((cotangent, piece))
    near, across, beside = call(
        product_kernel,
        (cotangent, w_second),
        [((len(x) * 2 * each, rows), BF16) for x in (NEAR, ACROSS, BESIDE)],
        [pltpu.VMEM((width, rows), BF16)] * 2,
    )
    came, across, beside = swap(piece, Z2), swap(across, Y), swap(beside, Z1)
    a, turn, keep, *sent = call(
        split_kernel,
        (piece, came, near, across, beside),
        [((x, LANES), BF16) for x in (2 * cut, 2 * rest + 4 * each, 12 * each)]
        + [((8 * each, rows), BF16)] * len(FAR),
    )
    came_a, came_b = swap(a, Z1), swap(turn, Y)
    sent = [swap(x, slot) for x, slot in zip(sent, FAR)]
    a, b, both = call(
        join_kernel,
        (a, came_a, turn, came_b),
        [((4 * size, LANES), BF16) for size in (cut, rest, cut + rest)],
    )
    core, far_b, far_a = swap(both, CORE), swap(b, Z1), swap(a, Y)
    (columns,) = call(
        columns_kernel, (keep, came_b, *sent), [((half * 2 * each, rows), BF16)], flops=8 * 10**9
    )
    far_a, far_b, core = lax.optimization_barrier((far_a, far_b, core))
    (pair,) = call(
        pair_kernel,
        (far_a, far_b, columns),
        [((4 * (cut + rest) + half * 2 * each, LANES), BF16)],
    )
    pair = swap(pair, CORE)
    early = call(
        functools.partial(early_kernel, own, slots, cut),
        (a, far_a, b, far_b, w_first),
        [
            ((total // 2, width), BF16),
            ((total // 2, width), BF16),
            ((half * rows, total), BF16),
            ((half, rows, rows), BF16),
            ((half, META, LANES), BF16),
            ((each, width), BF16),
        ],
        limit=LIMIT,
    )
    return call(
        functools.partial(step_kernel, own, slots, cut, rest),
        (core, pair, keep, came_b, *sent, *early, w_first, w_second),
        [((1, rows, width), BF16), ((each, width), F32), ((each, width), F32)],
        [
            pltpu.VMEM((GROUP * rows, width), BF16),
            pltpu.VMEM((GROUP * rows, total), BF16),
            pltpu.VMEM((total, width), BF16),
            pltpu.VMEM((GROUP, rows, rows), BF16),
            pltpu.VMEM((GROUP, META, LANES), BF16),
            pltpu.VMEM((each, GROUP * rows), BF16),
            pltpu.VMEM((each, GROUP * rows), BF16),
            pltpu.VMEM((total, width), BF16),
            pltpu.VMEM((1, rows, width), BF16),
            pltpu.VMEM((each, width), F32),
            pltpu.VMEM((each, width), F32),
            pltpu.SemaphoreType.DMA((3,)),
        ],
        LIMIT,
        leave=True,
    )


def split_body(features, counts, pick_owner, pick_local, adjacency, cotangent, w_first, w_second):
    owners = pick_owner[0]
    picks = pick_local[0]
    width = w_first.shape[0]
    slots = features.shape[1]
    count_picks = owners.shape[0]
    wanted = owners * features.shape[0] + picks
    feat_piece = lax.all_gather(features, "grp", axis=0, tiled=True)
    count_piece = lax.all_gather(counts, "grp", axis=0, tiled=True)
    live = jnp.take(count_piece, wanted, axis=0)
    rows = count_picks * slots
    inputs = jnp.take(feat_piece, wanted, axis=0).reshape(rows, width)
    mask = (jnp.arange(slots)[None, :] < live[:, None]).reshape(rows, 1).astype(BF16)
    inputs = inputs * mask
    maskf = mask.astype(F32)
    adj = adjacency[0]
    agg_first = nn(adj, inputs).astype(BF16)
    pre = nn(agg_first, w_first)
    hidden = (maskf * jax.nn.silu(pre)).astype(BF16)
    agg_second = nn(adj, hidden).astype(BF16)
    output = (maskf * nn(agg_second, w_second)).astype(BF16)
    dout = cotangent[0] * mask

    def summed(a, b):
        part = lax.dot_general(a, b, (((0,), (0,)), ((), ())), preferred_element_type=F32)
        return lax.psum_scatter(part, "grp", scatter_dimension=0, tiled=True)

    grad_second = summed(dout, agg_second)
    dagg = nt(dout, w_second).astype(BF16)
    back = lax.dot_general(adj, dagg, (((0,), (0,)), ((), ())), preferred_element_type=F32)
    sig = jax.nn.sigmoid(pre)
    dpre = (maskf * back * sig * (1.0 + pre * (1.0 - sig))).astype(BF16)
    grad_first = summed(dpre, agg_first)
    return (output.reshape(1, rows, width), grad_first, grad_second)


def solution(mesh):
    n = mesh.shape["grp"]

    def body(*args):
        rows = args[4].shape[1]
        return whole_body(*args) if n == GROUP and rows == LANES else split_body(*args)

    in_specs = (
        P(("parts", "grp"), None, None),
        P(("parts", "grp")),
        P(("parts", "grp"), None),
        P(("parts", "grp"), None),
        P(("parts", "grp"), None, None),
        P(("parts", "grp"), None, None),
        P(),
        P(),
    )
    out_specs = (
        P(("parts", "grp"), None, None),
        P(("parts", "grp"), None),
        P(("parts", "grp"), None),
    )
    return jax.shard_map(body, mesh=mesh, in_specs=in_specs, out_specs=out_specs, check_vma=False)
```

```python
import functools

import jax
import jax.numpy as jnp
from jax import lax
from jax.experimental import pallas as pl
from jax.experimental.pallas import tpu as pltpu
from jax.sharding import PartitionSpec as P

F32 = jnp.float32
BF16 = jnp.bfloat16
VMEM = pl.BlockSpec(memory_space=pltpu.VMEM)
HBM = pl.BlockSpec(memory_space=pltpu.HBM)
LANES = 128
META = 16
LIMIT = 24 * 2**20
SMALL = 8 * 2**20
Z2, Z1, Y, CORE = 8, 4, 2, 1
GROUP = 16
FAR = (Z2 | Z1, Z2)
NEAR = tuple(z | c for z in (0, *FAR) for c in (0, CORE))
ACROSS = tuple(Y | slot for slot in NEAR)
BESIDE = (Z1, Z1 | CORE, Z1 | Y, Z1 | Y | CORE)
PARTS = (ACROSS[:3], ACROSS[3:], BESIDE[:2], BESIDE[2:])
HALF_A = ((0, Z2, Z1, Z1 | Z2), (Y, Y | Z2, Y | Z1, Y | Z1 | Z2))
HALF_B = ((0, Z2, Y, Y | Z2), (Z1, Z1 | Z2, Z1 | Y, Z1 | Y | Z2))


def nn(a, b):
    return jnp.dot(a, b, preferred_element_type=F32)


def nt(a, b):
    return lax.dot_general(a, b, (((1,), (1,)), ((), ())), preferred_element_type=F32)


def start_all(moves, sems):
    copies = [pltpu.make_async_copy(a, b, sems.at[i]) for i, (a, b) in enumerate(moves)]
    for copy in copies:
        copy.start()
    return copies


def pack_kernel(counts, owner, local, features, adjacency, piece, *scratch):
    count, own_by, own_at, feat, adj, sems = scratch
    own, slots, width = features.shape
    rows = adjacency.shape[1]
    held = own * slots
    copies = start_all(zip((features, adjacency, counts, owner, local), (feat, adj, count, own_by, own_at)), sems)
    slot = lax.broadcasted_iota(jnp.int32, (slots, LANES), 0)
    line = lax.broadcasted_iota(jnp.int32, (META, LANES), 0)
    pick = lax.broadcasted_iota(jnp.int32, (META, LANES), 1) // slots
    meta = jnp.zeros((META, LANES), jnp.int32)
    for copy in copies:
        copy.wait()
    for i in range(own):
        live = slot < count[i]
        for b in range(width // LANES):
            block = feat[i, :, b * LANES : (b + 1) * LANES]
            at = b * held + i * slots
            piece[at : at + slots, :] = jnp.where(live, block, jnp.zeros_like(block))
        meta = jnp.where(line == 1 + i, count[i], meta)
    for k in range(owner.shape[1]):
        meta = jnp.where((line == 0) & (pick == k), own_by[0, k] * own + own_at[0, k], meta)
    at = held * (width // LANES)
    piece[at : at + rows, :] = adj[0]
    piece[at + rows : at + rows + META, :] = meta.astype(F32).astype(BF16)


def product_kernel(cotangent, w_second, near, *refs):
    *parts, turned, back = refs
    each = w_second.shape[0] // GROUP
    place = lax.axis_index("grp")
    cot = cotangent[0]
    turned[...] = cot.astype(F32).T.astype(BF16)
    back[...] = nt(w_second[...], cot).astype(BF16)
    for out, slots in zip((near, *parts), (NEAR, *PARTS)):
        for i, slot in enumerate(slots):
            span = pl.ds(pl.multiple_of((place ^ slot) * each, each), each)
            at = i * 2 * each
            out[at : at + each, :] = turned[span, :]
            out[at + each : at + 2 * each, :] = back[span, :]


def stack(out, at, *blocks):
    for block in blocks:
        out[at : at + block.shape[0], :] = block[...]
        at += block.shape[0]
    return at


def split_kernel(piece, came, near, across, further, beside, turned, half_a, turn, keep, one, two):
    cut = half_a.shape[0] // 2
    stack(half_a, 0, piece.at[:cut], came.at[:cut])
    rows = near.shape[0] // len(NEAR)
    stack(turn, 0, piece.at[cut:], came.at[cut:], turned)
    stack(keep, 0, near.at[: 2 * rows], across.at[: 2 * rows], beside)
    stack(one, 0, near.at[2 * rows : 4 * rows], across.at[2 * rows :], further.at[:rows])
    stack(two, 0, near.at[4 * rows :], further.at[rows:])


def join_kernel(half_a, came_a, turn, came_b, out_a, out_b, both):
    size = out_b.shape[0] // 2
    stack(out_a, 0, half_a, came_a)
    stack(out_b, 0, turn.at[:size], came_b.at[:size])
    stack(both, 0, out_a, out_b)


def block_of(slot, rows, keep, came, *sent):
    z, h, b = slot - slot % 4, slot // 2 % 2, slot % 2
    if z in FAR:
        ref, at = sent[FAR.index(z)], 2 * h + b
    elif z == 0 or h == 0:
        ref, at = keep, (4 if z else 2 * h) + b
    else:
        ref, at = came, b
    at *= rows
    if ref is came:
        at += came.shape[0] - 2 * rows
    return ref.at[at : at + rows]


def columns_kernel(*refs):
    *refs, out = refs
    rows = out.shape[0] * 2 // GROUP
    at = 0
    for slot in range(1, GROUP, 2):
        at = stack(out, at, block_of(slot, rows, *refs))


def pair_kernel(far_a, far_b, columns, out):
    stack(out, 0, far_a, far_b, columns)


def place_of(slot):
    return slot // 2 + GROUP // 2 * (slot % 2)


def lay_out(arrays, held, cut, feat, adj, meta):
    rows = adj.shape[1]
    for ref, at, slots in arrays[:2]:
        for slot in slots:
            p = place_of(slot)
            for b in range(cut // held):
                feat[p * held : (p + 1) * held, b * LANES : (b + 1) * LANES] = ref[at : at + held, :]
                at += held
    for ref, at, slots in arrays[2:]:
        for slot in slots:
            p = place_of(slot)
            for b in range(cut // held, feat.shape[1] // LANES):
                feat[p * held : (p + 1) * held, b * LANES : (b + 1) * LANES] = ref[at : at + held, :]
                at += held
            adj[p] = ref[at : at + rows, :]
            at += rows
            meta[p] = ref[at : at + META, :]
            at += META


def spread_of(place, held, slots, adj, picks):
    line = lax.broadcasted_iota(jnp.int32, (held, LANES), 0)
    lane = lax.broadcasted_iota(jnp.int32, (1, LANES), 1) % slots
    owners = [None] * GROUP
    for slot in range(GROUP):
        owners[place_of(slot)] = place ^ slot
    code = jnp.concatenate([line + owner * held for owner in owners], axis=0)
    chosen = jnp.where(code == picks * slots + lane, 1.0, 0.0).astype(BF16)
    return nt(adj, chosen).astype(BF16)


def early_kernel(own, slots, cut, a, far_a, b, far_b, w_first, feat, lifted, spread, adj, meta, w_piece):
    held = own * slots
    rows = adj.shape[1]
    place = lax.axis_index("grp")
    arrays = list(zip((a, far_a, b, far_b), HALF_A + HALF_B))
    lay_out([(ref, 0, at) for ref, at in arrays], held, cut, feat, adj, meta)
    lifted[...] = nn(feat[...], w_first[...]).astype(BF16)
    for p in range(GROUP // 2):
        picks = meta[p, 0:1, :].astype(F32).astype(jnp.int32)
        spread[p * rows : (p + 1) * rows, :] = spread_of(place, held, slots, adj[p], picks)
    each = w_piece.shape[0]
    wide = max(each, LANES)
    per = wide // each
    start = pl.multiple_of((place // per) * wide, wide)
    block = w_first[:, pl.ds(start, wide)].astype(F32).T
    part = block[:each]
    for q in range(1, per):
        part = jnp.where(place % per == q, block[q * each : (q + 1) * each], part)
    w_piece[...] = part.astype(BF16)


def step_kernel(own, slots, cut, rest, core, pair, *refs):
    blocks, refs = refs[: 2 + len(FAR)], refs[2 + len(FAR) :]
    early_feat, early_lifted, early_spread, early_adj, early_meta, w_piece = refs[:6]
    w_first, w_second, output, grad_first, grad_second = refs[6:11]
    hidden, spread, feat, adj, meta, dout, dpre, lifted, result, grads, second, sems = refs[11:]
    width = w_first.shape[0]
    held = own * slots
    rows = adj.shape[1]
    place = lax.axis_index("grp")
    first = GROUP // 2

    feat[: first * held, :] = early_feat[...]
    lifted[: first * held, :] = early_lifted[...]
    spread[: first * rows, :] = early_spread[...]
    adj[:first] = early_adj[...]
    meta[:first] = early_meta[...]
    arrays = []
    for size, start, halves in ((cut, 0, HALF_A), (rest, 4 * cut, HALF_B)):
        for ref, group in zip((core, pair), halves):
            arrays.append((ref, start, [slot | CORE for slot in group]))
    deep = 4 * (cut + rest)
    lay_out(arrays, held, cut, feat, adj, meta)
    metas = [meta[p].astype(F32) for p in range(GROUP)]
    picks = jnp.concatenate([m[0:1] for m in metas], axis=0).astype(jnp.int32)
    lane = lax.broadcasted_iota(jnp.int32, (GROUP, LANES), 1) % slots
    count = jnp.zeros((GROUP, LANES), jnp.int32)
    for slot in range(GROUP):
        for i in range(own):
            held_by = metas[place_of(slot)][1 + i : 2 + i].astype(jnp.int32)
            count = jnp.where(picks == (place ^ slot) * own + i, held_by, count)
    masks = (lane < count).astype(F32)

    late = slice(first * held, GROUP * held)
    lifted[late, :] = nn(feat[late, :], w_first[...]).astype(BF16)
    for p in range(first, GROUP):
        span = slice(p * rows, (p + 1) * rows)
        spread[span, :] = spread_of(place, held, slots, adj[p], picks[p : p + 1])
    lifted_piece = nt(w_piece[...], feat[...]).astype(BF16)
    pre_piece = nt(lifted_piece, spread[...])
    each = grad_first.shape[0]
    for slot in range(GROUP):
        p = place_of(slot)
        mask = masks[p : p + 1]
        span = slice(p * rows, (p + 1) * rows)
        if slot % 2:
            at = deep + slot // 2 * 2 * each
            source = pair[at : at + 2 * each, :]
        else:
            source = block_of(slot, 2 * each, *blocks)[...]
        back = nn((source.astype(F32) * mask).astype(BF16), adj[p]) * mask
        dout[:, span] = back[:each].astype(BF16)
        pre = pre_piece[:, span]
        sig = 0.5 + 0.5 * jnp.tanh(0.5 * pre)
        dpre[:, span] = (back[each:] * sig * (1.0 + pre * (1.0 - sig))).astype(BF16)

    chunk = min(width, 2 * LANES)
    for c in range(0, width, chunk):
        span = slice(c, c + chunk)
        half = 0.5 * nn(spread[...], lifted[:, span])
        hidden[:, span] = (half + half * jnp.tanh(half)).astype(BF16)
        if c:
            done = slice(c - chunk, c)
            second[:, done] = nn(dout[...], hidden[:, done])
        else:
            moved = nn(dpre[...], spread[...])
            grads[...] = nn(moved.astype(BF16), feat[...])
            first_out = pltpu.make_async_copy(grads, grad_first, sems.at[0])
            first_out.start()
    live = jnp.broadcast_to(masks[0:1], (rows, LANES)).T[:, :1]
    agg = nn(adj[0], (hidden[:rows, :].astype(F32) * live).astype(BF16)).astype(BF16)
    result[0] = (nn(agg, w_second[...]) * live).astype(BF16)
    output_out = pltpu.make_async_copy(result, output, sems.at[1])
    output_out.start()
    second[:, span] = nn(dout[...], hidden[:, span])
    second_out = pltpu.make_async_copy(second, grad_second, sems.at[2])
    second_out.start()
    for copy in (first_out, output_out, second_out):
        copy.wait()


def call(kernel, ins, outs, scratch=(), limit=SMALL, stay=False, leave=False, flops=0):
    if stay:
        ins = [pltpu.with_memory_space_constraint(x, pltpu.HBM) for x in ins]
    return pl.pallas_call(
        kernel,
        out_shape=tuple(jax.ShapeDtypeStruct(*out) for out in outs),
        in_specs=[HBM if stay else VMEM] * len(ins),
        out_specs=(HBM if leave else VMEM,) * len(outs),
        scratch_shapes=list(scratch),
        compiler_params=pltpu.CompilerParams(vmem_limit_bytes=limit),
        cost_estimate=pl.CostEstimate(flops=flops, bytes_accessed=0, transcendentals=0),
    )(*ins)


def whole_body(features, counts, pick_owner, pick_local, adjacency, cotangent, w_first, w_second):
    own, slots, width = features.shape
    rows = adjacency.shape[1]
    held = own * slots
    each = width // GROUP
    total = GROUP * held
    cut = held * (width // LANES)
    rest = held * (width // LANES) + rows + META - cut
    half = GROUP // 2

    def swap(x, slot):
        return lax.ppermute(x, "grp", [(i, i ^ slot) for i in range(GROUP)])

    (piece,) = call(
        pack_kernel,
        (counts, pick_owner, pick_local, features, adjacency),
        [((cut + rest, LANES), BF16)],
        [pltpu.SMEM(x.shape, jnp.int32) for x in (counts, pick_owner, pick_local)]
        + [pltpu.VMEM(x.shape, BF16) for x in (features, adjacency)]
        + [pltpu.SemaphoreType.DMA((5,))],
        stay=True,
        flops=10**10,
    )
    cotangent, _ = lax.optimization_barrier((cotangent, piece))
    near, *columns = call(
        product_kernel,
        (cotangent, w_second),
        [((len(x) * 2 * each, rows), BF16) for x in (NEAR, *PARTS)],
        [pltpu.VMEM((width, rows), BF16)] * 2,
    )
    came = swap(piece, Z2)
    columns = [swap(x, slot) for x, slot in zip(columns, (Y, Y, Z1, Z1))]
    a, turn, keep, *sent = call(
        split_kernel,
        (piece, came, near, *columns),
        [((x, LANES), BF16) for x in (2 * cut, 2 * rest + 4 * each, 12 * each)]
        + [((8 * each, rows), BF16)] * len(FAR),
    )
    came_a, came_b = swap(a, Z1), swap(turn, Y)
    sent = [swap(x, slot) for x, slot in zip(sent, FAR)]
    a, b, both = call(
        join_kernel,
        (a, came_a, turn, came_b),
        [((4 * size, LANES), BF16) for size in (cut, rest, cut + rest)],
    )
    core, far_b, far_a = swap(both, CORE), swap(b, Z1), swap(a, Y)
    (columns,) = call(
        columns_kernel, (keep, came_b, *sent), [((half * 2 * each, rows), BF16)], flops=8 * 10**9
    )
    far_a, far_b, core = lax.optimization_barrier((far_a, far_b, core))
    (pair,) = call(
        pair_kernel,
        (far_a, far_b, columns),
        [((4 * (cut + rest) + half * 2 * each, LANES), BF16)],
    )
    pair = swap(pair, CORE)
    early = call(
        functools.partial(early_kernel, own, slots, cut),
        (a, far_a, b, far_b, w_first),
        [
            ((total // 2, width), BF16),
            ((total // 2, width), BF16),
            ((half * rows, total), BF16),
            ((half, rows, rows), BF16),
            ((half, META, LANES), BF16),
            ((each, width), BF16),
        ],
        limit=LIMIT,
    )
    return call(
        functools.partial(step_kernel, own, slots, cut, rest),
        (core, pair, keep, came_b, *sent, *early, w_first, w_second),
        [((1, rows, width), BF16), ((each, width), F32), ((each, width), F32)],
        [
            pltpu.VMEM((GROUP * rows, width), BF16),
            pltpu.VMEM((GROUP * rows, total), BF16),
            pltpu.VMEM((total, width), BF16),
            pltpu.VMEM((GROUP, rows, rows), BF16),
            pltpu.VMEM((GROUP, META, LANES), BF16),
            pltpu.VMEM((each, GROUP * rows), BF16),
            pltpu.VMEM((each, GROUP * rows), BF16),
            pltpu.VMEM((total, width), BF16),
            pltpu.VMEM((1, rows, width), BF16),
            pltpu.VMEM((each, width), F32),
            pltpu.VMEM((each, width), F32),
            pltpu.SemaphoreType.DMA((3,)),
        ],
        LIMIT,
        leave=True,
    )


def split_body(features, counts, pick_owner, pick_local, adjacency, cotangent, w_first, w_second):
    owners = pick_owner[0]
    picks = pick_local[0]
    width = w_first.shape[0]
    slots = features.shape[1]
    count_picks = owners.shape[0]
    wanted = owners * features.shape[0] + picks
    feat_piece = lax.all_gather(features, "grp", axis=0, tiled=True)
    count_piece = lax.all_gather(counts, "grp", axis=0, tiled=True)
    live = jnp.take(count_piece, wanted, axis=0)
    rows = count_picks * slots
    inputs = jnp.take(feat_piece, wanted, axis=0).reshape(rows, width)
    mask = (jnp.arange(slots)[None, :] < live[:, None]).reshape(rows, 1).astype(BF16)
    inputs = inputs * mask
    maskf = mask.astype(F32)
    adj = adjacency[0]
    agg_first = nn(adj, inputs).astype(BF16)
    pre = nn(agg_first, w_first)
    hidden = (maskf * jax.nn.silu(pre)).astype(BF16)
    agg_second = nn(adj, hidden).astype(BF16)
    output = (maskf * nn(agg_second, w_second)).astype(BF16)
    dout = cotangent[0] * mask

    def summed(a, b):
        part = lax.dot_general(a, b, (((0,), (0,)), ((), ())), preferred_element_type=F32)
        return lax.psum_scatter(part, "grp", scatter_dimension=0, tiled=True)

    grad_second = summed(dout, agg_second)
    dagg = nt(dout, w_second).astype(BF16)
    back = lax.dot_general(adj, dagg, (((0,), (0,)), ((), ())), preferred_element_type=F32)
    sig = jax.nn.sigmoid(pre)
    dpre = (maskf * back * sig * (1.0 + pre * (1.0 - sig))).astype(BF16)
    grad_first = summed(dpre, agg_first)
    return (output.reshape(1, rows, width), grad_first, grad_second)


def solution(mesh):
    n = mesh.shape["grp"]

    def body(*args):
        rows = args[4].shape[1]
        return whole_body(*args) if n == GROUP and rows == LANES else split_body(*args)

    in_specs = (
        P(("parts", "grp"), None, None),
        P(("parts", "grp")),
        P(("parts", "grp"), None),
        P(("parts", "grp"), None),
        P(("parts", "grp"), None, None),
        P(("parts", "grp"), None, None),
        P(),
        P(),
    )
    out_specs = (
        P(("parts", "grp"), None, None),
        P(("parts", "grp"), None),
        P(("parts", "grp"), None),
    )
    return jax.shard_map(body, mesh=mesh, in_specs=in_specs, out_specs=out_specs, check_vma=False)
```

```python
import functools

import jax
import jax.numpy as jnp
from jax import lax
from jax.experimental import pallas as pl
from jax.experimental.pallas import tpu as pltpu
from jax.sharding import PartitionSpec as P

F32 = jnp.float32
BF16 = jnp.bfloat16
VMEM = pl.BlockSpec(memory_space=pltpu.VMEM)
HBM = pl.BlockSpec(memory_space=pltpu.HBM)
LANES = 128
META = 16
LIMIT = 24 * 2**20
SMALL = 8 * 2**20
Z2, Z1, Y, CORE = 8, 4, 2, 1
GROUP = 16
FAR = (Z2 | Z1, Z2)
NEAR = tuple(z | c for z in (0, *FAR) for c in (0, CORE))
ACROSS = tuple(Y | slot for slot in NEAR)
BESIDE = (Z1, Z1 | CORE, Z1 | Y, Z1 | Y | CORE)
HALF_A = ((0, Z2, Z1, Z1 | Z2), (Y, Y | Z2, Y | Z1, Y | Z1 | Z2))
HALF_B = ((0, Z2, Y, Y | Z2), (Z1, Z1 | Z2, Z1 | Y, Z1 | Y | Z2))


def nn(a, b):
    return jnp.dot(a, b, preferred_element_type=F32)


def nt(a, b):
    return lax.dot_general(a, b, (((1,), (1,)), ((), ())), preferred_element_type=F32)


def start_all(moves, sems):
    copies = [pltpu.make_async_copy(a, b, sems.at[i]) for i, (a, b) in enumerate(moves)]
    for copy in copies:
        copy.start()
    return copies


def pack_kernel(counts, owner, local, features, adjacency, piece, *scratch):
    count, own_by, own_at, feat, adj, sems = scratch
    own, slots, width = features.shape
    rows = adjacency.shape[1]
    held = own * slots
    copies = start_all(zip((features, adjacency, counts, owner, local), (feat, adj, count, own_by, own_at)), sems)
    slot = lax.broadcasted_iota(jnp.int32, (slots, LANES), 0)
    line = lax.broadcasted_iota(jnp.int32, (META, LANES), 0)
    pick = lax.broadcasted_iota(jnp.int32, (META, LANES), 1) // slots
    meta = jnp.zeros((META, LANES), jnp.int32)
    for copy in copies:
        copy.wait()
    for i in range(own):
        live = slot < count[i]
        for b in range(width // LANES):
            block = feat[i, :, b * LANES : (b + 1) * LANES]
            at = b * held + i * slots
            piece[at : at + slots, :] = jnp.where(live, block, jnp.zeros_like(block))
        meta = jnp.where(line == 1 + i, count[i], meta)
    for k in range(owner.shape[1]):
        meta = jnp.where((line == 0) & (pick == k), own_by[0, k] * own + own_at[0, k], meta)
    at = held * (width // LANES)
    piece[at : at + rows, :] = adj[0]
    piece[at + rows : at + rows + META, :] = meta.astype(F32).astype(BF16)


def product_kernel(cotangent, w_second, near, across, beside, turned, back):
    each = w_second.shape[0] // GROUP
    place = lax.axis_index("grp")
    cot = cotangent[0]
    turned[...] = cot.astype(F32).T.astype(BF16)
    back[...] = nt(w_second[...], cot).astype(BF16)
    for out, slots in ((near, NEAR), (across, ACROSS), (beside, BESIDE)):
        for i, slot in enumerate(slots):
            span = pl.ds(pl.multiple_of((place ^ slot) * each, each), each)
            at = i * 2 * each
            out[at : at + each, :] = turned[span, :]
            out[at + each : at + 2 * each, :] = back[span, :]


def stack(out, at, *blocks):
    for block in blocks:
        out[at : at + block.shape[0], :] = block[...]
        at += block.shape[0]
    return at


def split_kernel(piece, came, near, across, beside, half_a, turn, keep, *sent):
    cut = half_a.shape[0] // 2
    stack(half_a, 0, piece.at[:cut], came.at[:cut])
    two = beside.shape[0] // 2
    stack(turn, 0, piece.at[cut:], came.at[cut:], beside.at[two:])
    stack(keep, 0, near.at[:two], across.at[:two], beside.at[:two])
    for i, out in enumerate(sent, 1):
        span = slice(i * two, (i + 1) * two)
        stack(out, 0, near.at[span], across.at[span])


def join_kernel(half_a, came_a, turn, came_b, out_a, out_b, both):
    size = out_b.shape[0] // 2
    stack(out_a, 0, half_a, came_a)
    stack(out_b, 0, turn.at[:size], came_b.at[:size])
    stack(both, 0, out_a, out_b)


def block_of(slot, rows, keep, came, *sent):
    z, h, b = slot - slot % 4, slot // 2 % 2, slot % 2
    if z in FAR:
        ref, at = sent[FAR.index(z)], 2 * h + b
    elif z == 0 or h == 0:
        ref, at = keep, (4 if z else 2 * h) + b
    else:
        ref, at = came, b
    at *= rows
    if ref is came:
        at += came.shape[0] - 2 * rows
    return ref.at[at : at + rows]


def columns_kernel(*refs):
    *refs, out = refs
    rows = out.shape[0] * 2 // GROUP
    at = 0
    for slot in range(1, GROUP, 2):
        at = stack(out, at, block_of(slot, rows, *refs))


def pair_kernel(far_a, far_b, columns, out):
    stack(out, 0, far_a, far_b, columns)


def place_of(slot):
    return slot // 2 + GROUP // 2 * (slot % 2)


def lay_out(arrays, held, cut, feat, adj, meta):
    rows = adj.shape[1]
    for ref, at, slots in arrays[:2]:
        for slot in slots:
            p = place_of(slot)
            for b in range(cut // held):
                feat[p * held : (p + 1) * held, b * LANES : (b + 1) * LANES] = ref[at : at + held, :]
                at += held
    for ref, at, slots in arrays[2:]:
        for slot in slots:
            p = place_of(slot)
            for b in range(cut // held, feat.shape[1] // LANES):
                feat[p * held : (p + 1) * held, b * LANES : (b + 1) * LANES] = ref[at : at + held, :]
                at += held
            adj[p] = ref[at : at + rows, :]
            at += rows
            meta[p] = ref[at : at + META, :]
            at += META


def spread_of(place, held, slots, adj, picks):
    line = lax.broadcasted_iota(jnp.int32, (held, LANES), 0)
    lane = lax.broadcasted_iota(jnp.int32, (1, LANES), 1) % slots
    owners = [None] * GROUP
    for slot in range(GROUP):
        owners[place_of(slot)] = place ^ slot
    code = jnp.concatenate([line + owner * held for owner in owners], axis=0)
    chosen = jnp.where(code == picks * slots + lane, 1.0, 0.0).astype(BF16)
    return nt(adj, chosen).astype(BF16)


def early_kernel(own, slots, cut, a, far_a, b, far_b, w_first, feat, lifted, spread, adj, meta, w_piece, partial):
    held = own * slots
    rows = adj.shape[1]
    place = lax.axis_index("grp")
    arrays = list(zip((a, far_a, b, far_b), HALF_A + HALF_B))
    lay_out([(ref, 0, at) for ref, at in arrays], held, cut, feat, adj, meta)
    lifted[...] = nn(feat[...], w_first[...]).astype(BF16)
    for p in range(GROUP // 2):
        picks = meta[p, 0:1, :].astype(F32).astype(jnp.int32)
        spread[p * rows : (p + 1) * rows, :] = spread_of(place, held, slots, adj[p], picks)
    chunk = min(w_first.shape[1], 2 * LANES)
    for c in range(0, w_first.shape[1], chunk):
        partial[:, c : c + chunk] = nn(spread[:, : feat.shape[0]], lifted[:, c : c + chunk])
    each = w_piece.shape[0]
    wide = max(each, LANES)
    per = wide // each
    start = pl.multiple_of((place // per) * wide, wide)
    block = w_first[:, pl.ds(start, wide)].astype(F32).T
    part = block[:each]
    for q in range(1, per):
        part = jnp.where(place % per == q, block[q * each : (q + 1) * each], part)
    w_piece[...] = part.astype(BF16)


def step_kernel(own, slots, cut, rest, core, pair, *refs):
    blocks, refs = refs[: 2 + len(FAR)], refs[2 + len(FAR) :]
    early_feat, early_lifted, early_spread, early_adj, early_meta, w_piece = refs[:6]
    partial, w_first, w_second, output, grad_first, grad_second = refs[6:12]
    hidden, spread, feat, adj, meta, dout, dpre, lifted, result, grads, second, sems = refs[12:]
    width = w_first.shape[0]
    held = own * slots
    rows = adj.shape[1]
    place = lax.axis_index("grp")
    first = GROUP // 2

    feat[: first * held, :] = early_feat[...]
    lifted[: first * held, :] = early_lifted[...]
    spread[: first * rows, :] = early_spread[...]
    adj[:first] = early_adj[...]
    meta[:first] = early_meta[...]
    arrays = []
    for size, start, halves in ((cut, 0, HALF_A), (rest, 4 * cut, HALF_B)):
        for ref, group in zip((core, pair), halves):
            arrays.append((ref, start, [slot | CORE for slot in group]))
    deep = 4 * (cut + rest)
    lay_out(arrays, held, cut, feat, adj, meta)
    metas = [meta[p].astype(F32) for p in range(GROUP)]
    picks = jnp.concatenate([m[0:1] for m in metas], axis=0).astype(jnp.int32)
    lane = lax.broadcasted_iota(jnp.int32, (GROUP, LANES), 1) % slots
    count = jnp.zeros((GROUP, LANES), jnp.int32)
    for slot in range(GROUP):
        for i in range(own):
            held_by = metas[place_of(slot)][1 + i : 2 + i].astype(jnp.int32)
            count = jnp.where(picks == (place ^ slot) * own + i, held_by, count)
    masks = (lane < count).astype(F32)

    late = slice(first * held, GROUP * held)
    lifted[late, :] = nn(feat[late, :], w_first[...]).astype(BF16)
    for p in range(first, GROUP):
        span = slice(p * rows, (p + 1) * rows)
        spread[span, :] = spread_of(place, held, slots, adj[p], picks[p : p + 1])
    lifted_piece = nt(w_piece[...], feat[...]).astype(BF16)
    pre_piece = nt(lifted_piece, spread[...])
    each = grad_first.shape[0]
    for slot in range(GROUP):
        p = place_of(slot)
        mask = masks[p : p + 1]
        span = slice(p * rows, (p + 1) * rows)
        if slot % 2:
            at = deep + slot // 2 * 2 * each
            source = pair[at : at + 2 * each, :]
        else:
            source = block_of(slot, 2 * each, *blocks)[...]
        back = nn((source.astype(F32) * mask).astype(BF16), adj[p]) * mask
        dout[:, span] = back[:each].astype(BF16)
        pre = pre_piece[:, span]
        sig = 0.5 + 0.5 * jnp.tanh(0.5 * pre)
        dpre[:, span] = (back[each:] * sig * (1.0 + pre * (1.0 - sig))).astype(BF16)

    chunk = min(width, 2 * LANES)
    for c in range(0, width, chunk):
        span = slice(c, c + chunk)
        here = first * rows
        half = 0.5 * (partial[:, span] + nn(spread[:here, first * held :], lifted[late, span]))
        hidden[:here, span] = (half + half * jnp.tanh(half)).astype(BF16)
        half = 0.5 * nn(spread[here:, :], lifted[:, span])
        hidden[here:, span] = (half + half * jnp.tanh(half)).astype(BF16)
        if c:
            done = slice(c - chunk, c)
            second[:, done] = nn(dout[...], hidden[:, done])
        else:
            moved = nn(dpre[...], spread[...])
            grads[...] = nn(moved.astype(BF16), feat[...])
            first_out = pltpu.make_async_copy(grads, grad_first, sems.at[0])
            first_out.start()
    live = jnp.broadcast_to(masks[0:1], (rows, LANES)).T[:, :1]
    agg = nn(adj[0], (hidden[:rows, :].astype(F32) * live).astype(BF16)).astype(BF16)
    result[0] = (nn(agg, w_second[...]) * live).astype(BF16)
    output_out = pltpu.make_async_copy(result, output, sems.at[1])
    output_out.start()
    second[:, span] = nn(dout[...], hidden[:, span])
    second_out = pltpu.make_async_copy(second, grad_second, sems.at[2])
    second_out.start()
    for copy in (first_out, output_out, second_out):
        copy.wait()


def call(kernel, ins, outs, scratch=(), limit=SMALL, stay=False, leave=False, flops=0):
    if stay:
        ins = [pltpu.with_memory_space_constraint(x, pltpu.HBM) for x in ins]
    return pl.pallas_call(
        kernel,
        out_shape=tuple(jax.ShapeDtypeStruct(*out) for out in outs),
        in_specs=[HBM if stay else VMEM] * len(ins),
        out_specs=(HBM if leave else VMEM,) * len(outs),
        scratch_shapes=list(scratch),
        compiler_params=pltpu.CompilerParams(vmem_limit_bytes=limit),
        cost_estimate=pl.CostEstimate(flops=flops, bytes_accessed=0, transcendentals=0),
    )(*ins)


def whole_body(features, counts, pick_owner, pick_local, adjacency, cotangent, w_first, w_second):
    own, slots, width = features.shape
    rows = adjacency.shape[1]
    held = own * slots
    each = width // GROUP
    total = GROUP * held
    cut = held * (width // LANES)
    rest = held * (width // LANES) + rows + META - cut
    half = GROUP // 2

    def swap(x, slot):
        return lax.ppermute(x, "grp", [(i, i ^ slot) for i in range(GROUP)])

    (piece,) = call(
        pack_kernel,
        (counts, pick_owner, pick_local, features, adjacency),
        [((cut + rest, LANES), BF16)],
        [pltpu.SMEM(x.shape, jnp.int32) for x in (counts, pick_owner, pick_local)]
        + [pltpu.VMEM(x.shape, BF16) for x in (features, adjacency)]
        + [pltpu.SemaphoreType.DMA((5,))],
        stay=True,
        flops=10**10,
    )
    cotangent, _ = lax.optimization_barrier((cotangent, piece))
    near, across, beside = call(
        product_kernel,
        (cotangent, w_second),
        [((len(x) * 2 * each, rows), BF16) for x in (NEAR, ACROSS, BESIDE)],
        [pltpu.VMEM((width, rows), BF16)] * 2,
    )
    came, across, beside = swap(piece, Z2), swap(across, Y), swap(beside, Z1)
    a, turn, keep, *sent = call(
        split_kernel,
        (piece, came, near, across, beside),
        [((x, LANES), BF16) for x in (2 * cut, 2 * rest + 4 * each, 12 * each)]
        + [((8 * each, rows), BF16)] * len(FAR),
    )
    came_a, came_b = swap(a, Z1), swap(turn, Y)
    sent = [swap(x, slot) for x, slot in zip(sent, FAR)]
    a, b, both = call(
        join_kernel,
        (a, came_a, turn, came_b),
        [((4 * size, LANES), BF16) for size in (cut, rest, cut + rest)],
    )
    core, far_b, far_a = swap(both, CORE), swap(b, Z1), swap(a, Y)
    (columns,) = call(
        columns_kernel, (keep, came_b, *sent), [((half * 2 * each, rows), BF16)], flops=8 * 10**9
    )
    far_a, far_b, core = lax.optimization_barrier((far_a, far_b, core))
    (pair,) = call(
        pair_kernel,
        (far_a, far_b, columns),
        [((4 * (cut + rest) + half * 2 * each, LANES), BF16)],
    )
    pair = swap(pair, CORE)
    early = call(
        functools.partial(early_kernel, own, slots, cut),
        (a, far_a, b, far_b, w_first),
        [
            ((total // 2, width), BF16),
            ((total // 2, width), BF16),
            ((half * rows, total), BF16),
            ((half, rows, rows), BF16),
            ((half, META, LANES), BF16),
            ((each, width), BF16),
            ((half * rows, width), F32),
        ],
        limit=LIMIT,
    )
    return call(
        functools.partial(step_kernel, own, slots, cut, rest),
        (core, pair, keep, came_b, *sent, *early, w_first, w_second),
        [((1, rows, width), BF16), ((each, width), F32), ((each, width), F32)],
        [
            pltpu.VMEM((GROUP * rows, width), BF16),
            pltpu.VMEM((GROUP * rows, total), BF16),
            pltpu.VMEM((total, width), BF16),
            pltpu.VMEM((GROUP, rows, rows), BF16),
            pltpu.VMEM((GROUP, META, LANES), BF16),
            pltpu.VMEM((each, GROUP * rows), BF16),
            pltpu.VMEM((each, GROUP * rows), BF16),
            pltpu.VMEM((total, width), BF16),
            pltpu.VMEM((1, rows, width), BF16),
            pltpu.VMEM((each, width), F32),
            pltpu.VMEM((each, width), F32),
            pltpu.SemaphoreType.DMA((3,)),
        ],
        LIMIT,
        leave=True,
    )


def split_body(features, counts, pick_owner, pick_local, adjacency, cotangent, w_first, w_second):
    owners = pick_owner[0]
    picks = pick_local[0]
    width = w_first.shape[0]
    slots = features.shape[1]
    count_picks = owners.shape[0]
    wanted = owners * features.shape[0] + picks
    feat_piece = lax.all_gather(features, "grp", axis=0, tiled=True)
    count_piece = lax.all_gather(counts, "grp", axis=0, tiled=True)
    live = jnp.take(count_piece, wanted, axis=0)
    rows = count_picks * slots
    inputs = jnp.take(feat_piece, wanted, axis=0).reshape(rows, width)
    mask = (jnp.arange(slots)[None, :] < live[:, None]).reshape(rows, 1).astype(BF16)
    inputs = inputs * mask
    maskf = mask.astype(F32)
    adj = adjacency[0]
    agg_first = nn(adj, inputs).astype(BF16)
    pre = nn(agg_first, w_first)
    hidden = (maskf * jax.nn.silu(pre)).astype(BF16)
    agg_second = nn(adj, hidden).astype(BF16)
    output = (maskf * nn(agg_second, w_second)).astype(BF16)
    dout = cotangent[0] * mask

    def summed(a, b):
        part = lax.dot_general(a, b, (((0,), (0,)), ((), ())), preferred_element_type=F32)
        return lax.psum_scatter(part, "grp", scatter_dimension=0, tiled=True)

    grad_second = summed(dout, agg_second)
    dagg = nt(dout, w_second).astype(BF16)
    back = lax.dot_general(adj, dagg, (((0,), (0,)), ((), ())), preferred_element_type=F32)
    sig = jax.nn.sigmoid(pre)
    dpre = (maskf * back * sig * (1.0 + pre * (1.0 - sig))).astype(BF16)
    grad_first = summed(dpre, agg_first)
    return (output.reshape(1, rows, width), grad_first, grad_second)


def solution(mesh):
    n = mesh.shape["grp"]

    def body(*args):
        rows = args[4].shape[1]
        return whole_body(*args) if n == GROUP and rows == LANES else split_body(*args)

    in_specs = (
        P(("parts", "grp"), None, None),
        P(("parts", "grp")),
        P(("parts", "grp"), None),
        P(("parts", "grp"), None),
        P(("parts", "grp"), None, None),
        P(("parts", "grp"), None, None),
        P(),
        P(),
    )
    out_specs = (
        P(("parts", "grp"), None, None),
        P(("parts", "grp"), None),
        P(("parts", "grp"), None),
    )
    return jax.shard_map(body, mesh=mesh, in_specs=in_specs, out_specs=out_specs, check_vma=False)
```

```python
import functools

import jax
import jax.numpy as jnp
from jax import lax
from jax.experimental import pallas as pl
from jax.experimental.pallas import tpu as pltpu
from jax.sharding import PartitionSpec as P

F32 = jnp.float32
BF16 = jnp.bfloat16
VMEM = pl.BlockSpec(memory_space=pltpu.VMEM)
HBM = pl.BlockSpec(memory_space=pltpu.HBM)
LANES = 128
META = 16
LIMIT = 24 * 2**20
SMALL = 8 * 2**20
Z2, Z1, Y, CORE = 8, 4, 2, 1
GROUP = 16
FAR = (Z2 | Z1, Z2)
NEAR = tuple(z | c for z in (0, *FAR) for c in (0, CORE))
ACROSS = tuple(Y | slot for slot in NEAR)
BESIDE = (Z1, Z1 | CORE, Z1 | Y, Z1 | Y | CORE)
HALF_A = ((0, Z2, Z1, Z1 | Z2), (Y, Y | Z2, Y | Z1, Y | Z1 | Z2))
HALF_B = ((0, Z2, Y, Y | Z2), (Z1, Z1 | Z2, Z1 | Y, Z1 | Y | Z2))


def nn(a, b):
    return jnp.dot(a, b, preferred_element_type=F32)


def nt(a, b):
    return lax.dot_general(a, b, (((1,), (1,)), ((), ())), preferred_element_type=F32)


def start_all(moves, sems):
    copies = [pltpu.make_async_copy(a, b, sems.at[i]) for i, (a, b) in enumerate(moves)]
    for copy in copies:
        copy.start()
    return copies


def pack_kernel(counts, owner, local, features, adjacency, piece, *scratch):
    count, own_by, own_at, feat, adj, sems = scratch
    own, slots, width = features.shape
    rows = adjacency.shape[1]
    held = own * slots
    copies = start_all(zip((features, adjacency, counts, owner, local), (feat, adj, count, own_by, own_at)), sems)
    slot = lax.broadcasted_iota(jnp.int32, (slots, LANES), 0)
    line = lax.broadcasted_iota(jnp.int32, (META, LANES), 0)
    pick = lax.broadcasted_iota(jnp.int32, (META, LANES), 1) // slots
    meta = jnp.zeros((META, LANES), jnp.int32)
    for copy in copies:
        copy.wait()
    for i in range(own):
        live = slot < count[i]
        for b in range(width // LANES):
            block = feat[i, :, b * LANES : (b + 1) * LANES]
            at = b * held + i * slots
            piece[at : at + slots, :] = jnp.where(live, block, jnp.zeros_like(block))
        meta = jnp.where(line == 1 + i, count[i], meta)
    for k in range(owner.shape[1]):
        meta = jnp.where((line == 0) & (pick == k), own_by[0, k] * own + own_at[0, k], meta)
    at = held * (width // LANES)
    piece[at : at + rows, :] = adj[0]
    piece[at + rows : at + rows + META, :] = meta.astype(F32).astype(BF16)


def product_kernel(cotangent, w_second, near, across, beside, turned, back):
    each = w_second.shape[0] // GROUP
    place = lax.axis_index("grp")
    cot = cotangent[0]
    turned[...] = cot.astype(F32).T.astype(BF16)
    back[...] = nt(w_second[...], cot).astype(BF16)
    for out, slots in ((near, NEAR), (across, ACROSS), (beside, BESIDE)):
        for i, slot in enumerate(slots):
            span = pl.ds(pl.multiple_of((place ^ slot) * each, each), each)
            at = i * 2 * each
            out[at : at + each, :] = turned[span, :]
            out[at + each : at + 2 * each, :] = back[span, :]


def stack(out, at, *blocks):
    for block in blocks:
        out[at : at + block.shape[0], :] = block[...]
        at += block.shape[0]
    return at


def split_kernel(piece, came, near, across, beside, half_a, turn, keep, *sent):
    cut = half_a.shape[0] // 2
    stack(half_a, 0, piece.at[:cut], came.at[:cut])
    two = beside.shape[0] // 2
    stack(turn, 0, piece.at[cut:], came.at[cut:], beside.at[two:])
    stack(keep, 0, near.at[:two], across.at[:two], beside.at[:two])
    for i, out in enumerate(sent, 1):
        span = slice(i * two, (i + 1) * two)
        stack(out, 0, near.at[span], across.at[span])


def join_kernel(half_a, came_a, turn, came_b, out_a, out_b, both):
    size = out_b.shape[0] // 2
    stack(out_a, 0, half_a, came_a)
    stack(out_b, 0, turn.at[:size], came_b.at[:size])
    stack(both, 0, out_a, out_b)


def block_of(slot, rows, keep, came, *sent):
    z, h, b = slot - slot % 4, slot // 2 % 2, slot % 2
    if z in FAR:
        ref, at = sent[FAR.index(z)], 2 * h + b
    elif z == 0 or h == 0:
        ref, at = keep, (4 if z else 2 * h) + b
    else:
        ref, at = came, b
    at *= rows
    if ref is came:
        at += came.shape[0] - 2 * rows
    return ref.at[at : at + rows]


def columns_kernel(*refs):
    *refs, out = refs
    rows = out.shape[0] * 2 // GROUP
    at = 0
    for slot in range(1, GROUP, 2):
        at = stack(out, at, block_of(slot, rows, *refs))


def pair_kernel(far_a, far_b, columns, out):
    stack(out, 0, far_a, far_b, columns)


def place_of(slot):
    return slot // 2 + GROUP // 2 * (slot % 2)


def lay_out(arrays, held, cut, feat, adj, meta):
    rows = adj.shape[1]
    for ref, at, slots in arrays[:2]:
        for slot in slots:
            p = place_of(slot)
            for b in range(cut // held):
                feat[p * held : (p + 1) * held, b * LANES : (b + 1) * LANES] = ref[at : at + held, :]
                at += held
    for ref, at, slots in arrays[2:]:
        for slot in slots:
            p = place_of(slot)
            for b in range(cut // held, feat.shape[1] // LANES):
                feat[p * held : (p + 1) * held, b * LANES : (b + 1) * LANES] = ref[at : at + held, :]
                at += held
            adj[p] = ref[at : at + rows, :]
            at += rows
            meta[p] = ref[at : at + META, :]
            at += META


def spread_of(place, held, slots, adj, picks):
    line = lax.broadcasted_iota(jnp.int32, (held, LANES), 0)
    lane = lax.broadcasted_iota(jnp.int32, (1, LANES), 1) % slots
    owners = [None] * GROUP
    for slot in range(GROUP):
        owners[place_of(slot)] = place ^ slot
    code = jnp.concatenate([line + owner * held for owner in owners], axis=0)
    chosen = jnp.where(code == picks * slots + lane, 1.0, 0.0).astype(BF16)
    return nt(adj, chosen).astype(BF16)


def early_kernel(own, slots, cut, a, far_a, b, far_b, w_first, feat, lifted, spread, adj, meta, w_piece, partial):
    held = own * slots
    rows = adj.shape[1]
    place = lax.axis_index("grp")
    arrays = list(zip((a, far_a, b, far_b), HALF_A + HALF_B))
    lay_out([(ref, 0, at) for ref, at in arrays], held, cut, feat, adj, meta)
    lifted[...] = (0.5 * nn(feat[...], w_first[...])).astype(BF16)
    for p in range(GROUP // 2):
        picks = meta[p, 0:1, :].astype(F32).astype(jnp.int32)
        spread[p * rows : (p + 1) * rows, :] = spread_of(place, held, slots, adj[p], picks)
    chunk = min(w_first.shape[1], 2 * LANES)
    for c in range(0, w_first.shape[1], chunk):
        partial[:, c : c + chunk] = nn(spread[:, : feat.shape[0]], lifted[:, c : c + chunk])
    each = w_piece.shape[0]
    wide = max(each, LANES)
    per = wide // each
    start = pl.multiple_of((place // per) * wide, wide)
    block = w_first[:, pl.ds(start, wide)].astype(F32).T
    part = block[:each]
    for q in range(1, per):
        part = jnp.where(place % per == q, block[q * each : (q + 1) * each], part)
    w_piece[...] = part.astype(BF16)


def step_kernel(own, slots, cut, rest, core, pair, *refs):
    blocks, refs = refs[: 2 + len(FAR)], refs[2 + len(FAR) :]
    early_feat, early_lifted, early_spread, early_adj, early_meta, w_piece = refs[:6]
    partial, w_first, w_second, output, grad_first, grad_second = refs[6:12]
    hidden, spread, feat, adj, meta, dout, dpre, lifted, result, grads, second, sems = refs[12:]
    width = w_first.shape[0]
    held = own * slots
    rows = adj.shape[1]
    place = lax.axis_index("grp")
    first = GROUP // 2

    feat[: first * held, :] = early_feat[...]
    lifted[: first * held, :] = early_lifted[...]
    spread[: first * rows, :] = early_spread[...]
    adj[:first] = early_adj[...]
    meta[:first] = early_meta[...]
    arrays = []
    for size, start, halves in ((cut, 0, HALF_A), (rest, 4 * cut, HALF_B)):
        for ref, group in zip((core, pair), halves):
            arrays.append((ref, start, [slot | CORE for slot in group]))
    deep = 4 * (cut + rest)
    lay_out(arrays, held, cut, feat, adj, meta)
    metas = [meta[p].astype(F32) for p in range(GROUP)]
    picks = jnp.concatenate([m[0:1] for m in metas], axis=0).astype(jnp.int32)
    lane = lax.broadcasted_iota(jnp.int32, (GROUP, LANES), 1) % slots
    count = jnp.zeros((GROUP, LANES), jnp.int32)
    for slot in range(GROUP):
        for i in range(own):
            held_by = metas[place_of(slot)][1 + i : 2 + i].astype(jnp.int32)
            count = jnp.where(picks == (place ^ slot) * own + i, held_by, count)
    masks = (lane < count).astype(F32)

    late = slice(first * held, GROUP * held)
    lifted[late, :] = (0.5 * nn(feat[late, :], w_first[...])).astype(BF16)
    for p in range(first, GROUP):
        span = slice(p * rows, (p + 1) * rows)
        spread[span, :] = spread_of(place, held, slots, adj[p], picks[p : p + 1])
    lifted_piece = nt(w_piece[...], feat[...]).astype(BF16)
    pre_piece = nt(lifted_piece, spread[...])
    each = grad_first.shape[0]
    for slot in range(GROUP):
        p = place_of(slot)
        mask = masks[p : p + 1]
        span = slice(p * rows, (p + 1) * rows)
        if slot % 2:
            at = deep + slot // 2 * 2 * each
            source = pair[at : at + 2 * each, :]
        else:
            source = block_of(slot, 2 * each, *blocks)[...]
        back = nn((source.astype(F32) * mask).astype(BF16), adj[p]) * mask
        dout[:, span] = back[:each].astype(BF16)
        pre = pre_piece[:, span]
        sig = 0.5 + 0.5 * jnp.tanh(0.5 * pre)
        dpre[:, span] = (back[each:] * sig * (1.0 + pre * (1.0 - sig))).astype(BF16)

    chunk = min(width, 2 * LANES)
    for c in range(0, width, chunk):
        span = slice(c, c + chunk)
        here = first * rows
        half = partial[:, span] + nn(spread[:here, first * held :], lifted[late, span])
        hidden[:here, span] = (half + half * jnp.tanh(half)).astype(BF16)
        half = nn(spread[here:, :], lifted[:, span])
        hidden[here:, span] = (half + half * jnp.tanh(half)).astype(BF16)
        if c:
            done = slice(c - chunk, c)
            second[:, done] = nn(dout[...], hidden[:, done])
        else:
            moved = nn(dpre[...], spread[...])
            grads[...] = nn(moved.astype(BF16), feat[...])
            first_out = pltpu.make_async_copy(grads, grad_first, sems.at[0])
            first_out.start()
    live = jnp.broadcast_to(masks[0:1], (rows, LANES)).T[:, :1]
    agg = nn(adj[0], (hidden[:rows, :].astype(F32) * live).astype(BF16)).astype(BF16)
    result[0] = (nn(agg, w_second[...]) * live).astype(BF16)
    output_out = pltpu.make_async_copy(result, output, sems.at[1])
    output_out.start()
    second[:, span] = nn(dout[...], hidden[:, span])
    second_out = pltpu.make_async_copy(second, grad_second, sems.at[2])
    second_out.start()
    for copy in (first_out, output_out, second_out):
        copy.wait()


def call(kernel, ins, outs, scratch=(), limit=SMALL, stay=False, leave=False, flops=0):
    if stay:
        ins = [pltpu.with_memory_space_constraint(x, pltpu.HBM) for x in ins]
    return pl.pallas_call(
        kernel,
        out_shape=tuple(jax.ShapeDtypeStruct(*out) for out in outs),
        in_specs=[HBM if stay else VMEM] * len(ins),
        out_specs=(HBM if leave else VMEM,) * len(outs),
        scratch_shapes=list(scratch),
        compiler_params=pltpu.CompilerParams(vmem_limit_bytes=limit),
        cost_estimate=pl.CostEstimate(flops=flops, bytes_accessed=0, transcendentals=0),
    )(*ins)


def whole_body(features, counts, pick_owner, pick_local, adjacency, cotangent, w_first, w_second):
    own, slots, width = features.shape
    rows = adjacency.shape[1]
    held = own * slots
    each = width // GROUP
    total = GROUP * held
    cut = held * (width // LANES)
    rest = held * (width // LANES) + rows + META - cut
    half = GROUP // 2

    def swap(x, slot):
        return lax.ppermute(x, "grp", [(i, i ^ slot) for i in range(GROUP)])

    (piece,) = call(
        pack_kernel,
        (counts, pick_owner, pick_local, features, adjacency),
        [((cut + rest, LANES), BF16)],
        [pltpu.SMEM(x.shape, jnp.int32) for x in (counts, pick_owner, pick_local)]
        + [pltpu.VMEM(x.shape, BF16) for x in (features, adjacency)]
        + [pltpu.SemaphoreType.DMA((5,))],
        stay=True,
        flops=10**10,
    )
    cotangent, _ = lax.optimization_barrier((cotangent, piece))
    near, across, beside = call(
        product_kernel,
        (cotangent, w_second),
        [((len(x) * 2 * each, rows), BF16) for x in (NEAR, ACROSS, BESIDE)],
        [pltpu.VMEM((width, rows), BF16)] * 2,
    )
    came, across, beside = swap(piece, Z2), swap(across, Y), swap(beside, Z1)
    a, turn, keep, *sent = call(
        split_kernel,
        (piece, came, near, across, beside),
        [((x, LANES), BF16) for x in (2 * cut, 2 * rest + 4 * each, 12 * each)]
        + [((8 * each, rows), BF16)] * len(FAR),
    )
    came_a, came_b = swap(a, Z1), swap(turn, Y)
    sent = [swap(x, slot) for x, slot in zip(sent, FAR)]
    a, b, both = call(
        join_kernel,
        (a, came_a, turn, came_b),
        [((4 * size, LANES), BF16) for size in (cut, rest, cut + rest)],
    )
    core, far_b, far_a = swap(both, CORE), swap(b, Z1), swap(a, Y)
    (columns,) = call(
        columns_kernel, (keep, came_b, *sent), [((half * 2 * each, rows), BF16)], flops=8 * 10**9
    )
    far_a, far_b, core = lax.optimization_barrier((far_a, far_b, core))
    (pair,) = call(
        pair_kernel,
        (far_a, far_b, columns),
        [((4 * (cut + rest) + half * 2 * each, LANES), BF16)],
    )
    pair = swap(pair, CORE)
    early = call(
        functools.partial(early_kernel, own, slots, cut),
        (a, far_a, b, far_b, w_first),
        [
            ((total // 2, width), BF16),
            ((total // 2, width), BF16),
            ((half * rows, total), BF16),
            ((half, rows, rows), BF16),
            ((half, META, LANES), BF16),
            ((each, width), BF16),
            ((half * rows, width), F32),
        ],
        limit=LIMIT,
    )
    return call(
        functools.partial(step_kernel, own, slots, cut, rest),
        (core, pair, keep, came_b, *sent, *early, w_first, w_second),
        [((1, rows, width), BF16), ((each, width), F32), ((each, width), F32)],
        [
            pltpu.VMEM((GROUP * rows, width), BF16),
            pltpu.VMEM((GROUP * rows, total), BF16),
            pltpu.VMEM((total, width), BF16),
            pltpu.VMEM((GROUP, rows, rows), BF16),
            pltpu.VMEM((GROUP, META, LANES), BF16),
            pltpu.VMEM((each, GROUP * rows), BF16),
            pltpu.VMEM((each, GROUP * rows), BF16),
            pltpu.VMEM((total, width), BF16),
            pltpu.VMEM((1, rows, width), BF16),
            pltpu.VMEM((each, width), F32),
            pltpu.VMEM((each, width), F32),
            pltpu.SemaphoreType.DMA((3,)),
        ],
        LIMIT,
        leave=True,
    )


def split_body(features, counts, pick_owner, pick_local, adjacency, cotangent, w_first, w_second):
    owners = pick_owner[0]
    picks = pick_local[0]
    width = w_first.shape[0]
    slots = features.shape[1]
    count_picks = owners.shape[0]
    wanted = owners * features.shape[0] + picks
    feat_piece = lax.all_gather(features, "grp", axis=0, tiled=True)
    count_piece = lax.all_gather(counts, "grp", axis=0, tiled=True)
    live = jnp.take(count_piece, wanted, axis=0)
    rows = count_picks * slots
    inputs = jnp.take(feat_piece, wanted, axis=0).reshape(rows, width)
    mask = (jnp.arange(slots)[None, :] < live[:, None]).reshape(rows, 1).astype(BF16)
    inputs = inputs * mask
    maskf = mask.astype(F32)
    adj = adjacency[0]
    agg_first = nn(adj, inputs).astype(BF16)
    pre = nn(agg_first, w_first)
    hidden = (maskf * jax.nn.silu(pre)).astype(BF16)
    agg_second = nn(adj, hidden).astype(BF16)
    output = (maskf * nn(agg_second, w_second)).astype(BF16)
    dout = cotangent[0] * mask

    def summed(a, b):
        part = lax.dot_general(a, b, (((0,), (0,)), ((), ())), preferred_element_type=F32)
        return lax.psum_scatter(part, "grp", scatter_dimension=0, tiled=True)

    grad_second = summed(dout, agg_second)
    dagg = nt(dout, w_second).astype(BF16)
    back = lax.dot_general(adj, dagg, (((0,), (0,)), ((), ())), preferred_element_type=F32)
    sig = jax.nn.sigmoid(pre)
    dpre = (maskf * back * sig * (1.0 + pre * (1.0 - sig))).astype(BF16)
    grad_first = summed(dpre, agg_first)
    return (output.reshape(1, rows, width), grad_first, grad_second)


def solution(mesh):
    n = mesh.shape["grp"]

    def body(*args):
        rows = args[4].shape[1]
        return whole_body(*args) if n == GROUP and rows == LANES else split_body(*args)

    in_specs = (
        P(("parts", "grp"), None, None),
        P(("parts", "grp")),
        P(("parts", "grp"), None),
        P(("parts", "grp"), None),
        P(("parts", "grp"), None, None),
        P(("parts", "grp"), None, None),
        P(),
        P(),
    )
    out_specs = (
        P(("parts", "grp"), None, None),
        P(("parts", "grp"), None),
        P(("parts", "grp"), None),
    )
    return jax.shard_map(body, mesh=mesh, in_specs=in_specs, out_specs=out_specs, check_vma=False)
```

```python
import functools

import jax
import jax.numpy as jnp
from jax import lax
from jax.experimental import pallas as pl
from jax.experimental.pallas import tpu as pltpu
from jax.sharding import PartitionSpec as P

F32 = jnp.float32
BF16 = jnp.bfloat16
VMEM = pl.BlockSpec(memory_space=pltpu.VMEM)
HBM = pl.BlockSpec(memory_space=pltpu.HBM)
LANES = 128
META = 16
LIMIT = 24 * 2**20
SMALL = 8 * 2**20
Z2, Z1, Y, CORE = 8, 4, 2, 1
GROUP = 16
FAR = (Z2 | Z1, Z2)
NEAR = tuple(z | c for z in (0, *FAR) for c in (0, CORE))
ACROSS = tuple(Y | slot for slot in NEAR)
BESIDE = (Z1, Z1 | CORE, Z1 | Y, Z1 | Y | CORE)
HALF_A = ((0, Z2, Z1, Z1 | Z2), (Y, Y | Z2, Y | Z1, Y | Z1 | Z2))
HALF_B = ((0, Z2, Y, Y | Z2), (Z1, Z1 | Z2, Z1 | Y, Z1 | Y | Z2))


def nn(a, b):
    return jnp.dot(a, b, preferred_element_type=F32)


def nt(a, b):
    return lax.dot_general(a, b, (((1,), (1,)), ((), ())), preferred_element_type=F32)


def start_all(moves, sems):
    copies = [pltpu.make_async_copy(a, b, sems.at[i]) for i, (a, b) in enumerate(moves)]
    for copy in copies:
        copy.start()
    return copies


def pack_kernel(counts, owner, local, features, adjacency, piece, *scratch):
    count, own_by, own_at, feat, adj, sems = scratch
    own, slots, width = features.shape
    rows = adjacency.shape[1]
    held = own * slots
    copies = start_all(zip((features, adjacency, counts, owner, local), (feat, adj, count, own_by, own_at)), sems)
    slot = lax.broadcasted_iota(jnp.int32, (slots, LANES), 0)
    line = lax.broadcasted_iota(jnp.int32, (META, LANES), 0)
    pick = lax.broadcasted_iota(jnp.int32, (META, LANES), 1) // slots
    meta = jnp.zeros((META, LANES), jnp.int32)
    for copy in copies:
        copy.wait()
    for i in range(own):
        live = slot < count[i]
        for b in range(width // LANES):
            block = feat[i, :, b * LANES : (b + 1) * LANES]
            at = b * held + i * slots
            piece[at : at + slots, :] = jnp.where(live, block, jnp.zeros_like(block))
        meta = jnp.where(line == 1 + i, count[i], meta)
    for k in range(owner.shape[1]):
        meta = jnp.where((line == 0) & (pick == k), own_by[0, k] * own + own_at[0, k], meta)
    at = held * (width // LANES)
    piece[at : at + rows, :] = adj[0]
    piece[at + rows : at + rows + META, :] = meta.astype(F32).astype(BF16)


def product_kernel(cotangent, w_second, near, across, beside, turned, back):
    each = w_second.shape[0] // GROUP
    place = lax.axis_index("grp")
    cot = cotangent[0]
    turned[...] = cot.astype(F32).T.astype(BF16)
    back[...] = nt(w_second[...], cot).astype(BF16)
    for out, slots in ((near, NEAR), (across, ACROSS), (beside, BESIDE)):
        for i, slot in enumerate(slots):
            span = pl.ds(pl.multiple_of((place ^ slot) * each, each), each)
            at = i * 2 * each
            out[at : at + each, :] = turned[span, :]
            out[at + each : at + 2 * each, :] = back[span, :]


def stack(out, at, *blocks):
    for block in blocks:
        out[at : at + block.shape[0], :] = block[...]
        at += block.shape[0]
    return at


def split_kernel(piece, came, near, across, beside, half_a, turn, keep, *sent):
    cut = half_a.shape[0] // 2
    stack(half_a, 0, piece.at[:cut], came.at[:cut])
    two = beside.shape[0] // 2
    stack(turn, 0, piece.at[cut:], came.at[cut:], beside.at[two:])
    stack(keep, 0, near.at[:two], across.at[:two], beside.at[:two])
    for i, out in enumerate(sent, 1):
        span = slice(i * two, (i + 1) * two)
        stack(out, 0, near.at[span], across.at[span])


def join_kernel(half_a, came_a, turn, came_b, out_a, out_b, both):
    size = out_b.shape[0] // 2
    stack(out_a, 0, half_a, came_a)
    stack(out_b, 0, turn.at[:size], came_b.at[:size])
    stack(both, 0, out_a, out_b)


def block_of(slot, rows, keep, came, *sent):
    z, h, b = slot - slot % 4, slot // 2 % 2, slot % 2
    if z in FAR:
        ref, at = sent[FAR.index(z)], 2 * h + b
    elif z == 0 or h == 0:
        ref, at = keep, (4 if z else 2 * h) + b
    else:
        ref, at = came, b
    at *= rows
    if ref is came:
        at += came.shape[0] - 2 * rows
    return ref.at[at : at + rows]


def columns_kernel(*refs):
    *refs, out = refs
    rows = out.shape[0] * 2 // GROUP
    at = 0
    for slot in range(1, GROUP, 2):
        at = stack(out, at, block_of(slot, rows, *refs))


def pair_kernel(far_a, far_b, columns, out):
    stack(out, 0, far_a, far_b, columns)


def place_of(slot):
    return slot // 2 + GROUP // 2 * (slot % 2)


def lay_out(arrays, held, cut, feat, adj, meta):
    rows = adj.shape[1]
    for ref, at, slots in arrays[:2]:
        for slot in slots:
            p = place_of(slot)
            for b in range(cut // held):
                feat[p * held : (p + 1) * held, b * LANES : (b + 1) * LANES] = ref[at : at + held, :]
                at += held
    for ref, at, slots in arrays[2:]:
        for slot in slots:
            p = place_of(slot)
            for b in range(cut // held, feat.shape[1] // LANES):
                feat[p * held : (p + 1) * held, b * LANES : (b + 1) * LANES] = ref[at : at + held, :]
                at += held
            adj[p] = ref[at : at + rows, :]
            at += rows
            meta[p] = ref[at : at + META, :]
            at += META


def spread_of(place, held, slots, adj, picks):
    line = lax.broadcasted_iota(jnp.int32, (held, LANES), 0)
    lane = lax.broadcasted_iota(jnp.int32, (1, LANES), 1) % slots
    owners = [None] * GROUP
    for slot in range(GROUP):
        owners[place_of(slot)] = place ^ slot
    code = jnp.concatenate([line + owner * held for owner in owners], axis=0)
    chosen = jnp.where(code == picks * slots + lane, 1.0, 0.0).astype(BF16)
    return nt(adj, chosen).astype(BF16)


def early_kernel(own, slots, cut, a, far_a, b, far_b, w_first, feat, lifted, spread, adj, meta, w_piece, partial):
    held = own * slots
    rows = adj.shape[1]
    place = lax.axis_index("grp")
    arrays = list(zip((a, far_a, b, far_b), HALF_A + HALF_B))
    lay_out([(ref, 0, at) for ref, at in arrays], held, cut, feat, adj, meta)
    lifted[...] = (0.5 * nn(feat[...], w_first[...])).astype(BF16)
    for p in range(GROUP // 2):
        picks = meta[p, 0:1, :].astype(F32).astype(jnp.int32)
        spread[p * rows : (p + 1) * rows, :] = spread_of(place, held, slots, adj[p], picks)
    chunk = min(w_first.shape[1], 2 * LANES)
    for c in range(0, w_first.shape[1], chunk):
        partial[:, c : c + chunk] = nn(spread[:, : feat.shape[0]], lifted[:, c : c + chunk])
    each = w_piece.shape[0]
    wide = max(each, LANES)
    per = wide // each
    start = pl.multiple_of((place // per) * wide, wide)
    block = w_first[:, pl.ds(start, wide)].astype(F32).T
    part = block[:each]
    for q in range(1, per):
        part = jnp.where(place % per == q, block[q * each : (q + 1) * each], part)
    w_piece[...] = part.astype(BF16)


def step_kernel(own, slots, cut, rest, core, pair, *refs):
    blocks, refs = refs[: 2 + len(FAR)], refs[2 + len(FAR) :]
    early_feat, early_lifted, early_spread, early_adj, early_meta, w_piece = refs[:6]
    partial, w_first, w_second, output, grad_first, grad_second = refs[6:12]
    hidden, spread, feat, adj, meta, dout, dpre, lifted, result, grads, second, sems = refs[12:]
    width = w_first.shape[0]
    held = own * slots
    rows = adj.shape[1]
    place = lax.axis_index("grp")
    first = GROUP // 2

    feat[: first * held, :] = early_feat[...]
    lifted[: first * held, :] = early_lifted[...]
    spread[: first * rows, :] = early_spread[...]
    adj[:first] = early_adj[...]
    meta[:first] = early_meta[...]
    arrays = []
    for size, start, halves in ((cut, 0, HALF_A), (rest, 4 * cut, HALF_B)):
        for ref, group in zip((core, pair), halves):
            arrays.append((ref, start, [slot | CORE for slot in group]))
    deep = 4 * (cut + rest)
    lay_out(arrays, held, cut, feat, adj, meta)
    metas = [meta[p].astype(F32) for p in range(GROUP)]
    picks = jnp.concatenate([m[0:1] for m in metas], axis=0).astype(jnp.int32)
    lane = lax.broadcasted_iota(jnp.int32, (GROUP, LANES), 1) % slots
    count = jnp.zeros((GROUP, LANES), jnp.int32)
    for slot in range(GROUP):
        for i in range(own):
            held_by = metas[place_of(slot)][1 + i : 2 + i].astype(jnp.int32)
            count = jnp.where(picks == (place ^ slot) * own + i, held_by, count)
    masks = (lane < count).astype(F32)

    late = slice(first * held, GROUP * held)
    lifted[late, :] = (0.5 * nn(feat[late, :], w_first[...])).astype(BF16)
    for p in range(first, GROUP):
        span = slice(p * rows, (p + 1) * rows)
        spread[span, :] = spread_of(place, held, slots, adj[p], picks[p : p + 1])
    lifted_piece = nt(w_piece[...], feat[...]).astype(BF16)
    pre_piece = nt(lifted_piece, spread[...])
    each = grad_first.shape[0]
    for slot in range(GROUP):
        p = place_of(slot)
        mask = masks[p : p + 1]
        span = slice(p * rows, (p + 1) * rows)
        if slot % 2:
            at = deep + slot // 2 * 2 * each
            source = pair[at : at + 2 * each, :]
        else:
            source = block_of(slot, 2 * each, *blocks)[...]
        back = nn((source.astype(F32) * mask).astype(BF16), adj[p]) * mask
        dout[:, span] = back[:each].astype(BF16)
        pre = pre_piece[:, span]
        sig = 0.5 + 0.5 * jnp.tanh(0.5 * pre)
        dpre[:, span] = (back[each:] * sig * (1.0 + pre * (1.0 - sig))).astype(BF16)

    chunk = min(width, 4 * LANES)
    for c in range(0, width, chunk):
        span = slice(c, c + chunk)
        here = first * rows
        half = partial[:, span] + nn(spread[:here, first * held :], lifted[late, span])
        hidden[:here, span] = (half + half * jnp.tanh(half)).astype(BF16)
        half = nn(spread[here:, :], lifted[:, span])
        hidden[here:, span] = (half + half * jnp.tanh(half)).astype(BF16)
        if c:
            done = slice(c - chunk, c)
            second[:, done] = nn(dout[...], hidden[:, done])
        else:
            moved = nn(dpre[...], spread[...])
            grads[...] = nn(moved.astype(BF16), feat[...])
            first_out = pltpu.make_async_copy(grads, grad_first, sems.at[0])
            first_out.start()
    live = jnp.broadcast_to(masks[0:1], (rows, LANES)).T[:, :1]
    agg = nn(adj[0], (hidden[:rows, :].astype(F32) * live).astype(BF16)).astype(BF16)
    result[0] = (nn(agg, w_second[...]) * live).astype(BF16)
    output_out = pltpu.make_async_copy(result, output, sems.at[1])
    output_out.start()
    second[:, span] = nn(dout[...], hidden[:, span])
    second_out = pltpu.make_async_copy(second, grad_second, sems.at[2])
    second_out.start()
    for copy in (first_out, output_out, second_out):
        copy.wait()


def call(kernel, ins, outs, scratch=(), limit=SMALL, stay=False, leave=False, flops=0):
    if stay:
        ins = [pltpu.with_memory_space_constraint(x, pltpu.HBM) for x in ins]
    return pl.pallas_call(
        kernel,
        out_shape=tuple(jax.ShapeDtypeStruct(*out) for out in outs),
        in_specs=[HBM if stay else VMEM] * len(ins),
        out_specs=(HBM if leave else VMEM,) * len(outs),
        scratch_shapes=list(scratch),
        compiler_params=pltpu.CompilerParams(vmem_limit_bytes=limit),
        cost_estimate=pl.CostEstimate(flops=flops, bytes_accessed=0, transcendentals=0),
    )(*ins)


def whole_body(features, counts, pick_owner, pick_local, adjacency, cotangent, w_first, w_second):
    own, slots, width = features.shape
    rows = adjacency.shape[1]
    held = own * slots
    each = width // GROUP
    total = GROUP * held
    cut = held * (width // LANES)
    rest = held * (width // LANES) + rows + META - cut
    half = GROUP // 2

    def swap(x, slot):
        return lax.ppermute(x, "grp", [(i, i ^ slot) for i in range(GROUP)])

    (piece,) = call(
        pack_kernel,
        (counts, pick_owner, pick_local, features, adjacency),
        [((cut + rest, LANES), BF16)],
        [pltpu.SMEM(x.shape, jnp.int32) for x in (counts, pick_owner, pick_local)]
        + [pltpu.VMEM(x.shape, BF16) for x in (features, adjacency)]
        + [pltpu.SemaphoreType.DMA((5,))],
        stay=True,
        flops=10**10,
    )
    cotangent, _ = lax.optimization_barrier((cotangent, piece))
    near, across, beside = call(
        product_kernel,
        (cotangent, w_second),
        [((len(x) * 2 * each, rows), BF16) for x in (NEAR, ACROSS, BESIDE)],
        [pltpu.VMEM((width, rows), BF16)] * 2,
    )
    came, across, beside = swap(piece, Z2), swap(across, Y), swap(beside, Z1)
    a, turn, keep, *sent = call(
        split_kernel,
        (piece, came, near, across, beside),
        [((x, LANES), BF16) for x in (2 * cut, 2 * rest + 4 * each, 12 * each)]
        + [((8 * each, rows), BF16)] * len(FAR),
    )
    came_a, came_b = swap(a, Z1), swap(turn, Y)
    sent = [swap(x, slot) for x, slot in zip(sent, FAR)]
    a, b, both = call(
        join_kernel,
        (a, came_a, turn, came_b),
        [((4 * size, LANES), BF16) for size in (cut, rest, cut + rest)],
    )
    core, far_b, far_a = swap(both, CORE), swap(b, Z1), swap(a, Y)
    (columns,) = call(
        columns_kernel, (keep, came_b, *sent), [((half * 2 * each, rows), BF16)], flops=8 * 10**9
    )
    far_a, far_b, core = lax.optimization_barrier((far_a, far_b, core))
    (pair,) = call(
        pair_kernel,
        (far_a, far_b, columns),
        [((4 * (cut + rest) + half * 2 * each, LANES), BF16)],
    )
    pair = swap(pair, CORE)
    early = call(
        functools.partial(early_kernel, own, slots, cut),
        (a, far_a, b, far_b, w_first),
        [
            ((total // 2, width), BF16),
            ((total // 2, width), BF16),
            ((half * rows, total), BF16),
            ((half, rows, rows), BF16),
            ((half, META, LANES), BF16),
            ((each, width), BF16),
            ((half * rows, width), F32),
        ],
        limit=LIMIT,
    )
    return call(
        functools.partial(step_kernel, own, slots, cut, rest),
        (core, pair, keep, came_b, *sent, *early, w_first, w_second),
        [((1, rows, width), BF16), ((each, width), F32), ((each, width), F32)],
        [
            pltpu.VMEM((GROUP * rows, width), BF16),
            pltpu.VMEM((GROUP * rows, total), BF16),
            pltpu.VMEM((total, width), BF16),
            pltpu.VMEM((GROUP, rows, rows), BF16),
            pltpu.VMEM((GROUP, META, LANES), BF16),
            pltpu.VMEM((each, GROUP * rows), BF16),
            pltpu.VMEM((each, GROUP * rows), BF16),
            pltpu.VMEM((total, width), BF16),
            pltpu.VMEM((1, rows, width), BF16),
            pltpu.VMEM((each, width), F32),
            pltpu.VMEM((each, width), F32),
            pltpu.SemaphoreType.DMA((3,)),
        ],
        LIMIT,
        leave=True,
    )


def split_body(features, counts, pick_owner, pick_local, adjacency, cotangent, w_first, w_second):
    owners = pick_owner[0]
    picks = pick_local[0]
    width = w_first.shape[0]
    slots = features.shape[1]
    count_picks = owners.shape[0]
    wanted = owners * features.shape[0] + picks
    feat_piece = lax.all_gather(features, "grp", axis=0, tiled=True)
    count_piece = lax.all_gather(counts, "grp", axis=0, tiled=True)
    live = jnp.take(count_piece, wanted, axis=0)
    rows = count_picks * slots
    inputs = jnp.take(feat_piece, wanted, axis=0).reshape(rows, width)
    mask = (jnp.arange(slots)[None, :] < live[:, None]).reshape(rows, 1).astype(BF16)
    inputs = inputs * mask
    maskf = mask.astype(F32)
    adj = adjacency[0]
    agg_first = nn(adj, inputs).astype(BF16)
    pre = nn(agg_first, w_first)
    hidden = (maskf * jax.nn.silu(pre)).astype(BF16)
    agg_second = nn(adj, hidden).astype(BF16)
    output = (maskf * nn(agg_second, w_second)).astype(BF16)
    dout = cotangent[0] * mask

    def summed(a, b):
        part = lax.dot_general(a, b, (((0,), (0,)), ((), ())), preferred_element_type=F32)
        return lax.psum_scatter(part, "grp", scatter_dimension=0, tiled=True)

    grad_second = summed(dout, agg_second)
    dagg = nt(dout, w_second).astype(BF16)
    back = lax.dot_general(adj, dagg, (((0,), (0,)), ((), ())), preferred_element_type=F32)
    sig = jax.nn.sigmoid(pre)
    dpre = (maskf * back * sig * (1.0 + pre * (1.0 - sig))).astype(BF16)
    grad_first = summed(dpre, agg_first)
    return (output.reshape(1, rows, width), grad_first, grad_second)


def solution(mesh):
    n = mesh.shape["grp"]

    def body(*args):
        rows = args[4].shape[1]
        return whole_body(*args) if n == GROUP and rows == LANES else split_body(*args)

    in_specs = (
        P(("parts", "grp"), None, None),
        P(("parts", "grp")),
        P(("parts", "grp"), None),
        P(("parts", "grp"), None),
        P(("parts", "grp"), None, None),
        P(("parts", "grp"), None, None),
        P(),
        P(),
    )
    out_specs = (
        P(("parts", "grp"), None, None),
        P(("parts", "grp"), None),
        P(("parts", "grp"), None),
    )
    return jax.shard_map(body, mesh=mesh, in_specs=in_specs, out_specs=out_specs, check_vma=False)
```
